32 devices in a mesh: date: 8 (over z, x), row: 2 (over core), col: 2 (over y).
Axes of the slice: x: 2, y: 2, z: 4, core: 2. Of those that a mesh axis runs over, the one named last changes fastest.
Arguments:
- images: float32 [16, 2, 96, 1536], P('date', None, 'row', 'col'), may hold values from -8 to 8
- secondaries: int32 [16, 3], P('date'), may hold values from 0 to 15, as said below
Outputs:
- filtered: float32 [16, 3, 2, 48, 192], P('date', None, None, 'row', 'col')
- coherence: float32 [16, 3, 2, 48, 192], P('date', None, None, 'row', 'col')
The draws below stay inside these ranges and needn't reach their ends.
Inputs may be any that keep to these rules, and one draw needn't show every extreme that they name: secondaries[k, l] = (k + o) mod 16 for 3 distinct offsets o of 1 to 4, rising with l; the offset 4 occurs in every draw.
All inputs are finite; a program needn't handle non-finite values.
Results may differ from the reference program's by a relative error of at most 0.00005.
Values sent between devices are 32-bit elements; how exact they have to be, the bound alone decides.
A program may use at most 128 MiB of HBM per device.

```python
import math
import jax
import jax.numpy as jnp
from jax import lax

LINKS = 3
REACH = 4
LOOK_R = 2
LOOK_C = 8
PATCH = 32
KEEP = 24
MARGIN = 4
DATES = 16
ROWS = 96
COLS = 1536


def draw_images(key, part):
    key = jax.random.fold_in(key, 11)
    subkeys = jax.random.split(key, 5)
    scene = jnp.clip(jax.random.normal(subkeys[0], (2, ROWS, COLS), jnp.float32), -4.0, 4.0)
    rate_rows = jax.random.uniform(subkeys[1], (DATES, 1, 1), jnp.float32, -0.3, 0.3)
    rate_cols = jax.random.uniform(subkeys[2], (DATES, 1, 1), jnp.float32, -0.05, 0.05)
    offset = jax.random.uniform(subkeys[3], (DATES, 1, 1), jnp.float32, -math.pi, math.pi)
    row_axis = jnp.arange(ROWS, dtype=jnp.float32)[None, :, None]
    col_axis = jnp.arange(COLS, dtype=jnp.float32)[None, None, :]
    phases = rate_rows * row_axis + rate_cols * col_axis + offset
    noise = jnp.clip(jax.random.normal(subkeys[4], (DATES, 2, ROWS, COLS), jnp.float32), -4.0, 4.0)
    amplitude = jnp.ones((1, ROWS, 1), jnp.float32)
    cosine = jnp.cos(phases)
    sine = jnp.sin(phases)
    real_part = 0.8 * amplitude * (scene[0] * cosine - scene[1] * sine) + 0.6 * noise[:, 0]
    imag_part = 0.8 * amplitude * (scene[0] * sine + scene[1] * cosine) + 0.6 * noise[:, 1]
    return jnp.clip(jnp.stack([real_part, imag_part], axis=1), -8.0, 8.0)


def draw_secondaries(key, part):
    key = jax.random.fold_in(key, 23)
    dropped = jax.random.randint(key, (DATES,), 1, REACH + 1)
    date_ids = jnp.arange(DATES, dtype=jnp.int32)
    dropped = jnp.where(date_ids == 0, 1, dropped).astype(jnp.int32)
    counter = jnp.arange(1, LINKS + 1, dtype=jnp.int32)[None, :]
    offsets = counter + (counter >= dropped[:, None]).astype(jnp.int32)
    return ((date_ids[:, None] + offsets) % DATES).astype(jnp.int32)


def setup_inputs(seed: int = 0) -> dict:
    splits = jax.random.split(jax.random.key(seed), 3)
    images = draw_images(jax.random.fold_in(splits[2], 71), 0)
    secondaries = draw_secondaries(jax.random.fold_in(splits[2], 71), 0)
    return {"images": images, "secondaries": secondaries}


def multilook(values):
    extent = values.shape
    blocks = values.reshape(extent[:-2] + (extent[-2] // LOOK_R, LOOK_R, extent[-1] // LOOK_C, LOOK_C))
    return blocks.mean(axis=(-3, -1))

def window_last(grid_values, block_count):
    leading = grid_values.shape[:-1]
    head_part = grid_values[..., :block_count * KEEP].reshape(leading + (block_count, KEEP))
    widths = [(0, 0)] * (grid_values.ndim - 1) + [(0, 2 * KEEP - PATCH)]
    extended = jnp.pad(grid_values, widths)
    tail_part = extended[..., KEEP:].reshape(leading + (block_count, KEEP))[..., :PATCH - KEEP]
    return jnp.concatenate([head_part, tail_part], axis=-1)

def patches(grid_values, row_blocks, col_blocks):
    across = window_last(grid_values, col_blocks)
    turned = jnp.moveaxis(across, -3, -1)
    stacked = window_last(turned, row_blocks)
    return jnp.moveaxis(stacked, (-4, -3), (-2, -1))

def box_mean(padded, rows_out, cols_out):
    summed = jnp.zeros(padded.shape[:-2] + (rows_out, cols_out), padded.dtype)
    for row_step in (-1, 0, 1):
        for col_step in (-1, 0, 1):
            summed = summed + padded[..., MARGIN + row_step:MARGIN + row_step + rows_out, MARGIN + col_step:MARGIN + col_step + cols_out]
    return summed / 9.0

def coherence_from(real_pad, imag_pad, first_pad, second_pad, rows_out, cols_out):
    cross_real = box_mean(real_pad, rows_out, cols_out)
    cross_imag = box_mean(imag_pad, rows_out, cols_out)
    energy = box_mean(first_pad, rows_out, cols_out) * box_mean(second_pad, rows_out, cols_out)
    factor = lax.rsqrt(energy + 1e-06)
    return jnp.stack([cross_real * factor, cross_imag * factor], axis=-3)

def weights_of(power):
    smooth = jnp.zeros_like(power)
    for row_step in (-1, 0, 1):
        for col_step in (-1, 0, 1):
            smooth = smooth + jnp.roll(power, (row_step, col_step), axis=(-3, -1))
    smooth = smooth / 9.0
    level = lax.optimization_barrier(jnp.mean(power, axis=(-3, -1), keepdims=True))
    weight = (smooth + level + 1e-06) ** 0.25
    return weight / lax.optimization_barrier(jnp.mean(weight, axis=(-3, -1), keepdims=True))

def centre(values, row_blocks, col_blocks):
    kept = values[..., MARGIN:MARGIN + KEEP, :, MARGIN:MARGIN + KEEP]
    return kept.reshape(kept.shape[:-4] + (row_blocks * KEEP, col_blocks * KEEP))

def goldstein(real_pad, imag_pad, row_blocks, col_blocks):
    field = patches(real_pad, row_blocks, col_blocks) + 1j * patches(imag_pad, row_blocks, col_blocks)
    spectrum = jnp.fft.fft2(field, axes=(-3, -1))
    power = jnp.real(spectrum) ** 2 + jnp.imag(spectrum) ** 2
    result = jnp.fft.ifft2(spectrum * weights_of(power), axes=(-3, -1))
    return jnp.stack([centre(jnp.real(result), row_blocks, col_blocks), centre(jnp.imag(result), row_blocks, col_blocks)], axis=-3)

def reference(images, secondaries):
    rows_out = ROWS // LOOK_R
    cols_out = COLS // LOOK_C
    row_blocks = rows_out // KEEP
    col_blocks = cols_out // KEEP

    def widen(values):
        return jnp.pad(values, [(0, 0)] * (values.ndim - 2) + [(MARGIN, MARGIN), (MARGIN, MARGIN)])

    def one_date(entry):
        index, second_dates = entry
        own_date = lax.dynamic_index_in_dim(images, index, 0, keepdims=False)
        partners = jnp.take(images, second_dates, axis=0)
        pair_real = multilook(own_date[0] * partners[:, 0] + own_date[1] * partners[:, 1])
        pair_imag = multilook(own_date[1] * partners[:, 0] - own_date[0] * partners[:, 1])
        first_power = multilook(own_date[0] ** 2 + own_date[1] ** 2)[None]
        second_power = multilook(partners[:, 0] ** 2 + partners[:, 1] ** 2)
        real_pad = widen(pair_real)
        imag_pad = widen(pair_imag)
        coherent = coherence_from(real_pad, imag_pad, widen(first_power), widen(second_power), rows_out, cols_out)
        filtered = goldstein(real_pad, imag_pad, row_blocks, col_blocks)
        return (filtered, coherent)
    filtered, coherent = lax.map(one_date, (jnp.arange(DATES, dtype=jnp.int32), secondaries))
    return (filtered, coherent)
```

```python
import functools
import math

import jax
import jax.numpy as jnp
import ml_dtypes
import numpy as np
from jax import lax
from jax.experimental import pallas as pl
from jax.experimental.pallas import tpu as pltpu
from jax.sharding import PartitionSpec as P

LOOK_R = 2
LOOK_C = 8
PATCH = 32
KEEP = 24
MARGIN = 4
LANES = 128
BAND = 8
MESH = pl.DeviceIdType.MESH
HIGHEST = lax.Precision.HIGHEST


def tables(rows, cols):
    cells_r, cells_c = rows // LOOK_R, cols // LOOK_C
    blocks = cells_c // KEEP
    halo_r = MARGIN * LOOK_R
    tall = rows + 2 * halo_r

    looks = np.zeros((cols, LANES), np.float32)
    looks[np.arange(cols), np.arange(cols) // LOOK_C] = 1.0 / (LOOK_R * LOOK_C)

    def lane(x):
        if x < 0:
            return cells_c + MARGIN + x
        return x if x < cells_c else x + MARGIN

    ticks = np.arange(PATCH)
    angle = (ticks[:, None] * ticks[None, :] % PATCH) * (2.0 * math.pi / PATCH)
    cosine, sine = np.cos(angle), np.sin(angle)

    pick = np.zeros((PATCH, tall))
    pick[np.arange(tall) // LOOK_R, np.arange(tall)] = 1.0
    row_c, row_s = cosine @ pick, sine @ pick
    box_r = np.zeros((cells_r, PATCH))
    for y in range(cells_r):
        box_r[y, MARGIN + y - 1 : MARGIN + y + 2] = 1.0
    box_r = box_r @ pick
    none = np.zeros_like(box_r)
    row_fwd = np.block([[row_c, row_s], [-row_s, row_c], [box_r, none], [none, box_r]])

    col_c, col_s = np.zeros((LANES, LANES)), np.zeros((LANES, LANES))
    for b in range(blocks):
        for x in range(PATCH):
            at = lane(b * KEEP - MARGIN + x)
            col_c[at, b * PATCH : (b + 1) * PATCH] = cosine[x]
            col_s[at, b * PATCH : (b + 1) * PATCH] = sine[x]
    col_fwd = np.block([[col_c, -col_s], [col_s, col_c]])
    box_c = np.zeros((LANES, LANES))
    for x in range(cells_c):
        for step in (-1, 0, 1):
            box_c[lane(x + step), x] = 1.0

    group = np.kron(np.eye(LANES // PATCH), np.ones((PATCH, PATCH)))

    centre = slice(MARGIN, MARGIN + KEEP)
    row_inv = np.block([[cosine[centre], -sine[centre]], [sine[centre], cosine[centre]]])
    inv_c, inv_s = np.zeros((LANES, LANES)), np.zeros((LANES, LANES))
    for b in range(blocks):
        inv_c[b * PATCH : (b + 1) * PATCH, b * KEEP : (b + 1) * KEEP] = cosine[:, centre]
        inv_s[b * PATCH : (b + 1) * PATCH, b * KEEP : (b + 1) * KEEP] = sine[:, centre]
    col_inv = np.block([[inv_c, inv_s], [-inv_s, inv_c]]) / (PATCH * PATCH)
    single = [row_fwd, box_r, col_fwd, box_c, group, row_inv, col_inv]
    return [looks.astype(ml_dtypes.bfloat16)] + [np.asarray(t, np.float32) for t in single]


def dot(a, b):
    return lax.dot_general(
        a, b, (((1,), (0,)), ((), ())), precision=HIGHEST, preferred_element_type=jnp.float32
    )


def kernel(
    sizes,
    offs_ref,
    img_ref,
    looks_ref,
    row_fwd_ref,
    box_r_ref,
    col_fwd_ref,
    box_c_ref,
    group_ref,
    row_inv_ref,
    col_inv_ref,
    filt_ref,
    coh_ref,
    near,
    far,
    planes,
    edge_l,
    edge_r,
    side_l,
    side_r,
    near_send,
    near_recv,
    far_send,
    far_recv,
    halo_send,
    halo_recv,
):
    dates, n_rows, n_cols = sizes
    rows, cols = img_ref.shape[2], img_ref.shape[3]
    cells_c = cols // LOOK_C
    cells_r = rows // LOOK_R
    halo = MARGIN * LOOK_R
    chunks = rows // BAND
    date, row, col = lax.axis_index("date"), lax.axis_index("row"), lax.axis_index("col")
    odd = lax.rem(date, 2) == 1
    mate = date + 1 - 2 * lax.rem(date, 2)
    before = lax.rem(date + dates - 2, dates)
    after = lax.rem(date + 2, dates)
    steps = [(r, c) for r in (-1, 0, 1) for c in (-1, 0, 1) if (r, c) != (0, 0)]

    def there(step):
        test_r = [None, row < n_rows - 1, row > 0][step[0]]
        test_c = [None, col < n_cols - 1, col > 0][step[1]]
        tests = [t for t in (test_r, test_c) if t is not None]
        return functools.reduce(jnp.logical_and, tests)

    barrier = pltpu.get_barrier_semaphore()
    for other in (before, after, mate):
        pl.semaphore_signal(barrier, inc=1, device_id=(other, row, col), device_id_type=MESH)
    count = jnp.int32(3)
    for step in steps:
        here = there(step)

        @pl.when(here)
        def _():
            pl.semaphore_signal(
                barrier,
                inc=1,
                device_id=(date, row + step[0], col + step[1]),
                device_id_type=MESH,
            )

        count = count + here.astype(jnp.int32)
    pl.semaphore_wait(barrier, count)

    def band(c):
        return pl.ds(c * BAND, BAND)

    def far_copy(c):
        return pltpu.make_async_remote_copy(
            src_ref=img_ref.at[:, :, band(c)],
            dst_ref=far.at[:, :, band(c)],
            send_sem=far_send.at[c],
            recv_sem=far_recv.at[c],
            device_id=(before, row, col),
            device_id_type=MESH,
        )

    def near_copy(c, source):
        return pltpu.make_async_remote_copy(
            src_ref=source.at[:, :, band(c)],
            dst_ref=near.at[:, :, band(c)],
            send_sem=near_send.at[c],
            recv_sem=near_recv.at[c],
            device_id=(mate, row, col),
            device_id_type=MESH,
        )

    for c in range(chunks):
        far_copy(c).start()

        @pl.when(odd)
        def _():
            near_copy(c, img_ref).start()

    for step in steps:

        @pl.when(jnp.logical_not(there(step)))
        def _():
            r, c = step
            at = {-1: slice(0, halo), 0: slice(halo, halo + rows), 1: slice(halo + rows, None)}[r]
            if c == 0:
                planes[:, at] = jnp.zeros_like(planes[:, at])
            else:
                side = side_l if c < 0 else side_r
                side[at] = jnp.zeros_like(side[at])

    first = [[offs_ref[k, l] == l + 1 for l in range(3)] for k in range(2)]

    def process(c):
        at = band(c)

        def date_image(i):
            source = (img_ref, near, far)[i // 2]
            return source[i % 2, 0, at], source[i % 2, 1, at]

        images = [date_image(i) for i in range(6)]
        parts = []
        for k in range(2):
            a_r, a_i = images[k]
            for l in range(3):
                low, high = images[k + l + 1], images[k + l + 2]
                b_r = jnp.where(first[k][l], low[0], high[0])
                b_i = jnp.where(first[k][l], low[1], high[1])
                parts += [a_r * b_r + a_i * b_i, a_i * b_r - a_r * b_i]
        parts += [r * r + i * i for r, i in images]
        stacked = jnp.concatenate(parts, axis=0)
        high = stacked.astype(jnp.bfloat16)
        low = (stacked - high.astype(jnp.float32)).astype(jnp.bfloat16)
        looks = looks_ref[...]
        summed = jnp.dot(high, looks, preferred_element_type=jnp.float32) + jnp.dot(
            low, looks, preferred_element_type=jnp.float32
        )
        for p in range(len(parts)):
            planes[p, pl.ds(halo + c * BAND, BAND)] = summed[p * BAND : (p + 1) * BAND]

    for c in range(chunks):
        far_copy(c).wait_recv()

        @pl.when(jnp.logical_not(odd))
        def _():
            near_copy(c, far).start()

        near_copy(c, img_ref).wait_recv()
        process(c)

    count_planes = planes.shape[0]
    lanes = lax.broadcasted_iota(jnp.int32, (rows, LANES), 1)
    pack_l = jnp.zeros((rows, LANES), jnp.float32)
    pack_r = jnp.zeros((rows, LANES), jnp.float32)
    for p in range(count_planes):
        own = planes[p, halo : halo + rows]
        mine = (lanes >= p * MARGIN) & (lanes < (p + 1) * MARGIN)
        pack_l = jnp.where(mine, pltpu.roll(own, (p * MARGIN) % LANES, 1), pack_l)
        shift = (p * MARGIN - (cells_c - MARGIN)) % LANES
        pack_r = jnp.where(mine, pltpu.roll(own, shift, 1), pack_r)
    edge_l[...] = pack_l
    edge_r[...] = pack_r

    def halo_copy(n, step):
        r, c = step
        source_rows = {-1: slice(0, halo), 0: slice(0, rows), 1: slice(rows - halo, rows)}[r]
        target_rows = {
            -1: slice(halo + rows, rows + 2 * halo),
            0: slice(halo, halo + rows),
            1: slice(0, halo),
        }[r]
        if c == 0:
            shifted = slice(source_rows.start + halo, source_rows.stop + halo)
            source, target = planes.at[:, shifted], planes.at[:, target_rows]
        elif c < 0:
            source, target = edge_l.at[source_rows], side_r.at[target_rows]
        else:
            source, target = edge_r.at[source_rows], side_l.at[target_rows]
        return pltpu.make_async_remote_copy(
            src_ref=source,
            dst_ref=target,
            send_sem=halo_send.at[n],
            recv_sem=halo_recv.at[n],
            device_id=(date, row + r, col + c),
            device_id_type=MESH,
        )

    for n, step in enumerate(steps):

        @pl.when(there(step))
        def _():
            halo_copy(n, step).start()

    for n, step in enumerate(steps):
        @pl.when(there((-step[0], -step[1])))
        def _():
            halo_copy(n, step).wait_recv()

    tall = rows + 2 * halo
    wide = lax.broadcasted_iota(jnp.int32, (tall, LANES), 1)
    in_l = (wide >= cells_c) & (wide < cells_c + MARGIN)
    in_r = (wide >= cells_c + MARGIN) & (wide < cells_c + 2 * MARGIN)
    got_l, got_r = side_l[...], side_r[...]

    def whole(p):
        left = pltpu.roll(got_l, (cells_c - p * MARGIN) % LANES, 1)
        right = pltpu.roll(got_r, (cells_c + MARGIN - p * MARGIN) % LANES, 1)
        return jnp.where(in_l, left, jnp.where(in_r, right, planes[p]))

    row_fwd, box_r = row_fwd_ref[...], box_r_ref[...]
    spectra, boxes = [], []
    for p in range(6):
        both = jnp.concatenate([whole(2 * p), whole(2 * p + 1)], axis=0)
        out = dot(row_fwd, both)
        spectra.append(jnp.concatenate([out[:PATCH], out[PATCH : 2 * PATCH]], axis=1))
        boxes.append(out[2 * PATCH :])
    for p in range(12, 18):
        boxes.append(dot(box_r, whole(p)))
    box = dot(jnp.concatenate(boxes, axis=0), box_c_ref[...]) * (1.0 / 9.0)
    base = 12 * cells_r
    power = [box[base + i * cells_r : base + (i + 1) * cells_r] for i in range(6)]
    for k in range(2):
        for l in range(3):
            second = jnp.where(first[k][l], power[k + l + 1], power[k + l + 2])
            factor = lax.rsqrt(power[k] * second + 1e-06)
            for part in range(2):
                at = ((k * 3 + l) * 2 + part) * cells_r
                coh_ref[k, l, part] = (box[at : at + cells_r] * factor)[:, :cells_c]

    z = dot(jnp.concatenate(spectra, axis=0), col_fwd_ref[...])
    z_r, z_i = z[:, :LANES], z[:, LANES:]
    energy = z_r * z_r + z_i * z_i
    group = group_ref[...]
    lane32 = lax.rem(lax.broadcasted_iota(jnp.int32, (6 * PATCH, LANES), 1), PATCH)
    left = jnp.where(lane32 == 0, pltpu.roll(energy, LANES - PATCH + 1, 1), pltpu.roll(energy, 1, 1))
    right = jnp.where(
        lane32 == PATCH - 1, pltpu.roll(energy, PATCH - 1, 1), pltpu.roll(energy, LANES - 1, 1)
    )
    across = energy + left + right

    def per_patch(values):
        sums = [
            jnp.sum(values[p * PATCH : (p + 1) * PATCH], axis=0, keepdims=True) for p in range(6)
        ]
        sums += [jnp.zeros((2, LANES), jnp.float32)]
        return dot(jnp.concatenate(sums, axis=0), group) * (1.0 / (PATCH * PATCH))

    level = per_patch(energy)
    weights = []
    for p in range(6):
        part = across[p * PATCH : (p + 1) * PATCH]
        smooth = (part + pltpu.roll(part, 1, 0) + pltpu.roll(part, PATCH - 1, 0)) * (1.0 / 9.0)
        weights.append(jnp.sqrt(jnp.sqrt(smooth + level[p : p + 1] + 1e-06)))
    scale = 1.0 / per_patch(jnp.concatenate(weights, axis=0))
    row_inv = row_inv_ref[...]
    back = []
    for p in range(6):
        weight = weights[p] * scale[p : p + 1]
        at = slice(p * PATCH, (p + 1) * PATCH)
        both = jnp.concatenate([z_r[at] * weight, z_i[at] * weight], axis=0)
        out = dot(row_inv, both)
        back.append(jnp.concatenate([out[:KEEP], out[KEEP:]], axis=1))
    final = dot(jnp.concatenate(back, axis=0), col_inv_ref[...])
    for p in range(6):
        at = slice(p * KEEP, (p + 1) * KEEP)
        filt_ref[p // 3, p % 3, 0] = final[at, :cells_c]
        filt_ref[p // 3, p % 3, 1] = final[at, LANES : LANES + cells_c]

    for c in range(chunks):
        far_copy(c).wait_send()
        near_copy(c, img_ref).wait_send()
    for n, step in enumerate(steps):

        @pl.when(there(step))
        def _():
            halo_copy(n, step).wait_send()


def body(images, secondaries):
    per_device, _, rows, cols = images.shape
    links = secondaries.shape[1]
    dates = lax.axis_size("date")
    assert per_device == 2 and links == 3 and rows == 2 * KEEP and dates % 2 == 0 and dates > 4
    own = lax.axis_index("date") * per_device + jnp.arange(per_device, dtype=jnp.int32)
    offsets = (secondaries - own[:, None]) % (per_device * dates)
    cells_r, cells_c = rows // LOOK_R, cols // LOOK_C
    tall = rows + 2 * MARGIN * LOOK_R
    chunks = rows // BAND
    out = jax.ShapeDtypeStruct((per_device, links, 2, cells_r, cells_c), jnp.float32)
    constants = [jnp.asarray(t) for t in tables(rows, cols)]
    vmem = pl.BlockSpec(memory_space=pltpu.VMEM)
    sizes = (dates, lax.axis_size("row"), lax.axis_size("col"))
    dma = pltpu.SemaphoreType.DMA
    return pl.pallas_call(
        functools.partial(kernel, sizes),
        out_shape=(out, out),
        in_specs=[pl.BlockSpec(memory_space=pltpu.SMEM)] + [vmem] * (1 + len(constants)),
        out_specs=(vmem, vmem),
        scratch_shapes=[
            pltpu.VMEM(images.shape, jnp.float32),
            pltpu.VMEM(images.shape, jnp.float32),
            pltpu.VMEM((18, tall, LANES), jnp.float32),
            pltpu.VMEM((rows, LANES), jnp.float32),
            pltpu.VMEM((rows, LANES), jnp.float32),
            pltpu.VMEM((tall, LANES), jnp.float32),
            pltpu.VMEM((tall, LANES), jnp.float32),
            dma((chunks,)),
            dma((chunks,)),
            dma((chunks,)),
            dma((chunks,)),
            dma((8,)),
            dma((8,)),
        ],
        compiler_params=pltpu.CompilerParams(
            collective_id=0, has_side_effects=True, vmem_limit_bytes=32 * 1024 * 1024
        ),
        cost_estimate=pl.CostEstimate(flops=10**9, bytes_accessed=10**6, transcendentals=0),
    )(offsets, images, *constants)


def solution(mesh):
    in_specs = (P("date", None, "row", "col"), P("date", None))
    out_specs = (P("date", None, None, "row", "col"), P("date", None, None, "row", "col"))
    return jax.shard_map(body, mesh=mesh, in_specs=in_specs, out_specs=out_specs, check_vma=False)
```

```python
import functools
import math

import jax
import jax.numpy as jnp
import ml_dtypes
import numpy as np
from jax import lax
from jax.experimental import pallas as pl
from jax.experimental.pallas import tpu as pltpu
from jax.sharding import PartitionSpec as P

LOOK_R = 2
LOOK_C = 8
PATCH = 32
KEEP = 24
MARGIN = 4
LANES = 128
BAND = 8
MESH = pl.DeviceIdType.MESH


def tables(rows, cols):
    cells_r, cells_c = rows // LOOK_R, cols // LOOK_C
    blocks = cells_c // KEEP
    halo_r = MARGIN * LOOK_R
    tall = rows + 2 * halo_r

    def lane(x):
        if x < 0:
            return cells_c + MARGIN + x
        return x if x < cells_c else x + MARGIN

    ticks = np.arange(PATCH)
    angle = (ticks[:, None] * ticks[None, :] % PATCH) * (2.0 * math.pi / PATCH)
    cosine, sine = np.cos(angle), np.sin(angle)

    pick = np.zeros((PATCH, tall))
    pick[np.arange(tall) // LOOK_R, np.arange(tall)] = 1.0
    row_c, row_s = cosine @ pick, sine @ pick
    box_r = np.zeros((cells_r, PATCH))
    for y in range(cells_r):
        box_r[y, MARGIN + y - 1 : MARGIN + y + 2] = 1.0
    box_r = box_r @ pick
    none = np.zeros_like(box_r)
    row_fwd = np.block([[row_c, row_s], [-row_s, row_c], [box_r, none], [none, box_r]])

    col_c, col_s = np.zeros((LANES, LANES)), np.zeros((LANES, LANES))
    for b in range(blocks):
        for x in range(PATCH):
            at = lane(b * KEEP - MARGIN + x)
            col_c[at, b * PATCH : (b + 1) * PATCH] = cosine[x]
            col_s[at, b * PATCH : (b + 1) * PATCH] = sine[x]
    centre = slice(MARGIN, MARGIN + KEEP)
    row_inv = np.block([[cosine[centre], -sine[centre]], [sine[centre], cosine[centre]]])
    inv_c, inv_s = np.zeros((LANES, LANES)), np.zeros((LANES, LANES))
    for b in range(blocks):
        inv_c[b * PATCH : (b + 1) * PATCH, b * KEEP : (b + 1) * KEEP] = cosine[:, centre]
        inv_s[b * PATCH : (b + 1) * PATCH, b * KEEP : (b + 1) * KEEP] = sine[:, centre]
    scale = 1.0 / (PATCH * PATCH)
    row_inv = np.pad(row_inv, ((0, 0), (0, LANES - 2 * PATCH)))
    stacked = [row_fwd, col_c, col_s, inv_c * scale, inv_s * scale, row_inv]
    whole = np.concatenate(stacked, axis=0).astype(np.float32)
    high = whole.astype(ml_dtypes.bfloat16)
    low = (whole - high.astype(np.float32)).astype(ml_dtypes.bfloat16)
    starts = np.cumsum([0] + [t.shape[0] for t in stacked])
    return np.stack([high, low]), [int(n) for n in starts]


def split(x):
    high = x.astype(jnp.bfloat16)
    return high, (x - high.astype(jnp.float32)).astype(jnp.bfloat16)


def mul(a, b):
    return lax.dot_general(a, b, (((1,), (0,)), ((), ())), preferred_element_type=jnp.float32)


def dot(a, b):
    return mul(a[0], b[0]) + (mul(a[1], b[0]) + mul(a[0], b[1]))


def dot_exact(x, b):
    high, low = split(x)
    return mul(high, b) + mul(low, b)


def kernel(
    sizes,
    starts,
    sec_ref,
    img_hbm,
    table_hbm,
    filt_ref,
    coh_ref,
    img_ref,
    table,
    near,
    far,
    planes,
    edge_l,
    edge_r,
    side_l,
    side_r,
    near_send,
    near_recv,
    far_send,
    far_recv,
    halo_send,
    halo_recv,
    local_sem,
):
    dates, n_rows, n_cols = sizes
    rows, cols = img_ref.shape[2], img_ref.shape[3]
    cells_c = cols // LOOK_C
    cells_r = rows // LOOK_R
    halo = MARGIN * LOOK_R
    chunks = rows // BAND
    date, row, col = lax.axis_index("date"), lax.axis_index("row"), lax.axis_index("col")
    odd = lax.rem(date, 2) == 1
    mate = date + 1 - 2 * lax.rem(date, 2)
    before = lax.rem(date + dates - 2, dates)
    after = lax.rem(date + 2, dates)
    steps = [(r, c) for r in (-1, 0, 1) for c in (-1, 0, 1) if (r, c) != (0, 0)]

    def there(step):
        test_r = [None, row < n_rows - 1, row > 0][step[0]]
        test_c = [None, col < n_cols - 1, col > 0][step[1]]
        tests = [t for t in (test_r, test_c) if t is not None]
        return functools.reduce(jnp.logical_and, tests)

    order = [0, chunks - 1] + list(range(1, chunks - 1))
    load_img = pltpu.make_async_copy(img_hbm, img_ref, local_sem.at[0])
    load_table = pltpu.make_async_copy(table_hbm, table, local_sem.at[1])
    load_img.start()
    load_table.start()
    barrier = pltpu.get_barrier_semaphore()
    for other in (before, after, mate):
        pl.semaphore_signal(barrier, inc=1, device_id=(other, row, col), device_id_type=MESH)
    count = jnp.int32(3)
    for step in steps:
        here = there(step)

        @pl.when(here)
        def _():
            pl.semaphore_signal(
                barrier,
                inc=1,
                device_id=(date, row + step[0], col + step[1]),
                device_id_type=MESH,
            )

        count = count + here.astype(jnp.int32)
    pl.semaphore_wait(barrier, count)

    def band(c):
        return pl.ds(c * BAND, BAND)

    def far_copy(c):
        return pltpu.make_async_remote_copy(
            src_ref=img_hbm.at[:, :, band(c)],
            dst_ref=far.at[:, :, band(c)],
            send_sem=far_send.at[c],
            recv_sem=far_recv.at[c],
            device_id=(before, row, col),
            device_id_type=MESH,
        )

    def near_copy(c, source):
        return pltpu.make_async_remote_copy(
            src_ref=source.at[:, :, band(c)],
            dst_ref=near.at[:, :, band(c)],
            send_sem=near_send.at[c],
            recv_sem=near_recv.at[c],
            device_id=(mate, row, col),
            device_id_type=MESH,
        )

    for c in order:
        far_copy(c).start()

        @pl.when(odd)
        def _():
            near_copy(c, img_hbm).start()

    for step in steps:

        @pl.when(jnp.logical_not(there(step)))
        def _():
            r, c = step
            at = {-1: slice(0, halo), 0: slice(halo, halo + rows), 1: slice(halo + rows, None)}[r]
            if c == 0:
                planes[:, at] = jnp.zeros_like(planes[:, at])
            else:
                side = side_l if c < 0 else side_r
                side[at] = jnp.zeros_like(side[at])

    total = 2 * dates

    def is_first(k, l):
        return lax.rem(sec_ref[k, l] - (2 * date + k) + total, total) == l + 1

    first = [[is_first(k, l) for l in range(3)] for k in range(2)]

    def lane_of(x):
        return jnp.where(x < 0, cells_c + MARGIN + x, jnp.where(x < cells_c, x, x + MARGIN))

    cell = lax.broadcasted_iota(jnp.int32, (cols, LANES), 0) // LOOK_C
    looks = jnp.where(
        cell == lax.broadcasted_iota(jnp.int32, (cols, LANES), 1), 1.0 / (LOOK_R * LOOK_C), 0.0
    ).astype(jnp.bfloat16)
    from_lane = lax.broadcasted_iota(jnp.int32, (LANES, LANES), 0)
    to_lane = lax.broadcasted_iota(jnp.int32, (LANES, LANES), 1)
    box_c = (from_lane == to_lane) | (from_lane == lane_of(to_lane - 1))
    box_c = box_c | (from_lane == lane_of(to_lane + 1))
    box_c = jnp.where(box_c & (to_lane < cells_c), 1.0, 0.0).astype(jnp.bfloat16)
    group = jnp.where(from_lane // PATCH == to_lane // PATCH, 1.0, 0.0).astype(jnp.bfloat16)

    def process(c):
        at = band(c)

        def date_image(i):
            source = (img_ref, near, far)[i // 2]
            return source[i % 2, 0, at], source[i % 2, 1, at]

        images = [date_image(i) for i in range(6)]
        parts = []
        for k in range(2):
            a_r, a_i = images[k]
            for l in range(3):
                low, high = images[k + l + 1], images[k + l + 2]
                b_r = jnp.where(first[k][l], low[0], high[0])
                b_i = jnp.where(first[k][l], low[1], high[1])
                parts += [a_r * b_r + a_i * b_i, a_i * b_r - a_r * b_i]
        parts += [r * r + i * i for r, i in images]
        summed = dot_exact(jnp.concatenate(parts, axis=0), looks)
        lanes = lax.broadcasted_iota(jnp.int32, (BAND, LANES), 1)
        pack_l = jnp.zeros((BAND, LANES), jnp.float32)
        pack_r = jnp.zeros((BAND, LANES), jnp.float32)
        for p in range(len(parts)):
            own = summed[p * BAND : (p + 1) * BAND]
            planes[p, pl.ds(halo + c * BAND, BAND)] = own
            mine = (lanes >= p * MARGIN) & (lanes < (p + 1) * MARGIN)
            pack_l = jnp.where(mine, pltpu.roll(own, (p * MARGIN) % LANES, 1), pack_l)
            shift = (p * MARGIN - (cells_c - MARGIN)) % LANES
            pack_r = jnp.where(mine, pltpu.roll(own, shift, 1), pack_r)
        edge_l[at] = pack_l
        edge_r[at] = pack_r

    messages = []
    for step in steps:
        if step[0] == 0:
            messages += [(step, c * BAND, BAND, c) for c in range(chunks)]
        else:
            c = 0 if step[0] < 0 else chunks - 1
            messages.append((step, c * BAND, BAND, c))

    def halo_copy(n):
        (r, c), start, size, _ = messages[n]
        source_at = pl.ds(start, size)
        target_at = pl.ds(halo + start - r * rows, size)
        if c == 0:
            source, target = planes.at[:, pl.ds(halo + start, size)], planes.at[:, target_at]
        elif c < 0:
            source, target = edge_l.at[source_at], side_r.at[target_at]
        else:
            source, target = edge_r.at[source_at], side_l.at[target_at]
        return pltpu.make_async_remote_copy(
            src_ref=source,
            dst_ref=target,
            send_sem=halo_send.at[n],
            recv_sem=halo_recv.at[n],
            device_id=(date, row + r, col + c),
            device_id_type=MESH,
        )

    load_img.wait()
    for c in order:
        far_copy(c).wait_recv()

        @pl.when(jnp.logical_not(odd))
        def _():
            near_copy(c, far).start()

        near_copy(c, img_hbm).wait_recv()
        process(c)
        for step in steps:

            @pl.when(there(step))
            def _():
                for n, message in enumerate(messages):
                    if message[0] == step and message[3] == c:
                        halo_copy(n).start()

    load_table.wait()

    def part_of(i, j, lanes=LANES):
        rows_at = slice(starts[i], starts[j])
        return table[0, rows_at, :lanes], table[1, rows_at, :lanes]

    row_fwd = part_of(0, 1)
    box_r = table[0, starts[0] + 2 * PATCH : starts[0] + 2 * PATCH + cells_r, : rows + 2 * halo]
    col_fwd = [
        jnp.concatenate(
            [
                jnp.concatenate([cosine, -sine], axis=1),
                jnp.concatenate([sine, cosine], axis=1),
            ],
            axis=0,
        )
        for cosine, sine in zip(part_of(1, 2), part_of(2, 3))
    ]
    col_inv = [
        jnp.concatenate(
            [
                jnp.concatenate([cosine, sine], axis=1),
                jnp.concatenate([-sine, cosine], axis=1),
            ],
            axis=0,
        )
        for cosine, sine in zip(part_of(3, 4), part_of(4, 5))
    ]
    row_inv = part_of(5, 6, 2 * PATCH)

    for step in steps:

        @pl.when(there((-step[0], -step[1])))
        def _():
            for n, message in enumerate(messages):
                if message[0] == step:
                    halo_copy(n).wait_recv()

    tall = rows + 2 * halo
    wide = lax.broadcasted_iota(jnp.int32, (tall, LANES), 1)
    in_l = (wide >= cells_c) & (wide < cells_c + MARGIN)
    in_r = (wide >= cells_c + MARGIN) & (wide < cells_c + 2 * MARGIN)
    got_l, got_r = side_l[...], side_r[...]

    def whole(p):
        left = pltpu.roll(got_l, (cells_c - p * MARGIN) % LANES, 1)
        right = pltpu.roll(got_r, (cells_c + MARGIN - p * MARGIN) % LANES, 1)
        return jnp.where(in_l, left, jnp.where(in_r, right, planes[p]))

    def lane_tiles(x):
        return [x[:, i : i + LANES] for i in range(0, x.shape[1], LANES)]

    fields = [jnp.concatenate([whole(2 * p), whole(2 * p + 1)], axis=0) for p in range(6)]
    outs = lane_tiles(dot(row_fwd, split(jnp.concatenate(fields, axis=1))))
    spectra = [jnp.concatenate([o[:PATCH], o[PATCH : 2 * PATCH]], axis=1) for o in outs]
    boxes = [o[2 * PATCH :] for o in outs]
    high, low = split(jnp.concatenate([whole(p) for p in range(12, 18)], axis=1))
    boxes += lane_tiles(mul(box_r, high) + mul(box_r, low))
    box = dot_exact(jnp.concatenate(boxes, axis=0), box_c) * (1.0 / 9.0)
    base = 12 * cells_r
    power = [box[base + i * cells_r : base + (i + 1) * cells_r] for i in range(6)]
    for k in range(2):
        for l in range(3):
            second = jnp.where(first[k][l], power[k + l + 1], power[k + l + 2])
            factor = lax.rsqrt(power[k] * second + 1e-06)
            for part in range(2):
                at = ((k * 3 + l) * 2 + part) * cells_r
                coh_ref[k, l, part] = (box[at : at + cells_r] * factor)[:, :cells_c]

    z = dot(split(jnp.concatenate(spectra, axis=0)), col_fwd)
    z_r, z_i = z[:, :LANES], z[:, LANES:]
    energy = z_r * z_r + z_i * z_i
    lane32 = lax.rem(lax.broadcasted_iota(jnp.int32, (6 * PATCH, LANES), 1), PATCH)
    left = jnp.where(lane32 == 0, pltpu.roll(energy, LANES - PATCH + 1, 1), pltpu.roll(energy, 1, 1))
    right = jnp.where(
        lane32 == PATCH - 1, pltpu.roll(energy, PATCH - 1, 1), pltpu.roll(energy, LANES - 1, 1)
    )
    across = energy + left + right

    def per_patch(values):
        sums = [
            jnp.sum(values[p * PATCH : (p + 1) * PATCH], axis=0, keepdims=True) for p in range(6)
        ]
        sums += [jnp.zeros((2, LANES), jnp.float32)]
        return dot_exact(jnp.concatenate(sums, axis=0), group) * (1.0 / (PATCH * PATCH))

    level = per_patch(energy)
    weights = []
    for p in range(6):
        part = across[p * PATCH : (p + 1) * PATCH]
        smooth = (part + pltpu.roll(part, 1, 0) + pltpu.roll(part, PATCH - 1, 0)) * (1.0 / 9.0)
        weights.append(jnp.sqrt(jnp.sqrt(smooth + level[p : p + 1] + 1e-06)))
    scale = 1.0 / per_patch(jnp.concatenate(weights, axis=0))
    filtered = []
    for p in range(6):
        weight = weights[p] * scale[p : p + 1]
        at = slice(p * PATCH, (p + 1) * PATCH)
        filtered.append(jnp.concatenate([z_r[at] * weight, z_i[at] * weight], axis=0))
    outs = lane_tiles(dot(row_inv, split(jnp.concatenate(filtered, axis=1))))
    back = [jnp.concatenate([o[:KEEP], o[KEEP:]], axis=1) for o in outs]
    final = dot(split(jnp.concatenate(back, axis=0)), col_inv)
    for p in range(6):
        at = slice(p * KEEP, (p + 1) * KEEP)
        filt_ref[p // 3, p % 3, 0] = final[at, :cells_c]
        filt_ref[p // 3, p % 3, 1] = final[at, LANES : LANES + cells_c]

    for c in range(chunks):
        far_copy(c).wait_send()
        near_copy(c, img_hbm).wait_send()
    for step in steps:

        @pl.when(there(step))
        def _():
            for n, message in enumerate(messages):
                if message[0] == step:
                    halo_copy(n).wait_send()


def body(images, secondaries):
    per_device, _, rows, cols = images.shape
    links = secondaries.shape[1]
    dates = lax.axis_size("date")
    assert per_device == 2 and links == 3 and rows == 2 * KEEP and dates % 2 == 0 and dates > 4
    cells_r, cells_c = rows // LOOK_R, cols // LOOK_C
    tall = rows + 2 * MARGIN * LOOK_R
    chunks = rows // BAND
    out = jax.ShapeDtypeStruct((per_device, links, 2, cells_r, cells_c), jnp.float32)
    table, starts = tables(rows, cols)
    vmem = pl.BlockSpec(memory_space=pltpu.VMEM)
    hbm = pl.BlockSpec(memory_space=pltpu.HBM)
    sizes = (dates, lax.axis_size("row"), lax.axis_size("col"))
    dma = pltpu.SemaphoreType.DMA
    return pl.pallas_call(
        functools.partial(kernel, sizes, starts),
        out_shape=(out, out),
        in_specs=[pl.BlockSpec(memory_space=pltpu.SMEM), hbm, hbm],
        out_specs=(vmem, vmem),
        scratch_shapes=[
            pltpu.VMEM(images.shape, jnp.float32),
            pltpu.VMEM(table.shape, jnp.bfloat16),
            pltpu.VMEM(images.shape, jnp.float32),
            pltpu.VMEM(images.shape, jnp.float32),
            pltpu.VMEM((18, tall, LANES), jnp.float32),
            pltpu.VMEM((rows, LANES), jnp.float32),
            pltpu.VMEM((rows, LANES), jnp.float32),
            pltpu.VMEM((tall, LANES), jnp.float32),
            pltpu.VMEM((tall, LANES), jnp.float32),
            dma((chunks,)),
            dma((chunks,)),
            dma((chunks,)),
            dma((chunks,)),
            dma((6 + 2 * chunks,)),
            dma((6 + 2 * chunks,)),
            dma((2,)),
        ],
        compiler_params=pltpu.CompilerParams(
            collective_id=0, has_side_effects=True, vmem_limit_bytes=32 * 1024 * 1024
        ),
        cost_estimate=pl.CostEstimate(flops=10**9, bytes_accessed=10**6, transcendentals=0),
    )(secondaries, images, jnp.asarray(table))


def solution(mesh):
    in_specs = (P("date", None, "row", "col"), P("date", None))
    out_specs = (P("date", None, None, "row", "col"), P("date", None, None, "row", "col"))
    return jax.shard_map(body, mesh=mesh, in_specs=in_specs, out_specs=out_specs, check_vma=False)
```

```python
import functools
import math

import jax
import jax.numpy as jnp
import ml_dtypes
import numpy as np
from jax import lax
from jax.experimental import pallas as pl
from jax.experimental.pallas import tpu as pltpu
from jax.sharding import PartitionSpec as P

LOOK_R = 2
LOOK_C = 8
PATCH = 32
KEEP = 24
MARGIN = 4
LANES = 128
BAND = 8
PIECE = 256
VMEM_BYTES = 64 * 1024 * 1024 - 64 * 1024
MESH = pl.DeviceIdType.MESH


def tables(rows, cols):
    cells_r, cells_c = rows // LOOK_R, cols // LOOK_C
    blocks = cells_c // KEEP
    halo_r = MARGIN * LOOK_R
    tall = rows + 2 * halo_r

    def lane(x):
        if x < 0:
            return cells_c + MARGIN + x
        return x if x < cells_c else x + MARGIN

    ticks = np.arange(PATCH)
    angle = (ticks[:, None] * ticks[None, :] % PATCH) * (2.0 * math.pi / PATCH)
    cosine, sine = np.cos(angle), np.sin(angle)

    pick = np.zeros((PATCH, tall))
    pick[np.arange(tall) // LOOK_R, np.arange(tall)] = 1.0
    row_c, row_s = cosine @ pick, sine @ pick
    box_r = np.zeros((cells_r, PATCH))
    for y in range(cells_r):
        box_r[y, MARGIN + y - 1 : MARGIN + y + 2] = 1.0
    box_r = box_r @ pick
    none = np.zeros_like(box_r)
    row_fwd = np.block([[row_c, row_s], [-row_s, row_c], [box_r, none], [none, box_r]])

    col_c, col_s = np.zeros((LANES, LANES)), np.zeros((LANES, LANES))
    for b in range(blocks):
        for x in range(PATCH):
            at = lane(b * KEEP - MARGIN + x)
            col_c[at, b * PATCH : (b + 1) * PATCH] = cosine[x]
            col_s[at, b * PATCH : (b + 1) * PATCH] = sine[x]
    centre = slice(MARGIN, MARGIN + KEEP)
    row_inv = np.block([[cosine[centre], -sine[centre]], [sine[centre], cosine[centre]]])
    inv_c, inv_s = np.zeros((LANES, LANES)), np.zeros((LANES, LANES))
    for b in range(blocks):
        inv_c[b * PATCH : (b + 1) * PATCH, b * KEEP : (b + 1) * KEEP] = cosine[:, centre]
        inv_s[b * PATCH : (b + 1) * PATCH, b * KEEP : (b + 1) * KEEP] = sine[:, centre]
    scale = 1.0 / (PATCH * PATCH)
    row_inv = np.pad(row_inv, ((0, 0), (0, LANES - 2 * PATCH)))
    stacked = [row_fwd, col_c, col_s, inv_c * scale, inv_s * scale, row_inv]
    whole = np.concatenate(stacked, axis=0).astype(np.float32)
    high = whole.astype(ml_dtypes.bfloat16)
    low = (whole - high.astype(np.float32)).astype(ml_dtypes.bfloat16)
    starts = np.cumsum([0] + [t.shape[0] for t in stacked])
    return np.stack([high, low]), [int(n) for n in starts]


def split(x):
    high = x.astype(jnp.bfloat16)
    return high, (x - high.astype(jnp.float32)).astype(jnp.bfloat16)


def mul(a, b):
    return lax.dot_general(a, b, (((1,), (0,)), ((), ())), preferred_element_type=jnp.float32)


def dot(a, b):
    return mul(a[0], b[0]) + (mul(a[1], b[0]) + mul(a[0], b[1]))


def dot_exact(x, b):
    high, low = split(x)
    return mul(high, b) + mul(low, b)


def kernel(
    sizes,
    starts,
    sec_hbm,
    img_hbm,
    table_hbm,
    filt_ref,
    coh_ref,
    sec_ref,
    img_ref,
    table,
    near,
    far,
    planes,
    edge_l,
    edge_r,
    side_l,
    side_r,
    near_send,
    near_recv,
    far_send,
    far_recv,
    halo_send,
    halo_recv,
    local_sem,
):
    dates, n_rows, n_cols = sizes
    rows, cols = img_ref.shape[2], img_ref.shape[3]
    cells_c = cols // LOOK_C
    cells_r = rows // LOOK_R
    halo = MARGIN * LOOK_R
    chunks = rows // BAND
    date, row, col = lax.axis_index("date"), lax.axis_index("row"), lax.axis_index("col")
    odd = lax.rem(date, 2) == 1
    mate = date + 1 - 2 * lax.rem(date, 2)
    before = lax.rem(date + dates - 2, dates)
    after = lax.rem(date + 2, dates)
    steps = [(r, c) for r in (-1, 0, 1) for c in (-1, 0, 1) if (r, c) != (0, 0)]

    def there(step):
        test_r = [None, row < n_rows - 1, row > 0][step[0]]
        test_c = [None, col < n_cols - 1, col > 0][step[1]]
        tests = [t for t in (test_r, test_c) if t is not None]
        return functools.reduce(jnp.logical_and, tests)

    order = [0, chunks - 1] + list(range(1, chunks - 1))
    load_img = pltpu.make_async_copy(img_hbm, img_ref, local_sem.at[0])
    load_table = pltpu.make_async_copy(table_hbm, table, local_sem.at[1])
    load_sec = pltpu.make_async_copy(sec_hbm, sec_ref, local_sem.at[2])
    load_sec.start()
    load_img.start()
    load_table.start()
    barrier = pltpu.get_barrier_semaphore()
    for other in (before, after, mate):
        pl.semaphore_signal(barrier, inc=1, device_id=(other, row, col), device_id_type=MESH)
    count = jnp.int32(3)
    for step in steps:
        here = there(step)

        @pl.when(here)
        def _():
            pl.semaphore_signal(
                barrier,
                inc=1,
                device_id=(date, row + step[0], col + step[1]),
                device_id_type=MESH,
            )

        count = count + here.astype(jnp.int32)
    pl.semaphore_wait(barrier, count)

    def band(c):
        return pl.ds(c * BAND, BAND)

    pieces = cols // PIECE

    def far_copy(c, h):
        part = (slice(None), slice(None), band(c), pl.ds(h * PIECE, PIECE))
        return pltpu.make_async_remote_copy(
            src_ref=img_hbm.at[part],
            dst_ref=far.at[part],
            send_sem=far_send.at[c * pieces + h],
            recv_sem=far_recv.at[c * pieces + h],
            device_id=(before, row, col),
            device_id_type=MESH,
        )

    def near_copy(c, h, source):
        part = (slice(None), slice(None), band(c), pl.ds(h * PIECE, PIECE))
        return pltpu.make_async_remote_copy(
            src_ref=source.at[part],
            dst_ref=near.at[part],
            send_sem=near_send.at[c * pieces + h],
            recv_sem=near_recv.at[c * pieces + h],
            device_id=(mate, row, col),
            device_id_type=MESH,
        )

    for c in order:
        for h in range(pieces):
            far_copy(c, h).start()

            @pl.when(odd)
            def _():
                near_copy(c, h, img_hbm).start()

    for step in steps:

        @pl.when(jnp.logical_not(there(step)))
        def _():
            r, c = step
            at = {-1: slice(0, halo), 0: slice(halo, halo + rows), 1: slice(halo + rows, None)}[r]
            if c == 0:
                planes[:, at] = jnp.zeros_like(planes[:, at])
            else:
                side = side_l if c < 0 else side_r
                side[at] = jnp.zeros_like(side[at])

    total = 2 * dates
    load_sec.wait()

    def is_first(k, l):
        return lax.rem(sec_ref[k, l] - (2 * date + k) + total, total) == l + 1

    first = [[is_first(k, l) for l in range(3)] for k in range(2)]

    def lane_of(x):
        return jnp.where(x < 0, cells_c + MARGIN + x, jnp.where(x < cells_c, x, x + MARGIN))

    cell = lax.broadcasted_iota(jnp.int32, (cols, LANES), 0) // LOOK_C
    looks = jnp.where(
        cell == lax.broadcasted_iota(jnp.int32, (cols, LANES), 1), 1.0 / (LOOK_R * LOOK_C), 0.0
    ).astype(jnp.bfloat16)
    from_lane = lax.broadcasted_iota(jnp.int32, (LANES, LANES), 0)
    to_lane = lax.broadcasted_iota(jnp.int32, (LANES, LANES), 1)
    box_c = (from_lane == to_lane) | (from_lane == lane_of(to_lane - 1))
    box_c = box_c | (from_lane == lane_of(to_lane + 1))
    box_c = jnp.where(box_c & (to_lane < cells_c), 1.0, 0.0).astype(jnp.bfloat16)
    group = jnp.where(from_lane // PATCH == to_lane // PATCH, 1.0, 0.0).astype(jnp.bfloat16)

    def look_sums(c, h):
        at, across = band(c), pl.ds(h * PIECE, PIECE)

        def date_image(i):
            source = (img_ref, near, far)[i // 2]
            return source[i % 2, 0, at, across], source[i % 2, 1, at, across]

        images = [date_image(i) for i in range(6)]
        parts = []
        for k in range(2):
            a_r, a_i = images[k]
            for l in range(3):
                low, high = images[k + l + 1], images[k + l + 2]
                b_r = jnp.where(first[k][l], low[0], high[0])
                b_i = jnp.where(first[k][l], low[1], high[1])
                parts += [a_r * b_r + a_i * b_i, a_i * b_r - a_r * b_i]
        parts += [r * r + i * i for r, i in images]
        return dot_exact(jnp.concatenate(parts, axis=0), looks[h * PIECE : (h + 1) * PIECE])

    def keep(c, summed):
        at = band(c)
        lanes = lax.broadcasted_iota(jnp.int32, (BAND, LANES), 1)
        pack_l = jnp.zeros((BAND, LANES), jnp.float32)
        pack_r = jnp.zeros((BAND, LANES), jnp.float32)
        for p in range(planes.shape[0]):
            own = summed[p * BAND : (p + 1) * BAND]
            planes[p, pl.ds(halo + c * BAND, BAND)] = own
            mine = (lanes >= p * MARGIN) & (lanes < (p + 1) * MARGIN)
            pack_l = jnp.where(mine, pltpu.roll(own, (p * MARGIN) % LANES, 1), pack_l)
            shift = (p * MARGIN - (cells_c - MARGIN)) % LANES
            pack_r = jnp.where(mine, pltpu.roll(own, shift, 1), pack_r)
        edge_l[at] = pack_l
        edge_r[at] = pack_r

    messages = []
    for step in steps:
        if step[0] == 0:
            messages += [(step, c * BAND, BAND, c) for c in range(chunks)]
        else:
            c = 0 if step[0] < 0 else chunks - 1
            messages.append((step, c * BAND, BAND, c))

    def halo_copy(n):
        (r, c), start, size, _ = messages[n]
        source_at = pl.ds(start, size)
        target_at = pl.ds(halo + start - r * rows, size)
        if c == 0:
            source, target = planes.at[:, pl.ds(halo + start, size)], planes.at[:, target_at]
        elif c < 0:
            source, target = edge_l.at[source_at], side_r.at[target_at]
        else:
            source, target = edge_r.at[source_at], side_l.at[target_at]
        return pltpu.make_async_remote_copy(
            src_ref=source,
            dst_ref=target,
            send_sem=halo_send.at[n],
            recv_sem=halo_recv.at[n],
            device_id=(date, row + r, col + c),
            device_id_type=MESH,
        )

    load_img.wait()
    for c in order:
        summed = None
        for h in range(pieces):
            far_copy(c, h).wait_recv()

            @pl.when(jnp.logical_not(odd))
            def _():
                near_copy(c, h, far).start()

            near_copy(c, h, img_hbm).wait_recv()
            part = look_sums(c, h)
            summed = part if summed is None else summed + part
        keep(c, summed)
        for step in steps:

            @pl.when(there(step))
            def _():
                for n, message in enumerate(messages):
                    if message[0] == step and message[3] == c:
                        halo_copy(n).start()

    load_table.wait()

    def part_of(i, j, lanes=LANES):
        rows_at = slice(starts[i], starts[j])
        return table[0, rows_at, :lanes], table[1, rows_at, :lanes]

    row_fwd = part_of(0, 1)
    box_r = table[0, starts[0] + 2 * PATCH : starts[0] + 2 * PATCH + cells_r, : rows + 2 * halo]
    col_fwd = [
        jnp.concatenate(
            [
                jnp.concatenate([cosine, -sine], axis=1),
                jnp.concatenate([sine, cosine], axis=1),
            ],
            axis=0,
        )
        for cosine, sine in zip(part_of(1, 2), part_of(2, 3))
    ]
    col_inv = [
        jnp.concatenate(
            [
                jnp.concatenate([cosine, sine], axis=1),
                jnp.concatenate([-sine, cosine], axis=1),
            ],
            axis=0,
        )
        for cosine, sine in zip(part_of(3, 4), part_of(4, 5))
    ]
    row_inv = part_of(5, 6, 2 * PATCH)

    for step in steps:

        @pl.when(there((-step[0], -step[1])))
        def _():
            for n, message in enumerate(messages):
                if message[0] == step:
                    halo_copy(n).wait_recv()

    tall = rows + 2 * halo
    wide = lax.broadcasted_iota(jnp.int32, (tall, LANES), 1)
    in_l = (wide >= cells_c) & (wide < cells_c + MARGIN)
    in_r = (wide >= cells_c + MARGIN) & (wide < cells_c + 2 * MARGIN)
    got_l, got_r = side_l[...], side_r[...]

    def whole(p):
        left = pltpu.roll(got_l, (cells_c - p * MARGIN) % LANES, 1)
        right = pltpu.roll(got_r, (cells_c + MARGIN - p * MARGIN) % LANES, 1)
        return jnp.where(in_l, left, jnp.where(in_r, right, planes[p]))

    def lane_tiles(x):
        return [x[:, i : i + LANES] for i in range(0, x.shape[1], LANES)]

    fields = [jnp.concatenate([whole(2 * p), whole(2 * p + 1)], axis=0) for p in range(6)]
    outs = lane_tiles(dot(row_fwd, split(jnp.concatenate(fields, axis=1))))
    spectra = [jnp.concatenate([o[:PATCH], o[PATCH : 2 * PATCH]], axis=1) for o in outs]
    boxes = [o[2 * PATCH :] for o in outs]
    high, low = split(jnp.concatenate([whole(p) for p in range(12, 18)], axis=1))
    boxes += lane_tiles(mul(box_r, high) + mul(box_r, low))
    box = dot_exact(jnp.concatenate(boxes, axis=0), box_c) * (1.0 / 9.0)
    base = 12 * cells_r
    power = [box[base + i * cells_r : base + (i + 1) * cells_r] for i in range(6)]
    for k in range(2):
        for l in range(3):
            second = jnp.where(first[k][l], power[k + l + 1], power[k + l + 2])
            factor = lax.rsqrt(power[k] * second + 1e-06)
            for part in range(2):
                at = ((k * 3 + l) * 2 + part) * cells_r
                coh_ref[k, l, part] = (box[at : at + cells_r] * factor)[:, :cells_c]

    z = dot(split(jnp.concatenate(spectra, axis=0)), col_fwd)
    z_r, z_i = z[:, :LANES], z[:, LANES:]
    energy = z_r * z_r + z_i * z_i
    lane32 = lax.rem(lax.broadcasted_iota(jnp.int32, (6 * PATCH, LANES), 1), PATCH)
    left = jnp.where(lane32 == 0, pltpu.roll(energy, LANES - PATCH + 1, 1), pltpu.roll(energy, 1, 1))
    right = jnp.where(
        lane32 == PATCH - 1, pltpu.roll(energy, PATCH - 1, 1), pltpu.roll(energy, LANES - 1, 1)
    )
    across = energy + left + right

    def per_patch(values):
        sums = [
            jnp.sum(values[p * PATCH : (p + 1) * PATCH], axis=0, keepdims=True) for p in range(6)
        ]
        sums += [jnp.zeros((2, LANES), jnp.float32)]
        return dot_exact(jnp.concatenate(sums, axis=0), group) * (1.0 / (PATCH * PATCH))

    level = per_patch(energy)
    weights = []
    for p in range(6):
        part = across[p * PATCH : (p + 1) * PATCH]
        smooth = (part + pltpu.roll(part, 1, 0) + pltpu.roll(part, PATCH - 1, 0)) * (1.0 / 9.0)
        weights.append(jnp.sqrt(jnp.sqrt(smooth + level[p : p + 1] + 1e-06)))
    scale = 1.0 / per_patch(jnp.concatenate(weights, axis=0))
    filtered = []
    for p in range(6):
        weight = weights[p] * scale[p : p + 1]
        at = slice(p * PATCH, (p + 1) * PATCH)
        filtered.append(jnp.concatenate([z_r[at] * weight, z_i[at] * weight], axis=0))
    outs = lane_tiles(dot(row_inv, split(jnp.concatenate(filtered, axis=1))))
    back = [jnp.concatenate([o[:KEEP], o[KEEP:]], axis=1) for o in outs]
    final = dot(split(jnp.concatenate(back, axis=0)), col_inv)
    for p in range(6):
        at = slice(p * KEEP, (p + 1) * KEEP)
        filt_ref[p // 3, p % 3, 0] = final[at, :cells_c]
        filt_ref[p // 3, p % 3, 1] = final[at, LANES : LANES + cells_c]

    for c in range(chunks):
        for h in range(pieces):
            far_copy(c, h).wait_send()
            near_copy(c, h, img_hbm).wait_send()
    for step in steps:

        @pl.when(there(step))
        def _():
            for n, message in enumerate(messages):
                if message[0] == step:
                    halo_copy(n).wait_send()


def body(images, secondaries):
    per_device, _, rows, cols = images.shape
    links = secondaries.shape[1]
    dates = lax.axis_size("date")
    assert per_device == 2 and links == 3 and rows == 2 * KEEP and dates % 2 == 0 and dates > 4
    cells_r, cells_c = rows // LOOK_R, cols // LOOK_C
    tall = rows + 2 * MARGIN * LOOK_R
    chunks = rows // BAND
    out = jax.ShapeDtypeStruct((per_device, links, 2, cells_r, cells_c), jnp.float32)
    table, starts = tables(rows, cols)
    vmem = pl.BlockSpec(memory_space=pltpu.VMEM)
    hbm = pl.BlockSpec(memory_space=pltpu.HBM)
    sizes = (dates, lax.axis_size("row"), lax.axis_size("col"))
    dma = pltpu.SemaphoreType.DMA
    return pl.pallas_call(
        functools.partial(kernel, sizes, starts),
        out_shape=(out, out),
        in_specs=[hbm, hbm, hbm],
        out_specs=(vmem, vmem),
        scratch_shapes=[
            pltpu.SMEM(secondaries.shape, jnp.int32),
            pltpu.VMEM(images.shape, jnp.float32),
            pltpu.VMEM(table.shape, jnp.bfloat16),
            pltpu.VMEM(images.shape, jnp.float32),
            pltpu.VMEM(images.shape, jnp.float32),
            pltpu.VMEM((18, tall, LANES), jnp.float32),
            pltpu.VMEM((rows, LANES), jnp.float32),
            pltpu.VMEM((rows, LANES), jnp.float32),
            pltpu.VMEM((tall, LANES), jnp.float32),
            pltpu.VMEM((tall, LANES), jnp.float32),
            dma((chunks * (cols // PIECE),)),
            dma((chunks * (cols // PIECE),)),
            dma((chunks * (cols // PIECE),)),
            dma((chunks * (cols // PIECE),)),
            dma((6 + 2 * chunks,)),
            dma((6 + 2 * chunks,)),
            dma((3,)),
        ],
        compiler_params=pltpu.CompilerParams(
            collective_id=0, has_side_effects=True, vmem_limit_bytes=VMEM_BYTES
        ),
        cost_estimate=pl.CostEstimate(flops=10**9, bytes_accessed=10**6, transcendentals=0),
    )(secondaries, images, jnp.asarray(table))


def solution(mesh):
    in_specs = (P("date", None, "row", "col"), P("date", None))
    out_specs = (P("date", None, None, "row", "col"), P("date", None, None, "row", "col"))
    return jax.shard_map(body, mesh=mesh, in_specs=in_specs, out_specs=out_specs, check_vma=False)
```

```python
import functools
import math

import jax
import jax.numpy as jnp
import ml_dtypes
import numpy as np
from jax import lax
from jax.experimental import pallas as pl
from jax.experimental.pallas import tpu as pltpu
from jax.sharding import PartitionSpec as P

LOOK_R = 2
LOOK_C = 8
PATCH = 32
KEEP = 24
MARGIN = 4
LANES = 128
BAND = 8
PIECE = 256
VMEM_BYTES = 64 * 1024 * 1024 - 800 * 1024
MESH = pl.DeviceIdType.MESH


def tables(rows, cols):
    cells_r, cells_c = rows // LOOK_R, cols // LOOK_C
    blocks = cells_c // KEEP
    halo_r = MARGIN * LOOK_R
    tall = rows + 2 * halo_r

    def lane(x):
        if x < 0:
            return cells_c + MARGIN + x
        return x if x < cells_c else x + MARGIN

    ticks = np.arange(PATCH)
    angle = (ticks[:, None] * ticks[None, :] % PATCH) * (2.0 * math.pi / PATCH)
    cosine, sine = np.cos(angle), np.sin(angle)

    pick = np.zeros((PATCH, tall))
    pick[np.arange(tall) // LOOK_R, np.arange(tall)] = 1.0
    row_c, row_s = cosine @ pick, sine @ pick
    box_r = np.zeros((cells_r, PATCH))
    for y in range(cells_r):
        box_r[y, MARGIN + y - 1 : MARGIN + y + 2] = 1.0
    box_r = box_r @ pick
    none = np.zeros_like(box_r)
    row_fwd = np.block([[row_c, row_s], [-row_s, row_c], [box_r, none], [none, box_r]])

    col_c, col_s = np.zeros((LANES, LANES)), np.zeros((LANES, LANES))
    for b in range(blocks):
        for x in range(PATCH):
            at = lane(b * KEEP - MARGIN + x)
            col_c[at, b * PATCH : (b + 1) * PATCH] = cosine[x]
            col_s[at, b * PATCH : (b + 1) * PATCH] = sine[x]
    centre = slice(MARGIN, MARGIN + KEEP)
    row_inv = np.block([[cosine[centre], -sine[centre]], [sine[centre], cosine[centre]]])
    inv_c, inv_s = np.zeros((LANES, LANES)), np.zeros((LANES, LANES))
    for b in range(blocks):
        inv_c[b * PATCH : (b + 1) * PATCH, b * KEEP : (b + 1) * KEEP] = cosine[:, centre]
        inv_s[b * PATCH : (b + 1) * PATCH, b * KEEP : (b + 1) * KEEP] = sine[:, centre]
    scale = 1.0 / (PATCH * PATCH)
    row_inv = np.pad(row_inv, ((0, 0), (0, LANES - 2 * PATCH)))
    stacked = [row_fwd, col_c, col_s, inv_c * scale, inv_s * scale, row_inv]
    whole = np.concatenate(stacked, axis=0).astype(np.float32)
    high = whole.astype(ml_dtypes.bfloat16)
    low = (whole - high.astype(np.float32)).astype(ml_dtypes.bfloat16)
    starts = np.cumsum([0] + [t.shape[0] for t in stacked])
    return np.stack([high, low]), [int(n) for n in starts]


def split(x):
    high = x.astype(jnp.bfloat16)
    return high, (x - high.astype(jnp.float32)).astype(jnp.bfloat16)


def mul(a, b):
    return lax.dot_general(a, b, (((1,), (0,)), ((), ())), preferred_element_type=jnp.float32)


def dot(a, b):
    return mul(a[0], b[0]) + (mul(a[1], b[0]) + mul(a[0], b[1]))


def dot_exact(x, b):
    high, low = split(x)
    return mul(high, b) + mul(low, b)


def kernel(
    sizes,
    starts,
    sec_hbm,
    img_hbm,
    table_hbm,
    filt_ref,
    coh_ref,
    sec_ref,
    img_ref,
    table,
    near,
    far,
    planes,
    edge_l,
    edge_r,
    side_l,
    side_r,
    near_send,
    near_recv,
    far_send,
    far_recv,
    halo_send,
    halo_recv,
    local_sem,
):
    dates, n_rows, n_cols = sizes
    rows, cols = img_ref.shape[2], img_ref.shape[3]
    cells_c = cols // LOOK_C
    cells_r = rows // LOOK_R
    halo = MARGIN * LOOK_R
    chunks = rows // BAND
    date, row, col = lax.axis_index("date"), lax.axis_index("row"), lax.axis_index("col")
    odd = lax.rem(date, 2) == 1
    mate = date + 1 - 2 * lax.rem(date, 2)
    before = lax.rem(date + dates - 2, dates)
    after = lax.rem(date + 2, dates)
    steps = [(r, c) for r in (-1, 0, 1) for c in (-1, 0, 1) if (r, c) != (0, 0)]

    def there(step):
        test_r = [None, row < n_rows - 1, row > 0][step[0]]
        test_c = [None, col < n_cols - 1, col > 0][step[1]]
        tests = [t for t in (test_r, test_c) if t is not None]
        return functools.reduce(jnp.logical_and, tests)

    order = [0, chunks - 1] + list(range(1, chunks - 1))
    load_img = pltpu.make_async_copy(img_hbm, img_ref, local_sem.at[0])
    load_table = pltpu.make_async_copy(table_hbm, table, local_sem.at[1])
    load_sec = pltpu.make_async_copy(sec_hbm, sec_ref, local_sem.at[2])
    load_sec.start()
    load_img.start()
    load_table.start()
    barrier = pltpu.get_barrier_semaphore()
    for other in (before, after, mate):
        pl.semaphore_signal(barrier, inc=1, device_id=(other, row, col), device_id_type=MESH)
    count = jnp.int32(3)
    for step in steps:
        here = there(step)

        @pl.when(here)
        def _():
            pl.semaphore_signal(
                barrier,
                inc=1,
                device_id=(date, row + step[0], col + step[1]),
                device_id_type=MESH,
            )

        count = count + here.astype(jnp.int32)
    pl.semaphore_wait(barrier, count)

    def band(c):
        return pl.ds(c * BAND, BAND)

    pieces = cols // PIECE

    def far_copy(c, h):
        part = (slice(None), slice(None), band(c), pl.ds(h * PIECE, PIECE))
        return pltpu.make_async_remote_copy(
            src_ref=img_hbm.at[part],
            dst_ref=far.at[part],
            send_sem=far_send.at[c * pieces + h],
            recv_sem=far_recv.at[c * pieces + h],
            device_id=(before, row, col),
            device_id_type=MESH,
        )

    def near_copy(c, h, source):
        part = (slice(None), slice(None), band(c), pl.ds(h * PIECE, PIECE))
        return pltpu.make_async_remote_copy(
            src_ref=source.at[part],
            dst_ref=near.at[part],
            send_sem=near_send.at[c * pieces + h],
            recv_sem=near_recv.at[c * pieces + h],
            device_id=(mate, row, col),
            device_id_type=MESH,
        )

    for c in order:
        for h in range(pieces):
            far_copy(c, h).start()

            @pl.when(odd)
            def _():
                near_copy(c, h, img_hbm).start()

    for step in steps:

        @pl.when(jnp.logical_not(there(step)))
        def _():
            r, c = step
            at = {-1: slice(0, halo), 0: slice(halo, halo + rows), 1: slice(halo + rows, None)}[r]
            if c == 0:
                planes[:, at] = jnp.zeros_like(planes[:, at])
            else:
                side = side_l if c < 0 else side_r
                side[at] = jnp.zeros_like(side[at])

    total = 2 * dates
    load_sec.wait()

    def is_first(k, l):
        return lax.rem(sec_ref[k, l] - (2 * date + k) + total, total) == l + 1

    first = [[is_first(k, l) for l in range(3)] for k in range(2)]

    def lane_of(x):
        return jnp.where(x < 0, cells_c + MARGIN + x, jnp.where(x < cells_c, x, x + MARGIN))

    cell = lax.broadcasted_iota(jnp.int32, (cols, LANES), 0) // LOOK_C
    looks = jnp.where(
        cell == lax.broadcasted_iota(jnp.int32, (cols, LANES), 1), 1.0 / (LOOK_R * LOOK_C), 0.0
    ).astype(jnp.bfloat16)
    from_lane = lax.broadcasted_iota(jnp.int32, (LANES, LANES), 0)
    to_lane = lax.broadcasted_iota(jnp.int32, (LANES, LANES), 1)
    box_c = (from_lane == to_lane) | (from_lane == lane_of(to_lane - 1))
    box_c = box_c | (from_lane == lane_of(to_lane + 1))
    box_c = jnp.where(box_c & (to_lane < cells_c), 1.0, 0.0).astype(jnp.bfloat16)
    group = jnp.where(from_lane // PATCH == to_lane // PATCH, 1.0, 0.0).astype(jnp.bfloat16)

    def look_sums(c, h):
        at, across = band(c), pl.ds(h * PIECE, PIECE)

        def date_image(i):
            source = (img_ref, near, far)[i // 2]
            return source[i % 2, 0, at, across], source[i % 2, 1, at, across]

        images = [date_image(i) for i in range(6)]
        parts = []
        for k in range(2):
            a_r, a_i = images[k]
            for l in range(3):
                low, high = images[k + l + 1], images[k + l + 2]
                b_r = jnp.where(first[k][l], low[0], high[0])
                b_i = jnp.where(first[k][l], low[1], high[1])
                parts += [a_r * b_r + a_i * b_i, a_i * b_r - a_r * b_i]
        parts += [r * r + i * i for r, i in images]
        return dot_exact(jnp.concatenate(parts, axis=0), looks[h * PIECE : (h + 1) * PIECE])

    def keep(c, summed):
        at = band(c)
        lanes = lax.broadcasted_iota(jnp.int32, (BAND, LANES), 1)
        pack_l = jnp.zeros((BAND, LANES), jnp.float32)
        pack_r = jnp.zeros((BAND, LANES), jnp.float32)
        for p in range(planes.shape[0]):
            own = summed[p * BAND : (p + 1) * BAND]
            planes[p, pl.ds(halo + c * BAND, BAND)] = own
            mine = (lanes >= p * MARGIN) & (lanes < (p + 1) * MARGIN)
            pack_l = jnp.where(mine, pltpu.roll(own, (p * MARGIN) % LANES, 1), pack_l)
            shift = (p * MARGIN - (cells_c - MARGIN)) % LANES
            pack_r = jnp.where(mine, pltpu.roll(own, shift, 1), pack_r)
        edge_l[at] = pack_l
        edge_r[at] = pack_r

    messages = []
    for step in steps:
        if step[0] == 0:
            messages += [(step, c * BAND, BAND, c) for c in range(chunks)]
        else:
            c = 0 if step[0] < 0 else chunks - 1
            messages.append((step, c * BAND, BAND, c))

    def halo_copy(n):
        (r, c), start, size, _ = messages[n]
        source_at = pl.ds(start, size)
        target_at = pl.ds(halo + start - r * rows, size)
        if c == 0:
            source, target = planes.at[:, pl.ds(halo + start, size)], planes.at[:, target_at]
        elif c < 0:
            source, target = edge_l.at[source_at], side_r.at[target_at]
        else:
            source, target = edge_r.at[source_at], side_l.at[target_at]
        return pltpu.make_async_remote_copy(
            src_ref=source,
            dst_ref=target,
            send_sem=halo_send.at[n],
            recv_sem=halo_recv.at[n],
            device_id=(date, row + r, col + c),
            device_id_type=MESH,
        )

    load_img.wait()
    for c in order:
        summed = None
        for h in range(pieces):
            far_copy(c, h).wait_recv()

            @pl.when(jnp.logical_not(odd))
            def _():
                near_copy(c, h, far).start()

            near_copy(c, h, img_hbm).wait_recv()
            part = look_sums(c, h)
            summed = part if summed is None else summed + part
        keep(c, summed)
        for step in steps:

            @pl.when(there(step))
            def _():
                for n, message in enumerate(messages):
                    if message[0] == step and message[3] == c:
                        halo_copy(n).start()

    load_table.wait()

    def part_of(i, j, lanes=LANES):
        rows_at = slice(starts[i], starts[j])
        return table[0, rows_at, :lanes], table[1, rows_at, :lanes]

    row_fwd = part_of(0, 1)
    box_r = table[0, starts[0] + 2 * PATCH : starts[0] + 2 * PATCH + cells_r, : rows + 2 * halo]
    col_fwd = [
        jnp.concatenate(
            [
                jnp.concatenate([cosine, -sine], axis=1),
                jnp.concatenate([sine, cosine], axis=1),
            ],
            axis=0,
        )
        for cosine, sine in zip(part_of(1, 2), part_of(2, 3))
    ]
    col_inv = [
        jnp.concatenate(
            [
                jnp.concatenate([cosine, sine], axis=1),
                jnp.concatenate([-sine, cosine], axis=1),
            ],
            axis=0,
        )
        for cosine, sine in zip(part_of(3, 4), part_of(4, 5))
    ]
    row_inv = part_of(5, 6, 2 * PATCH)

    def wait_halo(sides):
        for step in steps:
            if (step[1] != 0) != sides:
                continue

            @pl.when(there((-step[0], -step[1])))
            def _():
                for n, message in enumerate(messages):
                    if message[0] == step:
                        halo_copy(n).wait_recv()

    def lane_tiles(x):
        return [x[:, i : i + LANES] for i in range(0, x.shape[1], LANES)]

    wait_halo(False)
    fields = [jnp.concatenate([planes[2 * p], planes[2 * p + 1]], axis=0) for p in range(6)]
    outs = lane_tiles(dot(row_fwd, split(jnp.concatenate(fields, axis=1))))
    high, low = split(jnp.concatenate([planes[p] for p in range(12, 18)], axis=1))
    outs += lane_tiles(mul(box_r, high) + mul(box_r, low))
    wait_halo(True)

    tall = rows + 2 * halo
    wide = lax.broadcasted_iota(jnp.int32, (tall, LANES), 1)
    in_left = lax.rem(wide, 2 * MARGIN) < MARGIN
    got_l, got_r = side_l[...], side_r[...]
    even = jnp.where(in_left, got_l, pltpu.roll(got_r, MARGIN, 1))
    later = jnp.where(in_left, pltpu.roll(got_l, LANES - MARGIN, 1), got_r)
    margins = dot(row_fwd, split(jnp.concatenate([even, later], axis=0)))

    def with_margins(out, q, at):
        moved = pltpu.roll(margins[at], (cells_c - 2 * MARGIN * q) % LANES, 1)
        lanes = lax.broadcasted_iota(jnp.int32, out.shape, 1)
        return jnp.where((lanes >= cells_c) & (lanes < cells_c + 2 * MARGIN), moved, out)

    middle = 2 * PATCH
    spectra, boxes = [], []
    for p in range(6):
        out = with_margins(outs[p], p, slice(None))
        spectra.append(jnp.concatenate([out[:PATCH], out[PATCH:middle]], axis=1))
        boxes.append(out[middle:])
    for i in range(6):
        start = middle + (i % 2) * cells_r
        boxes.append(with_margins(outs[6 + i], 6 + i // 2, slice(start, start + cells_r)))
    box = dot_exact(jnp.concatenate(boxes, axis=0), box_c) * (1.0 / 9.0)
    base = 12 * cells_r
    power = [box[base + i * cells_r : base + (i + 1) * cells_r] for i in range(6)]
    for k in range(2):
        for l in range(3):
            second = jnp.where(first[k][l], power[k + l + 1], power[k + l + 2])
            factor = lax.rsqrt(power[k] * second + 1e-06)
            for part in range(2):
                at = ((k * 3 + l) * 2 + part) * cells_r
                coh_ref[k, l, part] = (box[at : at + cells_r] * factor)[:, :cells_c]

    z = dot(split(jnp.concatenate(spectra, axis=0)), col_fwd)
    z_r, z_i = z[:, :LANES], z[:, LANES:]
    energy = z_r * z_r + z_i * z_i
    lane32 = lax.rem(lax.broadcasted_iota(jnp.int32, (6 * PATCH, LANES), 1), PATCH)
    left = jnp.where(lane32 == 0, pltpu.roll(energy, LANES - PATCH + 1, 1), pltpu.roll(energy, 1, 1))
    right = jnp.where(
        lane32 == PATCH - 1, pltpu.roll(energy, PATCH - 1, 1), pltpu.roll(energy, LANES - 1, 1)
    )
    across = energy + left + right

    def per_patch(values):
        sums = [
            jnp.sum(values[p * PATCH : (p + 1) * PATCH], axis=0, keepdims=True) for p in range(6)
        ]
        sums += [jnp.zeros((2, LANES), jnp.float32)]
        return dot_exact(jnp.concatenate(sums, axis=0), group) * (1.0 / (PATCH * PATCH))

    level = per_patch(energy)
    weights = []
    for p in range(6):
        part = across[p * PATCH : (p + 1) * PATCH]
        smooth = (part + pltpu.roll(part, 1, 0) + pltpu.roll(part, PATCH - 1, 0)) * (1.0 / 9.0)
        weights.append(jnp.sqrt(jnp.sqrt(smooth + level[p : p + 1] + 1e-06)))
    scale = 1.0 / per_patch(jnp.concatenate(weights, axis=0))
    filtered = []
    for p in range(6):
        weight = weights[p] * scale[p : p + 1]
        at = slice(p * PATCH, (p + 1) * PATCH)
        filtered.append(jnp.concatenate([z_r[at] * weight, z_i[at] * weight], axis=0))
    outs = lane_tiles(dot(row_inv, split(jnp.concatenate(filtered, axis=1))))
    back = [jnp.concatenate([o[:KEEP], o[KEEP:]], axis=1) for o in outs]
    final = dot(split(jnp.concatenate(back, axis=0)), col_inv)
    for p in range(6):
        at = slice(p * KEEP, (p + 1) * KEEP)
        filt_ref[p // 3, p % 3, 0] = final[at, :cells_c]
        filt_ref[p // 3, p % 3, 1] = final[at, LANES : LANES + cells_c]

    for c in range(chunks):
        for h in range(pieces):
            far_copy(c, h).wait_send()
            near_copy(c, h, img_hbm).wait_send()
    for step in steps:

        @pl.when(there(step))
        def _():
            for n, message in enumerate(messages):
                if message[0] == step:
                    halo_copy(n).wait_send()


def write(filt_in, coh_in, filt_out, coh_out, sems):
    copies = [
        pltpu.make_async_copy(filt_in, filt_out, sems.at[0]),
        pltpu.make_async_copy(coh_in, coh_out, sems.at[1]),
    ]
    for copy in copies:
        copy.start()
    for copy in copies:
        copy.wait()


def body(images, secondaries):
    per_device, _, rows, cols = images.shape
    links = secondaries.shape[1]
    dates = lax.axis_size("date")
    assert per_device == 2 and links == 3 and rows == 2 * KEEP and dates % 2 == 0 and dates > 4
    cells_r, cells_c = rows // LOOK_R, cols // LOOK_C
    tall = rows + 2 * MARGIN * LOOK_R
    chunks = rows // BAND
    out = jax.ShapeDtypeStruct((per_device, links, 2, cells_r, cells_c), jnp.float32)
    table, starts = tables(rows, cols)
    vmem = pl.BlockSpec(memory_space=pltpu.VMEM)
    hbm = pl.BlockSpec(memory_space=pltpu.HBM)
    sizes = (dates, lax.axis_size("row"), lax.axis_size("col"))
    dma = pltpu.SemaphoreType.DMA
    results = pl.pallas_call(
        functools.partial(kernel, sizes, starts),
        out_shape=(pltpu.VMEM(out.shape, out.dtype),) * 2,
        in_specs=[hbm, hbm, hbm],
        out_specs=(vmem, vmem),
        scratch_shapes=[
            pltpu.SMEM(secondaries.shape, jnp.int32),
            pltpu.VMEM(images.shape, jnp.float32),
            pltpu.VMEM(table.shape, jnp.bfloat16),
            pltpu.VMEM(images.shape, jnp.float32),
            pltpu.VMEM(images.shape, jnp.float32),
            pltpu.VMEM((18, tall, LANES), jnp.float32),
            pltpu.VMEM((rows, LANES), jnp.float32),
            pltpu.VMEM((rows, LANES), jnp.float32),
            pltpu.VMEM((tall, LANES), jnp.float32),
            pltpu.VMEM((tall, LANES), jnp.float32),
            dma((chunks * (cols // PIECE),)),
            dma((chunks * (cols // PIECE),)),
            dma((chunks * (cols // PIECE),)),
            dma((chunks * (cols // PIECE),)),
            dma((6 + 2 * chunks,)),
            dma((6 + 2 * chunks,)),
            dma((3,)),
        ],
        compiler_params=pltpu.CompilerParams(
            collective_id=0, has_side_effects=True, vmem_limit_bytes=VMEM_BYTES
        ),
        cost_estimate=pl.CostEstimate(flops=10**9, bytes_accessed=10**6, transcendentals=0),
    )(secondaries, images, jnp.asarray(table))
    return pl.pallas_call(
        write,
        out_shape=(out, out),
        in_specs=[vmem, vmem],
        out_specs=(hbm, hbm),
        scratch_shapes=[dma((2,))],
        compiler_params=pltpu.CompilerParams(vmem_limit_bytes=1024 * 1024),
    )(*results)


def solution(mesh):
    in_specs = (P("date", None, "row", "col"), P("date", None))
    out_specs = (P("date", None, None, "row", "col"), P("date", None, None, "row", "col"))
    return jax.shard_map(body, mesh=mesh, in_specs=in_specs, out_specs=out_specs, check_vma=False)
```

```python
import functools
import math

import jax
import jax.numpy as jnp
import ml_dtypes
import numpy as np
from jax import lax
from jax.experimental import pallas as pl
from jax.experimental.pallas import tpu as pltpu
from jax.sharding import PartitionSpec as P

LOOK_R = 2
LOOK_C = 8
PATCH = 32
KEEP = 24
MARGIN = 4
LANES = 128
BAND = 8
PIECE = 256
DIRECT = 2
VMEM_BYTES = 64 * 1024 * 1024 - 800 * 1024
MESH = pl.DeviceIdType.MESH


def tables(rows, cols):
    cells_r, cells_c = rows // LOOK_R, cols // LOOK_C
    blocks = cells_c // KEEP
    halo_r = MARGIN * LOOK_R
    tall = rows + 2 * halo_r

    def lane(x):
        if x < 0:
            return cells_c + MARGIN + x
        return x if x < cells_c else x + MARGIN

    ticks = np.arange(PATCH)
    angle = (ticks[:, None] * ticks[None, :] % PATCH) * (2.0 * math.pi / PATCH)
    cosine, sine = np.cos(angle), np.sin(angle)

    pick = np.zeros((PATCH, tall))
    pick[np.arange(tall) // LOOK_R, np.arange(tall)] = 1.0
    row_c, row_s = cosine @ pick, sine @ pick
    box_r = np.zeros((cells_r, PATCH))
    for y in range(cells_r):
        box_r[y, MARGIN + y - 1 : MARGIN + y + 2] = 1.0
    box_r = box_r @ pick
    none = np.zeros_like(box_r)
    row_fwd = np.block([[row_c, row_s], [-row_s, row_c], [box_r, none], [none, box_r]])

    col_c, col_s = np.zeros((LANES, LANES)), np.zeros((LANES, LANES))
    for b in range(blocks):
        for x in range(PATCH):
            at = lane(b * KEEP - MARGIN + x)
            col_c[at, b * PATCH : (b + 1) * PATCH] = cosine[x]
            col_s[at, b * PATCH : (b + 1) * PATCH] = sine[x]
    centre = slice(MARGIN, MARGIN + KEEP)
    row_inv = np.block([[cosine[centre], -sine[centre]], [sine[centre], cosine[centre]]])
    inv_c, inv_s = np.zeros((LANES, LANES)), np.zeros((LANES, LANES))
    for b in range(blocks):
        inv_c[b * PATCH : (b + 1) * PATCH, b * KEEP : (b + 1) * KEEP] = cosine[:, centre]
        inv_s[b * PATCH : (b + 1) * PATCH, b * KEEP : (b + 1) * KEEP] = sine[:, centre]
    scale = 1.0 / (PATCH * PATCH)
    row_inv = np.pad(row_inv, ((0, 0), (0, LANES - 2 * PATCH)))
    stacked = [row_fwd, col_c, col_s, inv_c * scale, inv_s * scale, row_inv]
    whole = np.concatenate(stacked, axis=0).astype(np.float32)
    high = whole.astype(ml_dtypes.bfloat16)
    low = (whole - high.astype(np.float32)).astype(ml_dtypes.bfloat16)
    starts = np.cumsum([0] + [t.shape[0] for t in stacked])
    return np.stack([high, low]), [int(n) for n in starts]


def split(x):
    high = x.astype(jnp.bfloat16)
    return high, (x - high.astype(jnp.float32)).astype(jnp.bfloat16)


def mul(a, b):
    return lax.dot_general(a, b, (((1,), (0,)), ((), ())), preferred_element_type=jnp.float32)


def dot(a, b):
    return mul(a[0], b[0]) + (mul(a[1], b[0]) + mul(a[0], b[1]))


def dot_exact(x, b):
    high, low = split(x)
    return mul(high, b) + mul(low, b)


def kernel(
    sizes,
    starts,
    sec_hbm,
    img_hbm,
    table_hbm,
    filt_ref,
    coh_ref,
    sec_ref,
    img_ref,
    table,
    near,
    far,
    planes,
    edge_l,
    edge_r,
    side_l,
    side_r,
    near_send,
    near_recv,
    far_send,
    far_recv,
    halo_send,
    halo_recv,
    local_sem,
):
    dates, n_rows, n_cols = sizes
    rows, cols = img_ref.shape[2], img_ref.shape[3]
    cells_c = cols // LOOK_C
    cells_r = rows // LOOK_R
    halo = MARGIN * LOOK_R
    chunks = rows // BAND
    date, row, col = lax.axis_index("date"), lax.axis_index("row"), lax.axis_index("col")
    odd = lax.rem(date, 2) == 1
    mate = date + 1 - 2 * lax.rem(date, 2)
    cross = lax.rem(date + dates - 1 + 2 * lax.rem(date, 2), dates)
    before = lax.rem(date + dates - 2, dates)
    after = lax.rem(date + 2, dates)
    steps = [(r, c) for r in (-1, 0, 1) for c in (-1, 0, 1) if (r, c) != (0, 0)]

    def there(step):
        test_r = [None, row < n_rows - 1, row > 0][step[0]]
        test_c = [None, col < n_cols - 1, col > 0][step[1]]
        tests = [t for t in (test_r, test_c) if t is not None]
        return functools.reduce(jnp.logical_and, tests)

    order = [0, chunks - 1] + list(range(1, chunks - 1))
    load_img = pltpu.make_async_copy(img_hbm, img_ref, local_sem.at[0])
    load_table = pltpu.make_async_copy(table_hbm, table, local_sem.at[1])
    load_sec = pltpu.make_async_copy(sec_hbm, sec_ref, local_sem.at[2])
    load_sec.start()
    load_img.start()
    load_table.start()
    barrier = pltpu.get_barrier_semaphore()
    for other in (before, after, mate, cross):
        pl.semaphore_signal(barrier, inc=1, device_id=(other, row, col), device_id_type=MESH)
    count = jnp.int32(4)
    for step in steps:
        here = there(step)

        @pl.when(here)
        def _():
            pl.semaphore_signal(
                barrier,
                inc=1,
                device_id=(date, row + step[0], col + step[1]),
                device_id_type=MESH,
            )

        count = count + here.astype(jnp.int32)
    pl.semaphore_wait(barrier, count)

    def band(c):
        return pl.ds(c * BAND, BAND)

    pieces = cols // PIECE

    def far_copy(c, h):
        part = (slice(None), slice(None), band(c), pl.ds(h * PIECE, PIECE))
        return pltpu.make_async_remote_copy(
            src_ref=img_hbm.at[part],
            dst_ref=far.at[part],
            send_sem=far_send.at[c * pieces + h],
            recv_sem=far_recv.at[c * pieces + h],
            device_id=(before, row, col),
            device_id_type=MESH,
        )

    def near_copy(c, h, source, target=mate):
        part = (slice(None), slice(None), band(c), pl.ds(h * PIECE, PIECE))
        return pltpu.make_async_remote_copy(
            src_ref=source.at[part],
            dst_ref=near.at[part],
            send_sem=near_send.at[c * pieces + h],
            recv_sem=near_recv.at[c * pieces + h],
            device_id=(target, row, col),
            device_id_type=MESH,
        )

    every = [(c, h) for c in order for h in range(pieces)]
    direct = every[len(every) - DIRECT :]
    for c, h in direct:

        @pl.when(jnp.logical_not(odd))
        def _():
            near_copy(c, h, img_hbm, cross).start()

    for c in order:
        for h in range(pieces):
            far_copy(c, h).start()

            @pl.when(odd)
            def _():
                near_copy(c, h, img_hbm).start()

    for step in steps:

        @pl.when(jnp.logical_not(there(step)))
        def _():
            r, c = step
            at = {-1: slice(0, halo), 0: slice(halo, halo + rows), 1: slice(halo + rows, None)}[r]
            if c == 0:
                planes[:, at] = jnp.zeros_like(planes[:, at])
            else:
                side = side_l if c < 0 else side_r
                side[at] = jnp.zeros_like(side[at])

    total = 2 * dates
    load_sec.wait()

    def is_first(k, l):
        return lax.rem(sec_ref[k, l] - (2 * date + k) + total, total) == l + 1

    first = [[is_first(k, l) for l in range(3)] for k in range(2)]

    def lane_of(x):
        return jnp.where(x < 0, cells_c + MARGIN + x, jnp.where(x < cells_c, x, x + MARGIN))

    cell = lax.broadcasted_iota(jnp.int32, (cols, LANES), 0) // LOOK_C
    looks = jnp.where(
        cell == lax.broadcasted_iota(jnp.int32, (cols, LANES), 1), 1.0 / (LOOK_R * LOOK_C), 0.0
    ).astype(jnp.bfloat16)
    from_lane = lax.broadcasted_iota(jnp.int32, (LANES, LANES), 0)
    to_lane = lax.broadcasted_iota(jnp.int32, (LANES, LANES), 1)
    box_c = (from_lane == to_lane) | (from_lane == lane_of(to_lane - 1))
    box_c = box_c | (from_lane == lane_of(to_lane + 1))
    box_c = jnp.where(box_c & (to_lane < cells_c), 1.0, 0.0).astype(jnp.bfloat16)
    group = jnp.where(from_lane // PATCH == to_lane // PATCH, 1.0, 0.0).astype(jnp.bfloat16)

    def look_sums(c, h):
        at, across = band(c), pl.ds(h * PIECE, PIECE)

        def date_image(i):
            source = (img_ref, near, far)[i // 2]
            return source[i % 2, 0, at, across], source[i % 2, 1, at, across]

        images = [date_image(i) for i in range(6)]
        parts = []
        for k in range(2):
            a_r, a_i = images[k]
            for l in range(3):
                low, high = images[k + l + 1], images[k + l + 2]
                b_r = jnp.where(first[k][l], low[0], high[0])
                b_i = jnp.where(first[k][l], low[1], high[1])
                parts += [a_r * b_r + a_i * b_i, a_i * b_r - a_r * b_i]
        parts += [r * r + i * i for r, i in images]
        return dot_exact(jnp.concatenate(parts, axis=0), looks[h * PIECE : (h + 1) * PIECE])

    def keep(c, summed):
        at = band(c)
        lanes = lax.broadcasted_iota(jnp.int32, (BAND, LANES), 1)
        pack_l = jnp.zeros((BAND, LANES), jnp.float32)
        pack_r = jnp.zeros((BAND, LANES), jnp.float32)
        for p in range(planes.shape[0]):
            own = summed[p * BAND : (p + 1) * BAND]
            planes[p, pl.ds(halo + c * BAND, BAND)] = own
            mine = (lanes >= p * MARGIN) & (lanes < (p + 1) * MARGIN)
            pack_l = jnp.where(mine, pltpu.roll(own, (p * MARGIN) % LANES, 1), pack_l)
            shift = (p * MARGIN - (cells_c - MARGIN)) % LANES
            pack_r = jnp.where(mine, pltpu.roll(own, shift, 1), pack_r)
        edge_l[at] = pack_l
        edge_r[at] = pack_r

    messages = []
    for step in steps:
        if step[0] == 0:
            messages += [(step, c * BAND, BAND, c) for c in range(chunks)]
        else:
            c = 0 if step[0] < 0 else chunks - 1
            messages.append((step, c * BAND, BAND, c))

    def halo_copy(n):
        (r, c), start, size, _ = messages[n]
        source_at = pl.ds(start, size)
        target_at = pl.ds(halo + start - r * rows, size)
        if c == 0:
            source, target = planes.at[:, pl.ds(halo + start, size)], planes.at[:, target_at]
        elif c < 0:
            source, target = edge_l.at[source_at], side_r.at[target_at]
        else:
            source, target = edge_r.at[source_at], side_l.at[target_at]
        return pltpu.make_async_remote_copy(
            src_ref=source,
            dst_ref=target,
            send_sem=halo_send.at[n],
            recv_sem=halo_recv.at[n],
            device_id=(date, row + r, col + c),
            device_id_type=MESH,
        )

    load_img.wait()
    for c in order:
        summed = None
        for h in range(pieces):
            far_copy(c, h).wait_recv()

            if (c, h) not in direct:

                @pl.when(jnp.logical_not(odd))
                def _():
                    near_copy(c, h, far).start()

            near_copy(c, h, img_hbm).wait_recv()
            part = look_sums(c, h)
            summed = part if summed is None else summed + part
        keep(c, summed)
        for step in steps:

            @pl.when(there(step))
            def _():
                for n, message in enumerate(messages):
                    if message[0] == step and message[3] == c:
                        halo_copy(n).start()

    load_table.wait()

    def part_of(i, j, lanes=LANES):
        rows_at = slice(starts[i], starts[j])
        return table[0, rows_at, :lanes], table[1, rows_at, :lanes]

    row_fwd = part_of(0, 1)
    box_r = table[0, starts[0] + 2 * PATCH : starts[0] + 2 * PATCH + cells_r, : rows + 2 * halo]
    col_fwd = [
        jnp.concatenate(
            [
                jnp.concatenate([cosine, -sine], axis=1),
                jnp.concatenate([sine, cosine], axis=1),
            ],
            axis=0,
        )
        for cosine, sine in zip(part_of(1, 2), part_of(2, 3))
    ]
    col_inv = [
        jnp.concatenate(
            [
                jnp.concatenate([cosine, sine], axis=1),
                jnp.concatenate([-sine, cosine], axis=1),
            ],
            axis=0,
        )
        for cosine, sine in zip(part_of(3, 4), part_of(4, 5))
    ]
    row_inv = part_of(5, 6, 2 * PATCH)

    def wait_halo(sides):
        for step in steps:
            if (step[1] != 0) != sides:
                continue

            @pl.when(there((-step[0], -step[1])))
            def _():
                for n, message in enumerate(messages):
                    if message[0] == step:
                        halo_copy(n).wait_recv()

    def lane_tiles(x):
        return [x[:, i : i + LANES] for i in range(0, x.shape[1], LANES)]

    wait_halo(False)
    fields = [jnp.concatenate([planes[2 * p], planes[2 * p + 1]], axis=0) for p in range(6)]
    outs = lane_tiles(dot(row_fwd, split(jnp.concatenate(fields, axis=1))))
    high, low = split(jnp.concatenate([planes[p] for p in range(12, 18)], axis=1))
    outs += lane_tiles(mul(box_r, high) + mul(box_r, low))
    wait_halo(True)

    tall = rows + 2 * halo
    wide = lax.broadcasted_iota(jnp.int32, (tall, LANES), 1)
    in_left = lax.rem(wide, 2 * MARGIN) < MARGIN
    got_l, got_r = side_l[...], side_r[...]
    even = jnp.where(in_left, got_l, pltpu.roll(got_r, MARGIN, 1))
    later = jnp.where(in_left, pltpu.roll(got_l, LANES - MARGIN, 1), got_r)
    margins = dot(row_fwd, split(jnp.concatenate([even, later], axis=0)))

    def with_margins(out, q, at):
        moved = pltpu.roll(margins[at], (cells_c - 2 * MARGIN * q) % LANES, 1)
        lanes = lax.broadcasted_iota(jnp.int32, out.shape, 1)
        return jnp.where((lanes >= cells_c) & (lanes < cells_c + 2 * MARGIN), moved, out)

    middle = 2 * PATCH
    spectra, boxes = [], []
    for p in range(6):
        out = with_margins(outs[p], p, slice(None))
        spectra.append(jnp.concatenate([out[:PATCH], out[PATCH:middle]], axis=1))
        boxes.append(out[middle:])
    for i in range(6):
        start = middle + (i % 2) * cells_r
        boxes.append(with_margins(outs[6 + i], 6 + i // 2, slice(start, start + cells_r)))
    box = dot_exact(jnp.concatenate(boxes, axis=0), box_c) * (1.0 / 9.0)
    base = 12 * cells_r
    power = [box[base + i * cells_r : base + (i + 1) * cells_r] for i in range(6)]
    for k in range(2):
        for l in range(3):
            second = jnp.where(first[k][l], power[k + l + 1], power[k + l + 2])
            factor = lax.rsqrt(power[k] * second + 1e-06)
            for part in range(2):
                at = ((k * 3 + l) * 2 + part) * cells_r
                coh_ref[k, l, part] = (box[at : at + cells_r] * factor)[:, :cells_c]

    z = dot(split(jnp.concatenate(spectra, axis=0)), col_fwd)
    z_r, z_i = z[:, :LANES], z[:, LANES:]
    energy = z_r * z_r + z_i * z_i
    lane32 = lax.rem(lax.broadcasted_iota(jnp.int32, (6 * PATCH, LANES), 1), PATCH)
    left = jnp.where(lane32 == 0, pltpu.roll(energy, LANES - PATCH + 1, 1), pltpu.roll(energy, 1, 1))
    right = jnp.where(
        lane32 == PATCH - 1, pltpu.roll(energy, PATCH - 1, 1), pltpu.roll(energy, LANES - 1, 1)
    )
    across = energy + left + right

    def per_patch(values):
        sums = [
            jnp.sum(values[p * PATCH : (p + 1) * PATCH], axis=0, keepdims=True) for p in range(6)
        ]
        sums += [jnp.zeros((2, LANES), jnp.float32)]
        return dot_exact(jnp.concatenate(sums, axis=0), group) * (1.0 / (PATCH * PATCH))

    level = per_patch(energy)
    weights = []
    for p in range(6):
        part = across[p * PATCH : (p + 1) * PATCH]
        smooth = (part + pltpu.roll(part, 1, 0) + pltpu.roll(part, PATCH - 1, 0)) * (1.0 / 9.0)
        weights.append(jnp.sqrt(jnp.sqrt(smooth + level[p : p + 1] + 1e-06)))
    scale = 1.0 / per_patch(jnp.concatenate(weights, axis=0))
    filtered = []
    for p in range(6):
        weight = weights[p] * scale[p : p + 1]
        at = slice(p * PATCH, (p + 1) * PATCH)
        filtered.append(jnp.concatenate([z_r[at] * weight, z_i[at] * weight], axis=0))
    outs = lane_tiles(dot(row_inv, split(jnp.concatenate(filtered, axis=1))))
    back = [jnp.concatenate([o[:KEEP], o[KEEP:]], axis=1) for o in outs]
    final = dot(split(jnp.concatenate(back, axis=0)), col_inv)
    for p in range(6):
        at = slice(p * KEEP, (p + 1) * KEEP)
        filt_ref[p // 3, p % 3, 0] = final[at, :cells_c]
        filt_ref[p // 3, p % 3, 1] = final[at, LANES : LANES + cells_c]

    for c in range(chunks):
        for h in range(pieces):
            far_copy(c, h).wait_send()
            near_copy(c, h, img_hbm).wait_send()
    for step in steps:

        @pl.when(there(step))
        def _():
            for n, message in enumerate(messages):
                if message[0] == step:
                    halo_copy(n).wait_send()


def write(filt_in, coh_in, filt_out, coh_out, sems):
    copies = [
        pltpu.make_async_copy(filt_in, filt_out, sems.at[0]),
        pltpu.make_async_copy(coh_in, coh_out, sems.at[1]),
    ]
    for copy in copies:
        copy.start()
    for copy in copies:
        copy.wait()


def body(images, secondaries):
    per_device, _, rows, cols = images.shape
    links = secondaries.shape[1]
    dates = lax.axis_size("date")
    assert per_device == 2 and links == 3 and rows == 2 * KEEP and dates % 2 == 0 and dates > 4
    cells_r, cells_c = rows // LOOK_R, cols // LOOK_C
    tall = rows + 2 * MARGIN * LOOK_R
    chunks = rows // BAND
    out = jax.ShapeDtypeStruct((per_device, links, 2, cells_r, cells_c), jnp.float32)
    table, starts = tables(rows, cols)
    vmem = pl.BlockSpec(memory_space=pltpu.VMEM)
    hbm = pl.BlockSpec(memory_space=pltpu.HBM)
    sizes = (dates, lax.axis_size("row"), lax.axis_size("col"))
    dma = pltpu.SemaphoreType.DMA
    results = pl.pallas_call(
        functools.partial(kernel, sizes, starts),
        out_shape=(pltpu.VMEM(out.shape, out.dtype),) * 2,
        in_specs=[hbm, hbm, hbm],
        out_specs=(vmem, vmem),
        scratch_shapes=[
            pltpu.SMEM(secondaries.shape, jnp.int32),
            pltpu.VMEM(images.shape, jnp.float32),
            pltpu.VMEM(table.shape, jnp.bfloat16),
            pltpu.VMEM(images.shape, jnp.float32),
            pltpu.VMEM(images.shape, jnp.float32),
            pltpu.VMEM((18, tall, LANES), jnp.float32),
            pltpu.VMEM((rows, LANES), jnp.float32),
            pltpu.VMEM((rows, LANES), jnp.float32),
            pltpu.VMEM((tall, LANES), jnp.float32),
            pltpu.VMEM((tall, LANES), jnp.float32),
            dma((chunks * (cols // PIECE),)),
            dma((chunks * (cols // PIECE),)),
            dma((chunks * (cols // PIECE),)),
            dma((chunks * (cols // PIECE),)),
            dma((6 + 2 * chunks,)),
            dma((6 + 2 * chunks,)),
            dma((3,)),
        ],
        compiler_params=pltpu.CompilerParams(
            collective_id=0, has_side_effects=True, vmem_limit_bytes=VMEM_BYTES
        ),
        cost_estimate=pl.CostEstimate(flops=10**9, bytes_accessed=10**6, transcendentals=0),
    )(secondaries, images, jnp.asarray(table))
    return pl.pallas_call(
        write,
        out_shape=(out, out),
        in_specs=[vmem, vmem],
        out_specs=(hbm, hbm),
        scratch_shapes=[dma((2,))],
        compiler_params=pltpu.CompilerParams(vmem_limit_bytes=1024 * 1024),
    )(*results)


def solution(mesh):
    in_specs = (P("date", None, "row", "col"), P("date", None))
    out_specs = (P("date", None, None, "row", "col"), P("date", None, None, "row", "col"))
    return jax.shard_map(body, mesh=mesh, in_specs=in_specs, out_specs=out_specs, check_vma=False)
```

```python
import functools
import math

import jax
import jax.numpy as jnp
import ml_dtypes
import numpy as np
from jax import lax
from jax.experimental import pallas as pl
from jax.experimental.pallas import tpu as pltpu
from jax.sharding import PartitionSpec as P

LOOK_R = 2
LOOK_C = 8
PATCH = 32
KEEP = 24
MARGIN = 4
LANES = 128
BAND = 8
PIECE = 256
VMEM_BYTES = 64 * 1024 * 1024 - 800 * 1024
MESH = pl.DeviceIdType.MESH


def tables(rows, cols):
    cells_r, cells_c = rows // LOOK_R, cols // LOOK_C
    blocks = cells_c // KEEP
    halo_r = MARGIN * LOOK_R
    tall = rows + 2 * halo_r

    def lane(x):
        if x < 0:
            return cells_c + MARGIN + x
        return x if x < cells_c else x + MARGIN

    ticks = np.arange(PATCH)
    angle = (ticks[:, None] * ticks[None, :] % PATCH) * (2.0 * math.pi / PATCH)
    cosine, sine = np.cos(angle), np.sin(angle)

    pick = np.zeros((PATCH, tall))
    pick[np.arange(tall) // LOOK_R, np.arange(tall)] = 1.0
    row_c, row_s = cosine @ pick, sine @ pick
    box_r = np.zeros((cells_r, PATCH))
    for y in range(cells_r):
        box_r[y, MARGIN + y - 1 : MARGIN + y + 2] = 1.0
    box_r = box_r @ pick
    none = np.zeros_like(box_r)
    row_fwd = np.block([[row_c, row_s], [-row_s, row_c], [box_r, none], [none, box_r]])

    col_c, col_s = np.zeros((LANES, LANES)), np.zeros((LANES, LANES))
    for b in range(blocks):
        for x in range(PATCH):
            at = lane(b * KEEP - MARGIN + x)
            col_c[at, b * PATCH : (b + 1) * PATCH] = cosine[x]
            col_s[at, b * PATCH : (b + 1) * PATCH] = sine[x]
    centre = slice(MARGIN, MARGIN + KEEP)
    row_inv = np.block([[cosine[centre], -sine[centre]], [sine[centre], cosine[centre]]])
    inv_c, inv_s = np.zeros((LANES, LANES)), np.zeros((LANES, LANES))
    for b in range(blocks):
        inv_c[b * PATCH : (b + 1) * PATCH, b * KEEP : (b + 1) * KEEP] = cosine[:, centre]
        inv_s[b * PATCH : (b + 1) * PATCH, b * KEEP : (b + 1) * KEEP] = sine[:, centre]
    scale = 1.0 / (PATCH * PATCH)
    row_inv = np.concatenate([row_inv, row_inv], axis=1)
    stacked = [row_fwd, col_c, col_s, inv_c * scale, inv_s * scale, row_inv]
    whole = np.concatenate(stacked, axis=0).astype(np.float32)
    high = whole.astype(ml_dtypes.bfloat16)
    low = (whole - high.astype(np.float32)).astype(ml_dtypes.bfloat16)
    starts = np.cumsum([0] + [t.shape[0] for t in stacked])
    return np.stack([high, low]), [int(n) for n in starts]


def split(x):
    high = x.astype(jnp.bfloat16)
    return high, (x - high.astype(jnp.float32)).astype(jnp.bfloat16)


def mul(a, b):
    return lax.dot_general(a, b, (((1,), (0,)), ((), ())), preferred_element_type=jnp.float32)


def dot(a, b):
    return mul(a[0], b[0]) + (mul(a[1], b[0]) + mul(a[0], b[1]))


def dot_exact(x, b):
    high, low = split(x)
    return mul(high, b) + mul(low, b)


def dot_rows(twice, low_table, x):
    high, low = split(x)
    return mul(twice, jnp.concatenate([high, low], axis=0)) + mul(low_table, high)


def dot_twice(x, twice):
    return mul(jnp.concatenate(split(x), axis=1), twice)


def kernel(
    sizes,
    starts,
    sec_hbm,
    img_hbm,
    table_hbm,
    filt_ref,
    coh_ref,
    sec_ref,
    img_ref,
    table,
    near,
    far,
    planes,
    edge_l,
    edge_r,
    side_l,
    side_r,
    near_send,
    near_recv,
    far_send,
    far_recv,
    halo_send,
    halo_recv,
    local_sem,
):
    dates, n_rows, n_cols = sizes
    rows, cols = img_ref.shape[2], img_ref.shape[3]
    cells_c = cols // LOOK_C
    cells_r = rows // LOOK_R
    halo = MARGIN * LOOK_R
    chunks = rows // BAND
    date, row, col = lax.axis_index("date"), lax.axis_index("row"), lax.axis_index("col")
    odd = lax.rem(date, 2) == 1
    mate = date + 1 - 2 * lax.rem(date, 2)
    before = lax.rem(date + dates - 2, dates)
    after = lax.rem(date + 2, dates)
    steps = [(r, c) for r in (-1, 0, 1) for c in (-1, 0, 1) if (r, c) != (0, 0)]

    def there(step):
        test_r = [None, row < n_rows - 1, row > 0][step[0]]
        test_c = [None, col < n_cols - 1, col > 0][step[1]]
        tests = [t for t in (test_r, test_c) if t is not None]
        return functools.reduce(jnp.logical_and, tests)

    order = [0, chunks - 1] + list(range(1, chunks - 1))
    load_img = pltpu.make_async_copy(img_hbm, img_ref, local_sem.at[0])
    load_table = pltpu.make_async_copy(table_hbm, table, local_sem.at[1])
    load_sec = pltpu.make_async_copy(sec_hbm, sec_ref, local_sem.at[2])
    load_sec.start()
    load_img.start()
    load_table.start()
    barrier = pltpu.get_barrier_semaphore()
    for other in (before, after, mate):
        pl.semaphore_signal(barrier, inc=1, device_id=(other, row, col), device_id_type=MESH)
    count = jnp.int32(3)
    for step in steps:
        here = there(step)

        @pl.when(here)
        def _():
            pl.semaphore_signal(
                barrier,
                inc=1,
                device_id=(date, row + step[0], col + step[1]),
                device_id_type=MESH,
            )

        count = count + here.astype(jnp.int32)
    pl.semaphore_wait(barrier, count)

    def band(c):
        return pl.ds(c * BAND, BAND)

    pieces = cols // PIECE

    def far_copy(c, h):
        part = (slice(None), slice(None), band(c), pl.ds(h * PIECE, PIECE))
        return pltpu.make_async_remote_copy(
            src_ref=img_hbm.at[part],
            dst_ref=far.at[part],
            send_sem=far_send.at[c * pieces + h],
            recv_sem=far_recv.at[c * pieces + h],
            device_id=(before, row, col),
            device_id_type=MESH,
        )

    def near_copy(c, h, source):
        part = (slice(None), slice(None), band(c), pl.ds(h * PIECE, PIECE))
        return pltpu.make_async_remote_copy(
            src_ref=source.at[part],
            dst_ref=near.at[part],
            send_sem=near_send.at[c * pieces + h],
            recv_sem=near_recv.at[c * pieces + h],
            device_id=(mate, row, col),
            device_id_type=MESH,
        )

    for c in order:
        for h in range(pieces):
            far_copy(c, h).start()

            @pl.when(odd)
            def _():
                near_copy(c, h, img_hbm).start()

    for step in steps:

        @pl.when(jnp.logical_not(there(step)))
        def _():
            r, c = step
            at = {-1: slice(0, halo), 0: slice(halo, halo + rows), 1: slice(halo + rows, None)}[r]
            if c == 0:
                planes[:, at] = jnp.zeros_like(planes[:, at])
            else:
                side = side_l if c < 0 else side_r
                side[at] = jnp.zeros_like(side[at])

    total = 2 * dates
    load_sec.wait()

    def is_first(k, l):
        return lax.rem(sec_ref[k, l] - (2 * date + k) + total, total) == l + 1

    first = [[is_first(k, l) for l in range(3)] for k in range(2)]

    def lane_of(x):
        return jnp.where(x < 0, cells_c + MARGIN + x, jnp.where(x < cells_c, x, x + MARGIN))

    cell = lax.broadcasted_iota(jnp.int32, (cols, LANES), 0) // LOOK_C
    looks = jnp.where(
        cell == lax.broadcasted_iota(jnp.int32, (cols, LANES), 1), 1.0 / (LOOK_R * LOOK_C), 0.0
    ).astype(jnp.bfloat16)
    from_lane = lax.broadcasted_iota(jnp.int32, (LANES, LANES), 0)
    to_lane = lax.broadcasted_iota(jnp.int32, (LANES, LANES), 1)
    box_c = (from_lane == to_lane) | (from_lane == lane_of(to_lane - 1))
    box_c = box_c | (from_lane == lane_of(to_lane + 1))
    box_c = jnp.where(box_c & (to_lane < cells_c), 1.0, 0.0).astype(jnp.bfloat16)
    box_c = jnp.concatenate([box_c, box_c], axis=0)
    from_cell = jnp.where(
        from_lane < cells_c,
        from_lane,
        jnp.where(from_lane < cells_c + MARGIN, from_lane - cells_c, from_lane) - MARGIN,
    )
    in_patch = from_cell - (to_lane // PATCH * KEEP - MARGIN)
    window = (in_patch >= 0) & (in_patch < PATCH) & (from_lane < cells_c + 2 * MARGIN)
    window = jnp.where(window, 1.0, 0.0).astype(jnp.bfloat16)
    group = jnp.where(from_lane // PATCH == to_lane // PATCH, 1.0, 0.0).astype(jnp.bfloat16)

    def look_sums(c, h):
        at, across = band(c), pl.ds(h * PIECE, PIECE)

        def date_image(i):
            source = (img_ref, near, far)[i // 2]
            return source[i % 2, 0, at, across], source[i % 2, 1, at, across]

        images = [date_image(i) for i in range(6)]
        parts = []
        for k in range(2):
            a_r, a_i = images[k]
            for l in range(3):
                low, high = images[k + l + 1], images[k + l + 2]
                b_r = jnp.where(first[k][l], low[0], high[0])
                b_i = jnp.where(first[k][l], low[1], high[1])
                parts += [a_r * b_r + a_i * b_i, a_i * b_r - a_r * b_i]
        parts += [r * r + i * i for r, i in images]
        return dot_exact(jnp.concatenate(parts, axis=0), looks[h * PIECE : (h + 1) * PIECE])

    def keep(c, summed):
        at = band(c)
        lanes = lax.broadcasted_iota(jnp.int32, (BAND, LANES), 1)
        pack_l = jnp.zeros((BAND, LANES), jnp.float32)
        pack_r = jnp.zeros((BAND, LANES), jnp.float32)
        for p in range(planes.shape[0]):
            own = summed[p * BAND : (p + 1) * BAND]
            planes[p, pl.ds(halo + c * BAND, BAND)] = own
            mine = (lanes >= p * MARGIN) & (lanes < (p + 1) * MARGIN)
            pack_l = jnp.where(mine, pltpu.roll(own, (p * MARGIN) % LANES, 1), pack_l)
            shift = (p * MARGIN - (cells_c - MARGIN)) % LANES
            pack_r = jnp.where(mine, pltpu.roll(own, shift, 1), pack_r)
        edge_l[at] = pack_l
        edge_r[at] = pack_r

    messages = []
    for step in steps:
        if step[0] == 0:
            messages += [(step, c * BAND, BAND, c) for c in range(chunks)]
        else:
            c = 0 if step[0] < 0 else chunks - 1
            messages.append((step, c * BAND, BAND, c))

    def halo_copy(n):
        (r, c), start, size, _ = messages[n]
        source_at = pl.ds(start, size)
        target_at = pl.ds(halo + start - r * rows, size)
        if c == 0:
            source, target = planes.at[:, pl.ds(halo + start, size)], planes.at[:, target_at]
        elif c < 0:
            source, target = edge_l.at[source_at], side_r.at[target_at]
        else:
            source, target = edge_r.at[source_at], side_l.at[target_at]
        return pltpu.make_async_remote_copy(
            src_ref=source,
            dst_ref=target,
            send_sem=halo_send.at[n],
            recv_sem=halo_recv.at[n],
            device_id=(date, row + r, col + c),
            device_id_type=MESH,
        )

    load_img.wait()
    for c in order:
        summed = None
        for h in range(pieces):
            far_copy(c, h).wait_recv()

            @pl.when(jnp.logical_not(odd))
            def _():
                near_copy(c, h, far).start()

            near_copy(c, h, img_hbm).wait_recv()
            part = look_sums(c, h)
            summed = part if summed is None else summed + part
        keep(c, summed)
        for step in steps:

            @pl.when(there(step))
            def _():
                for n, message in enumerate(messages):
                    if message[0] == step and message[3] == c:
                        halo_copy(n).start()

    load_table.wait()

    def part_of(i, j, lanes=LANES):
        rows_at = slice(starts[i], starts[j])
        return table[0, rows_at, :lanes], table[1, rows_at, :lanes]

    row_fwd, row_fwd_low = part_of(0, 1)
    row_fwd = jnp.concatenate([row_fwd, row_fwd], axis=1)
    box_r = table[0, starts[0] + 2 * PATCH : starts[0] + 2 * PATCH + cells_r, : rows + 2 * halo]
    col_fwd = [
        jnp.concatenate(
            [
                jnp.concatenate([cosine, -sine], axis=1),
                jnp.concatenate([sine, cosine], axis=1),
            ],
            axis=0,
        )
        for cosine, sine in zip(part_of(1, 2), part_of(2, 3))
    ]
    col_inv = [
        jnp.concatenate(
            [
                jnp.concatenate([cosine, sine], axis=1),
                jnp.concatenate([-sine, cosine], axis=1),
            ],
            axis=0,
        )
        for cosine, sine in zip(part_of(3, 4), part_of(4, 5))
    ]
    row_inv = table[0, starts[5] : starts[6]]
    row_inv_low = table[1, starts[5] : starts[6], : 2 * PATCH]

    def wait_halo(sides):
        for step in steps:
            if (step[1] != 0) != sides:
                continue

            @pl.when(there((-step[0], -step[1])))
            def _():
                for n, message in enumerate(messages):
                    if message[0] == step:
                        halo_copy(n).wait_recv()

    def lane_tiles(x):
        return [x[:, i : i + LANES] for i in range(0, x.shape[1], LANES)]

    wait_halo(False)
    fields = [jnp.concatenate([planes[2 * p], planes[2 * p + 1]], axis=0) for p in range(6)]
    outs = lane_tiles(dot_rows(row_fwd, row_fwd_low, jnp.concatenate(fields, axis=1)))
    powers = jnp.concatenate([planes[p] for p in range(12, 18)], axis=1)
    box_twice = jnp.concatenate([box_r, box_r], axis=1)
    outs += lane_tiles(mul(box_twice, jnp.concatenate(split(powers), axis=0)))
    wait_halo(True)

    tall = rows + 2 * halo
    wide = lax.broadcasted_iota(jnp.int32, (tall, LANES), 1)
    in_left = lax.rem(wide, 2 * MARGIN) < MARGIN
    got_l, got_r = side_l[...], side_r[...]
    even = jnp.where(in_left, got_l, pltpu.roll(got_r, MARGIN, 1))
    later = jnp.where(in_left, pltpu.roll(got_l, LANES - MARGIN, 1), got_r)
    margins = dot_rows(row_fwd, row_fwd_low, jnp.concatenate([even, later], axis=0))

    def with_margins(out, q, at):
        moved = pltpu.roll(margins[at], (cells_c - 2 * MARGIN * q) % LANES, 1)
        lanes = lax.broadcasted_iota(jnp.int32, out.shape, 1)
        return jnp.where((lanes >= cells_c) & (lanes < cells_c + 2 * MARGIN), moved, out)

    middle = 2 * PATCH
    spectra, boxes = [], []
    for p in range(6):
        out = with_margins(outs[p], p, slice(None))
        spectra.append(jnp.concatenate([out[:PATCH], out[PATCH:middle]], axis=1))
        boxes.append(out[middle:])
    for i in range(6):
        start = middle + (i % 2) * cells_r
        boxes.append(with_margins(outs[6 + i], 6 + i // 2, slice(start, start + cells_r)))
    box = dot_twice(jnp.concatenate(boxes, axis=0), box_c) * (1.0 / 9.0)
    base = 12 * cells_r
    power = [box[base + i * cells_r : base + (i + 1) * cells_r] for i in range(6)]
    for k in range(2):
        for l in range(3):
            second = jnp.where(first[k][l], power[k + l + 1], power[k + l + 2])
            factor = lax.rsqrt(power[k] * second + 1e-06)
            for part in range(2):
                at = ((k * 3 + l) * 2 + part) * cells_r
                coh_ref[k, l, part] = (box[at : at + cells_r] * factor)[:, :cells_c]

    z = dot(split(jnp.concatenate(spectra, axis=0)), col_fwd)
    z_r, z_i = z[:, :LANES], z[:, LANES:]
    energy = z_r * z_r + z_i * z_i
    lane32 = lax.rem(lax.broadcasted_iota(jnp.int32, (6 * PATCH, LANES), 1), PATCH)
    left = jnp.where(lane32 == 0, pltpu.roll(energy, LANES - PATCH + 1, 1), pltpu.roll(energy, 1, 1))
    right = jnp.where(
        lane32 == PATCH - 1, pltpu.roll(energy, PATCH - 1, 1), pltpu.roll(energy, LANES - 1, 1)
    )
    across = energy + left + right

    def per_patch(tiles, sums_of, scale):
        sums = [jnp.sum(tile, axis=0, keepdims=True) for tile in tiles]
        sums += [jnp.zeros((2, LANES), jnp.float32)]
        return dot_exact(jnp.concatenate(sums, axis=0), sums_of) * scale

    level = per_patch(
        [s[:, :LANES] * s[:, :LANES] + s[:, LANES:] * s[:, LANES:] for s in spectra],
        window,
        1.0 / PATCH,
    )
    weights = []
    for p in range(6):
        part = across[p * PATCH : (p + 1) * PATCH]
        smooth = (part + pltpu.roll(part, 1, 0) + pltpu.roll(part, PATCH - 1, 0)) * (1.0 / 9.0)
        weights.append(jnp.sqrt(jnp.sqrt(smooth + level[p : p + 1] + 1e-06)))
    scale = 1.0 / per_patch(weights, group, 1.0 / (PATCH * PATCH))
    filtered = []
    for p in range(6):
        weight = weights[p]
        at = slice(p * PATCH, (p + 1) * PATCH)
        filtered.append(jnp.concatenate([z_r[at] * weight, z_i[at] * weight], axis=0))
    outs = lane_tiles(dot_rows(row_inv, row_inv_low, jnp.concatenate(filtered, axis=1)))
    outs = [o * scale[p : p + 1] for p, o in enumerate(outs)]
    back = [jnp.concatenate([o[:KEEP], o[KEEP:]], axis=1) for o in outs]
    final = dot(split(jnp.concatenate(back, axis=0)), col_inv)
    for p in range(6):
        at = slice(p * KEEP, (p + 1) * KEEP)
        filt_ref[p // 3, p % 3, 0] = final[at, :cells_c]
        filt_ref[p // 3, p % 3, 1] = final[at, LANES : LANES + cells_c]

    for c in range(chunks):
        for h in range(pieces):
            far_copy(c, h).wait_send()
            near_copy(c, h, img_hbm).wait_send()
    for step in steps:

        @pl.when(there(step))
        def _():
            for n, message in enumerate(messages):
                if message[0] == step:
                    halo_copy(n).wait_send()


def write(filt_in, coh_in, filt_out, coh_out, sems):
    copies = [
        pltpu.make_async_copy(filt_in, filt_out, sems.at[0]),
        pltpu.make_async_copy(coh_in, coh_out, sems.at[1]),
    ]
    for copy in copies:
        copy.start()
    for copy in copies:
        copy.wait()


def body(images, secondaries):
    per_device, _, rows, cols = images.shape
    links = secondaries.shape[1]
    dates = lax.axis_size("date")
    assert per_device == 2 and links == 3 and rows == 2 * KEEP and dates % 2 == 0 and dates > 4
    cells_r, cells_c = rows // LOOK_R, cols // LOOK_C
    tall = rows + 2 * MARGIN * LOOK_R
    chunks = rows // BAND
    out = jax.ShapeDtypeStruct((per_device, links, 2, cells_r, cells_c), jnp.float32)
    table, starts = tables(rows, cols)
    vmem = pl.BlockSpec(memory_space=pltpu.VMEM)
    hbm = pl.BlockSpec(memory_space=pltpu.HBM)
    sizes = (dates, lax.axis_size("row"), lax.axis_size("col"))
    dma = pltpu.SemaphoreType.DMA
    results = pl.pallas_call(
        functools.partial(kernel, sizes, starts),
        out_shape=(pltpu.VMEM(out.shape, out.dtype),) * 2,
        in_specs=[hbm, hbm, hbm],
        out_specs=(vmem, vmem),
        scratch_shapes=[
            pltpu.SMEM(secondaries.shape, jnp.int32),
            pltpu.VMEM(images.shape, jnp.float32),
            pltpu.VMEM(table.shape, jnp.bfloat16),
            pltpu.VMEM(images.shape, jnp.float32),
            pltpu.VMEM(images.shape, jnp.float32),
            pltpu.VMEM((18, tall, LANES), jnp.float32),
            pltpu.VMEM((rows, LANES), jnp.float32),
            pltpu.VMEM((rows, LANES), jnp.float32),
            pltpu.VMEM((tall, LANES), jnp.float32),
            pltpu.VMEM((tall, LANES), jnp.float32),
            dma((chunks * (cols // PIECE),)),
            dma((chunks * (cols // PIECE),)),
            dma((chunks * (cols // PIECE),)),
            dma((chunks * (cols // PIECE),)),
            dma((6 + 2 * chunks,)),
            dma((6 + 2 * chunks,)),
            dma((3,)),
        ],
        compiler_params=pltpu.CompilerParams(
            collective_id=0, has_side_effects=True, vmem_limit_bytes=VMEM_BYTES
        ),
        cost_estimate=pl.CostEstimate(flops=10**9, bytes_accessed=10**6, transcendentals=0),
    )(secondaries, images, jnp.asarray(table))
    return pl.pallas_call(
        write,
        out_shape=(out, out),
        in_specs=[vmem, vmem],
        out_specs=(hbm, hbm),
        scratch_shapes=[dma((2,))],
        compiler_params=pltpu.CompilerParams(vmem_limit_bytes=1024 * 1024),
    )(*results)


def solution(mesh):
    in_specs = (P("date", None, "row", "col"), P("date", None))
    out_specs = (P("date", None, None, "row", "col"), P("date", None, None, "row", "col"))
    return jax.shard_map(body, mesh=mesh, in_specs=in_specs, out_specs=out_specs, check_vma=False)
```

```python
import functools
import math

import jax
import jax.numpy as jnp
import ml_dtypes
import numpy as np
from jax import lax
from jax.experimental import pallas as pl
from jax.experimental.pallas import tpu as pltpu
from jax.sharding import PartitionSpec as P

LOOK_R = 2
LOOK_C = 8
PATCH = 32
KEEP = 24
MARGIN = 4
LANES = 128
BAND = 8
PIECE = 256
VMEM_BYTES = 64 * 1024 * 1024 - 800 * 1024
MESH = pl.DeviceIdType.MESH


def tables(rows, cols):
    cells_r, cells_c = rows // LOOK_R, cols // LOOK_C
    blocks = cells_c // KEEP
    halo_r = MARGIN * LOOK_R
    tall = rows + 2 * halo_r

    def lane(x):
        if x < 0:
            return cells_c + MARGIN + x
        return x if x < cells_c else x + MARGIN

    ticks = np.arange(PATCH)
    angle = (ticks[:, None] * ticks[None, :] % PATCH) * (2.0 * math.pi / PATCH)
    cosine, sine = np.cos(angle), np.sin(angle)

    pick = np.zeros((PATCH, tall))
    pick[np.arange(tall) // LOOK_R, np.arange(tall)] = 1.0
    row_c, row_s = cosine @ pick, sine @ pick
    box_r = np.zeros((cells_r, PATCH))
    for y in range(cells_r):
        box_r[y, MARGIN + y - 1 : MARGIN + y + 2] = 1.0
    box_r = box_r @ pick
    none = np.zeros_like(box_r)
    row_fwd = np.block([[row_c, row_s], [-row_s, row_c], [box_r, none], [none, box_r]])

    col_c, col_s = np.zeros((LANES, LANES)), np.zeros((LANES, LANES))
    for b in range(blocks):
        for x in range(PATCH):
            at = lane(b * KEEP - MARGIN + x)
            col_c[at, b * PATCH : (b + 1) * PATCH] = cosine[x]
            col_s[at, b * PATCH : (b + 1) * PATCH] = sine[x]
    centre = slice(MARGIN, MARGIN + KEEP)
    row_inv = np.block([[cosine[centre], -sine[centre]], [sine[centre], cosine[centre]]])
    inv_c, inv_s = np.zeros((LANES, LANES)), np.zeros((LANES, LANES))
    for b in range(blocks):
        inv_c[b * PATCH : (b + 1) * PATCH, b * KEEP : (b + 1) * KEEP] = cosine[:, centre]
        inv_s[b * PATCH : (b + 1) * PATCH, b * KEEP : (b + 1) * KEEP] = sine[:, centre]
    scale = 1.0 / (PATCH * PATCH)
    row_inv = np.concatenate([row_inv, row_inv], axis=1)
    stacked = [row_fwd, col_c, col_s, inv_c * scale, inv_s * scale, row_inv]
    whole = np.concatenate(stacked, axis=0).astype(np.float32)
    high = whole.astype(ml_dtypes.bfloat16)
    low = (whole - high.astype(np.float32)).astype(ml_dtypes.bfloat16)
    starts = np.cumsum([0] + [t.shape[0] for t in stacked])
    return np.stack([high, low]), [int(n) for n in starts]


def split(x):
    high = x.astype(jnp.bfloat16)
    return high, (x - high.astype(jnp.float32)).astype(jnp.bfloat16)


def mul(a, b):
    return lax.dot_general(a, b, (((1,), (0,)), ((), ())), preferred_element_type=jnp.float32)


def dot(a, b):
    return mul(a[0], b[0]) + (mul(a[1], b[0]) + mul(a[0], b[1]))


def dot_exact(x, b):
    high, low = split(x)
    return mul(high, b) + mul(low, b)


def dot_rows(twice, low_table, x):
    high, low = split(x)
    return mul(twice, jnp.concatenate([high, low], axis=0)) + mul(low_table, high)


def dot_twice(x, twice):
    return mul(jnp.concatenate(split(x), axis=1), twice)


def kernel(
    sizes,
    starts,
    sec_hbm,
    img_hbm,
    table_hbm,
    filt_ref,
    coh_ref,
    sec_ref,
    img_ref,
    table,
    near,
    far,
    planes,
    edge_l,
    edge_r,
    side_l,
    side_r,
    near_send,
    near_recv,
    far_send,
    far_recv,
    halo_send,
    halo_recv,
    local_sem,
):
    dates, n_rows, n_cols = sizes
    rows, cols = img_ref.shape[2], img_ref.shape[3]
    cells_c = cols // LOOK_C
    cells_r = rows // LOOK_R
    halo = MARGIN * LOOK_R
    chunks = rows // BAND
    date, row, col = lax.axis_index("date"), lax.axis_index("row"), lax.axis_index("col")
    odd = lax.rem(date, 2) == 1
    mate = date + 1 - 2 * lax.rem(date, 2)
    before = lax.rem(date + dates - 2, dates)
    after = lax.rem(date + 2, dates)
    steps = [(r, c) for r in (-1, 0, 1) for c in (-1, 0, 1) if (r, c) != (0, 0)]

    def there(step):
        test_r = [None, row < n_rows - 1, row > 0][step[0]]
        test_c = [None, col < n_cols - 1, col > 0][step[1]]
        tests = [t for t in (test_r, test_c) if t is not None]
        return functools.reduce(jnp.logical_and, tests)

    order = [0, chunks - 1] + list(range(1, chunks - 1))
    load_img = pltpu.make_async_copy(img_hbm, img_ref, local_sem.at[0])
    load_table = pltpu.make_async_copy(table_hbm, table, local_sem.at[1])
    load_sec = pltpu.make_async_copy(sec_hbm, sec_ref, local_sem.at[2])
    load_sec.start()
    load_img.start()
    load_table.start()
    barrier = pltpu.get_barrier_semaphore()
    for other in (before, after, mate):
        pl.semaphore_signal(barrier, inc=1, device_id=(other, row, col), device_id_type=MESH)
    count = jnp.int32(3)
    for step in steps:
        here = there(step)

        @pl.when(here)
        def _():
            pl.semaphore_signal(
                barrier,
                inc=1,
                device_id=(date, row + step[0], col + step[1]),
                device_id_type=MESH,
            )

        count = count + here.astype(jnp.int32)
    pl.semaphore_wait(barrier, count)

    def band(c):
        return pl.ds(c * BAND, BAND)

    pieces = cols // PIECE

    def far_copy(c, h):
        part = (slice(None), slice(None), band(c), pl.ds(h * PIECE, PIECE))
        return pltpu.make_async_remote_copy(
            src_ref=img_hbm.at[part],
            dst_ref=far.at[part],
            send_sem=far_send.at[c * pieces + h],
            recv_sem=far_recv.at[c * pieces + h],
            device_id=(before, row, col),
            device_id_type=MESH,
        )

    def near_copy(c, h, source):
        part = (slice(None), slice(None), band(c), pl.ds(h * PIECE, PIECE))
        return pltpu.make_async_remote_copy(
            src_ref=source.at[part],
            dst_ref=near.at[part],
            send_sem=near_send.at[c * pieces + h],
            recv_sem=near_recv.at[c * pieces + h],
            device_id=(mate, row, col),
            device_id_type=MESH,
        )

    for c in order:
        for h in range(pieces):
            far_copy(c, h).start()

            @pl.when(odd)
            def _():
                near_copy(c, h, img_hbm).start()

    for step in steps:

        @pl.when(jnp.logical_not(there(step)))
        def _():
            r, c = step
            at = {-1: slice(0, halo), 0: slice(halo, halo + rows), 1: slice(halo + rows, None)}[r]
            if c == 0:
                planes[:, at] = jnp.zeros_like(planes[:, at])
            else:
                side = side_l if c < 0 else side_r
                side[at] = jnp.zeros_like(side[at])

    total = 2 * dates
    load_sec.wait()

    def is_first(k, l):
        return lax.rem(sec_ref[k, l] - (2 * date + k) + total, total) == l + 1

    first = [[is_first(k, l) for l in range(3)] for k in range(2)]

    def lane_of(x):
        return jnp.where(x < 0, cells_c + MARGIN + x, jnp.where(x < cells_c, x, x + MARGIN))

    cell = lax.broadcasted_iota(jnp.int32, (cols, LANES), 0) // LOOK_C
    looks = jnp.where(
        cell == lax.broadcasted_iota(jnp.int32, (cols, LANES), 1), 1.0 / (LOOK_R * LOOK_C), 0.0
    ).astype(jnp.bfloat16)
    from_lane = lax.broadcasted_iota(jnp.int32, (LANES, LANES), 0)
    to_lane = lax.broadcasted_iota(jnp.int32, (LANES, LANES), 1)
    box_c = (from_lane == to_lane) | (from_lane == lane_of(to_lane - 1))
    box_c = box_c | (from_lane == lane_of(to_lane + 1))
    box_c = jnp.where(box_c & (to_lane < cells_c), 1.0, 0.0).astype(jnp.bfloat16)
    box_c = jnp.concatenate([box_c, box_c], axis=0)
    from_cell = jnp.where(
        from_lane < cells_c,
        from_lane,
        jnp.where(from_lane < cells_c + MARGIN, from_lane - cells_c, from_lane) - MARGIN,
    )
    in_patch = from_cell - (to_lane // PATCH * KEEP - MARGIN)
    window = (in_patch >= 0) & (in_patch < PATCH) & (from_lane < cells_c + 2 * MARGIN)
    window = jnp.where(window, 1.0, 0.0).astype(jnp.bfloat16)
    group = jnp.where(from_lane // PATCH == to_lane // PATCH, 1.0, 0.0).astype(jnp.bfloat16)

    def look_sums(c, h):
        at, across = band(c), pl.ds(h * PIECE, PIECE)

        def date_image(i):
            source = (img_ref, near, far)[i // 2]
            return source[i % 2, 0, at, across], source[i % 2, 1, at, across]

        images = [date_image(i) for i in range(6)]
        parts = []
        for k in range(2):
            a_r, a_i = images[k]
            for l in range(3):
                low, high = images[k + l + 1], images[k + l + 2]
                b_r = jnp.where(first[k][l], low[0], high[0])
                b_i = jnp.where(first[k][l], low[1], high[1])
                parts += [a_r * b_r + a_i * b_i, a_i * b_r - a_r * b_i]
        parts += [r * r + i * i for r, i in images]
        return dot_exact(jnp.concatenate(parts, axis=0), looks[h * PIECE : (h + 1) * PIECE])

    def keep(c, summed):
        at = band(c)
        lanes = lax.broadcasted_iota(jnp.int32, (BAND, LANES), 1)
        pack_l = jnp.zeros((BAND, LANES), jnp.float32)
        pack_r = jnp.zeros((BAND, LANES), jnp.float32)
        for p in range(planes.shape[0]):
            own = summed[p * BAND : (p + 1) * BAND]
            planes[p, pl.ds(halo + c * BAND, BAND)] = own
            mine = (lanes >= p * MARGIN) & (lanes < (p + 1) * MARGIN)
            pack_l = jnp.where(mine, pltpu.roll(own, (p * MARGIN) % LANES, 1), pack_l)
            shift = (p * MARGIN - (cells_c - MARGIN)) % LANES
            pack_r = jnp.where(mine, pltpu.roll(own, shift, 1), pack_r)
        edge_l[at] = pack_l
        edge_r[at] = pack_r

    messages = []
    for step in steps:
        if step[0] == 0:
            messages += [(step, c * BAND, BAND, c) for c in range(chunks)]
        else:
            c = 0 if step[0] < 0 else chunks - 1
            messages.append((step, c * BAND, BAND, c))

    def halo_copy(n):
        (r, c), start, size, _ = messages[n]
        source_at = pl.ds(start, size)
        target_at = pl.ds(halo + start - r * rows, size)
        if c == 0:
            source, target = planes.at[:, pl.ds(halo + start, size)], planes.at[:, target_at]
        elif c < 0:
            source, target = edge_l.at[source_at], side_r.at[target_at]
        else:
            source, target = edge_r.at[source_at], side_l.at[target_at]
        return pltpu.make_async_remote_copy(
            src_ref=source,
            dst_ref=target,
            send_sem=halo_send.at[n],
            recv_sem=halo_recv.at[n],
            device_id=(date, row + r, col + c),
            device_id_type=MESH,
        )

    load_img.wait()
    every = [(c, h) for c in order for h in range(pieces)]
    summed = None
    for now, done in zip(every + [None], [None] + every):
        if now is not None:
            far_copy(*now).wait_recv()

            @pl.when(jnp.logical_not(odd))
            def _():
                near_copy(*now, far).start()

        if done is None:
            continue
        c, h = done
        near_copy(c, h, img_hbm).wait_recv()
        part = look_sums(c, h)
        summed = part if h == 0 else summed + part
        if h < pieces - 1:
            continue
        keep(c, summed)
        for step in steps:

            @pl.when(there(step))
            def _():
                for n, message in enumerate(messages):
                    if message[0] == step and message[3] == c:
                        halo_copy(n).start()

    load_table.wait()

    def part_of(i, j, lanes=LANES):
        rows_at = slice(starts[i], starts[j])
        return table[0, rows_at, :lanes], table[1, rows_at, :lanes]

    row_fwd, row_fwd_low = part_of(0, 1)
    row_fwd = jnp.concatenate([row_fwd, row_fwd], axis=1)
    box_r = table[0, starts[0] + 2 * PATCH : starts[0] + 2 * PATCH + cells_r, : rows + 2 * halo]
    col_fwd = [
        jnp.concatenate(
            [
                jnp.concatenate([cosine, -sine], axis=1),
                jnp.concatenate([sine, cosine], axis=1),
            ],
            axis=0,
        )
        for cosine, sine in zip(part_of(1, 2), part_of(2, 3))
    ]
    col_inv = [
        jnp.concatenate(
            [
                jnp.concatenate([cosine, sine], axis=1),
                jnp.concatenate([-sine, cosine], axis=1),
            ],
            axis=0,
        )
        for cosine, sine in zip(part_of(3, 4), part_of(4, 5))
    ]
    row_inv = table[0, starts[5] : starts[6]]
    row_inv_low = table[1, starts[5] : starts[6], : 2 * PATCH]

    def wait_halo(sides):
        for step in steps:
            if (step[1] != 0) != sides:
                continue

            @pl.when(there((-step[0], -step[1])))
            def _():
                for n, message in enumerate(messages):
                    if message[0] == step:
                        halo_copy(n).wait_recv()

    def lane_tiles(x):
        return [x[:, i : i + LANES] for i in range(0, x.shape[1], LANES)]

    wait_halo(False)
    fields = [jnp.concatenate([planes[2 * p], planes[2 * p + 1]], axis=0) for p in range(6)]
    outs = lane_tiles(dot_rows(row_fwd, row_fwd_low, jnp.concatenate(fields, axis=1)))
    powers = jnp.concatenate([planes[p] for p in range(12, 18)], axis=1)
    box_twice = jnp.concatenate([box_r, box_r], axis=1)
    outs += lane_tiles(mul(box_twice, jnp.concatenate(split(powers), axis=0)))
    wait_halo(True)

    tall = rows + 2 * halo
    wide = lax.broadcasted_iota(jnp.int32, (tall, LANES), 1)
    in_left = lax.rem(wide, 2 * MARGIN) < MARGIN
    got_l, got_r = side_l[...], side_r[...]
    even = jnp.where(in_left, got_l, pltpu.roll(got_r, MARGIN, 1))
    later = jnp.where(in_left, pltpu.roll(got_l, LANES - MARGIN, 1), got_r)
    margins = dot_rows(row_fwd, row_fwd_low, jnp.concatenate([even, later], axis=0))

    def with_margins(out, q, at):
        moved = pltpu.roll(margins[at], (cells_c - 2 * MARGIN * q) % LANES, 1)
        lanes = lax.broadcasted_iota(jnp.int32, out.shape, 1)
        return jnp.where((lanes >= cells_c) & (lanes < cells_c + 2 * MARGIN), moved, out)

    middle = 2 * PATCH
    spectra, boxes = [], []
    for p in range(6):
        out = with_margins(outs[p], p, slice(None))
        spectra.append(jnp.concatenate([out[:PATCH], out[PATCH:middle]], axis=1))
        boxes.append(out[middle:])
    for i in range(6):
        start = middle + (i % 2) * cells_r
        boxes.append(with_margins(outs[6 + i], 6 + i // 2, slice(start, start + cells_r)))
    box = dot_twice(jnp.concatenate(boxes, axis=0), box_c) * (1.0 / 9.0)
    base = 12 * cells_r
    power = [box[base + i * cells_r : base + (i + 1) * cells_r] for i in range(6)]
    for k in range(2):
        for l in range(3):
            second = jnp.where(first[k][l], power[k + l + 1], power[k + l + 2])
            factor = lax.rsqrt(power[k] * second + 1e-06)
            for part in range(2):
                at = ((k * 3 + l) * 2 + part) * cells_r
                coh_ref[k, l, part] = (box[at : at + cells_r] * factor)[:, :cells_c]

    z = dot(split(jnp.concatenate(spectra, axis=0)), col_fwd)
    z_r, z_i = z[:, :LANES], z[:, LANES:]
    energy = z_r * z_r + z_i * z_i
    lane32 = lax.rem(lax.broadcasted_iota(jnp.int32, (6 * PATCH, LANES), 1), PATCH)
    left = jnp.where(lane32 == 0, pltpu.roll(energy, LANES - PATCH + 1, 1), pltpu.roll(energy, 1, 1))
    right = jnp.where(
        lane32 == PATCH - 1, pltpu.roll(energy, PATCH - 1, 1), pltpu.roll(energy, LANES - 1, 1)
    )
    across = energy + left + right

    def per_patch(tiles, sums_of, scale):
        sums = [jnp.sum(tile, axis=0, keepdims=True) for tile in tiles]
        sums += [jnp.zeros((2, LANES), jnp.float32)]
        return dot_exact(jnp.concatenate(sums, axis=0), sums_of) * scale

    level = per_patch(
        [s[:, :LANES] * s[:, :LANES] + s[:, LANES:] * s[:, LANES:] for s in spectra],
        window,
        1.0 / PATCH,
    )
    weights = []
    for p in range(6):
        part = across[p * PATCH : (p + 1) * PATCH]
        smooth = (part + pltpu.roll(part, 1, 0) + pltpu.roll(part, PATCH - 1, 0)) * (1.0 / 9.0)
        weights.append(jnp.sqrt(jnp.sqrt(smooth + level[p : p + 1] + 1e-06)))
    scale = 1.0 / per_patch(weights, group, 1.0 / (PATCH * PATCH))
    filtered = []
    for p in range(6):
        weight = weights[p]
        at = slice(p * PATCH, (p + 1) * PATCH)
        filtered.append(jnp.concatenate([z_r[at] * weight, z_i[at] * weight], axis=0))
    outs = lane_tiles(dot_rows(row_inv, row_inv_low, jnp.concatenate(filtered, axis=1)))
    outs = [o * scale[p : p + 1] for p, o in enumerate(outs)]
    back = [jnp.concatenate([o[:KEEP], o[KEEP:]], axis=1) for o in outs]
    final = dot(split(jnp.concatenate(back, axis=0)), col_inv)
    for p in range(6):
        at = slice(p * KEEP, (p + 1) * KEEP)
        filt_ref[p // 3, p % 3, 0] = final[at, :cells_c]
        filt_ref[p // 3, p % 3, 1] = final[at, LANES : LANES + cells_c]

    for c in range(chunks):
        for h in range(pieces):
            far_copy(c, h).wait_send()
            near_copy(c, h, img_hbm).wait_send()
    for step in steps:

        @pl.when(there(step))
        def _():
            for n, message in enumerate(messages):
                if message[0] == step:
                    halo_copy(n).wait_send()


def write(filt_in, coh_in, filt_out, coh_out, sems):
    copies = [
        pltpu.make_async_copy(filt_in, filt_out, sems.at[0]),
        pltpu.make_async_copy(coh_in, coh_out, sems.at[1]),
    ]
    for copy in copies:
        copy.start()
    for copy in copies:
        copy.wait()


def body(images, secondaries):
    per_device, _, rows, cols = images.shape
    links = secondaries.shape[1]
    dates = lax.axis_size("date")
    assert per_device == 2 and links == 3 and rows == 2 * KEEP and dates % 2 == 0 and dates > 4
    cells_r, cells_c = rows // LOOK_R, cols // LOOK_C
    tall = rows + 2 * MARGIN * LOOK_R
    chunks = rows // BAND
    out = jax.ShapeDtypeStruct((per_device, links, 2, cells_r, cells_c), jnp.float32)
    table, starts = tables(rows, cols)
    vmem = pl.BlockSpec(memory_space=pltpu.VMEM)
    hbm = pl.BlockSpec(memory_space=pltpu.HBM)
    sizes = (dates, lax.axis_size("row"), lax.axis_size("col"))
    dma = pltpu.SemaphoreType.DMA
    results = pl.pallas_call(
        functools.partial(kernel, sizes, starts),
        out_shape=(pltpu.VMEM(out.shape, out.dtype),) * 2,
        in_specs=[hbm, hbm, hbm],
        out_specs=(vmem, vmem),
        scratch_shapes=[
            pltpu.SMEM(secondaries.shape, jnp.int32),
            pltpu.VMEM(images.shape, jnp.float32),
            pltpu.VMEM(table.shape, jnp.bfloat16),
            pltpu.VMEM(images.shape, jnp.float32),
            pltpu.VMEM(images.shape, jnp.float32),
            pltpu.VMEM((18, tall, LANES), jnp.float32),
            pltpu.VMEM((rows, LANES), jnp.float32),
            pltpu.VMEM((rows, LANES), jnp.float32),
            pltpu.VMEM((tall, LANES), jnp.float32),
            pltpu.VMEM((tall, LANES), jnp.float32),
            dma((chunks * (cols // PIECE),)),
            dma((chunks * (cols // PIECE),)),
            dma((chunks * (cols // PIECE),)),
            dma((chunks * (cols // PIECE),)),
            dma((6 + 2 * chunks,)),
            dma((6 + 2 * chunks,)),
            dma((3,)),
        ],
        compiler_params=pltpu.CompilerParams(
            collective_id=0, has_side_effects=True, vmem_limit_bytes=VMEM_BYTES
        ),
        cost_estimate=pl.CostEstimate(flops=10**9, bytes_accessed=10**6, transcendentals=0),
    )(secondaries, images, jnp.asarray(table))
    return pl.pallas_call(
        write,
        out_shape=(out, out),
        in_specs=[vmem, vmem],
        out_specs=(hbm, hbm),
        scratch_shapes=[dma((2,))],
        compiler_params=pltpu.CompilerParams(vmem_limit_bytes=1024 * 1024),
    )(*results)


def solution(mesh):
    in_specs = (P("date", None, "row", "col"), P("date", None))
    out_specs = (P("date", None, None, "row", "col"), P("date", None, None, "row", "col"))
    return jax.shard_map(body, mesh=mesh, in_specs=in_specs, out_specs=out_specs, check_vma=False)
```

```python
import functools
import math

import jax
import jax.numpy as jnp
import ml_dtypes
import numpy as np
from jax import lax
from jax.experimental import pallas as pl
from jax.experimental.pallas import tpu as pltpu
from jax.sharding import PartitionSpec as P

LOOK_R = 2
LOOK_C = 8
PATCH = 32
KEEP = 24
MARGIN = 4
LANES = 128
BAND = 8
PIECE = 256
DIRECT = 2
VMEM_BYTES = 64 * 1024 * 1024 - 800 * 1024
MESH = pl.DeviceIdType.MESH


def tables(rows, cols):
    cells_r, cells_c = rows // LOOK_R, cols // LOOK_C
    blocks = cells_c // KEEP
    halo_r = MARGIN * LOOK_R
    tall = rows + 2 * halo_r

    def lane(x):
        if x < 0:
            return cells_c + MARGIN + x
        return x if x < cells_c else x + MARGIN

    ticks = np.arange(PATCH)
    angle = (ticks[:, None] * ticks[None, :] % PATCH) * (2.0 * math.pi / PATCH)
    cosine, sine = np.cos(angle), np.sin(angle)

    pick = np.zeros((PATCH, tall))
    pick[np.arange(tall) // LOOK_R, np.arange(tall)] = 1.0
    row_c, row_s = cosine @ pick, sine @ pick
    box_r = np.zeros((cells_r, PATCH))
    for y in range(cells_r):
        box_r[y, MARGIN + y - 1 : MARGIN + y + 2] = 1.0
    box_r = box_r @ pick
    none = np.zeros_like(box_r)
    row_fwd = np.block([[row_c, row_s], [-row_s, row_c], [box_r, none], [none, box_r]])

    col_c, col_s = np.zeros((LANES, LANES)), np.zeros((LANES, LANES))
    for b in range(blocks):
        for x in range(PATCH):
            at = lane(b * KEEP - MARGIN + x)
            col_c[at, b * PATCH : (b + 1) * PATCH] = cosine[x]
            col_s[at, b * PATCH : (b + 1) * PATCH] = sine[x]
    centre = slice(MARGIN, MARGIN + KEEP)
    row_inv = np.block([[cosine[centre], -sine[centre]], [sine[centre], cosine[centre]]])
    inv_c, inv_s = np.zeros((LANES, LANES)), np.zeros((LANES, LANES))
    for b in range(blocks):
        inv_c[b * PATCH : (b + 1) * PATCH, b * KEEP : (b + 1) * KEEP] = cosine[:, centre]
        inv_s[b * PATCH : (b + 1) * PATCH, b * KEEP : (b + 1) * KEEP] = sine[:, centre]
    scale = 1.0 / (PATCH * PATCH)
    row_inv = np.concatenate([row_inv, row_inv], axis=1)
    stacked = [row_fwd, col_c, col_s, inv_c * scale, inv_s * scale, row_inv]
    whole = np.concatenate(stacked, axis=0).astype(np.float32)
    high = whole.astype(ml_dtypes.bfloat16)
    low = (whole - high.astype(np.float32)).astype(ml_dtypes.bfloat16)
    starts = np.cumsum([0] + [t.shape[0] for t in stacked])
    return np.stack([high, low]), [int(n) for n in starts]


def split(x):
    high = x.astype(jnp.bfloat16)
    return high, (x - high.astype(jnp.float32)).astype(jnp.bfloat16)


def mul(a, b):
    return lax.dot_general(a, b, (((1,), (0,)), ((), ())), preferred_element_type=jnp.float32)


def dot(a, b):
    return mul(a[0], b[0]) + (mul(a[1], b[0]) + mul(a[0], b[1]))


def dot_exact(x, b):
    high, low = split(x)
    return mul(high, b) + mul(low, b)


def dot_rows(twice, low_table, x):
    high, low = split(x)
    return mul(twice, jnp.concatenate([high, low], axis=0)) + mul(low_table, high)


def dot_twice(x, twice):
    return mul(jnp.concatenate(split(x), axis=1), twice)


def kernel(
    sizes,
    starts,
    sec_hbm,
    img_hbm,
    table_hbm,
    filt_ref,
    coh_ref,
    sec_ref,
    img_ref,
    table,
    near,
    far,
    passing,
    planes,
    edge_l,
    edge_r,
    side_l,
    side_r,
    near_send,
    near_recv,
    far_send,
    far_recv,
    halo_send,
    halo_recv,
    pass_send,
    pass_recv,
    local_sem,
):
    dates, n_rows, n_cols = sizes
    rows, cols = img_ref.shape[2], img_ref.shape[3]
    cells_c = cols // LOOK_C
    cells_r = rows // LOOK_R
    halo = MARGIN * LOOK_R
    chunks = rows // BAND
    date, row, col = lax.axis_index("date"), lax.axis_index("row"), lax.axis_index("col")
    odd = lax.rem(date, 2) == 1
    mate = date + 1 - 2 * lax.rem(date, 2)
    before = lax.rem(date + dates - 2, dates)
    after = lax.rem(date + 2, dates)
    steps = [(r, c) for r in (-1, 0, 1) for c in (-1, 0, 1) if (r, c) != (0, 0)]

    def there(step):
        test_r = [None, row < n_rows - 1, row > 0][step[0]]
        test_c = [None, col < n_cols - 1, col > 0][step[1]]
        tests = [t for t in (test_r, test_c) if t is not None]
        return functools.reduce(jnp.logical_and, tests)

    order = [0, chunks - 1] + list(range(1, chunks - 1))
    load_img = pltpu.make_async_copy(img_hbm, img_ref, local_sem.at[0])
    load_table = pltpu.make_async_copy(table_hbm, table, local_sem.at[1])
    load_sec = pltpu.make_async_copy(sec_hbm, sec_ref, local_sem.at[2])
    load_sec.start()
    load_img.start()
    load_table.start()
    barrier = pltpu.get_barrier_semaphore()
    for other in (before, after, mate):
        pl.semaphore_signal(barrier, inc=1, device_id=(other, row, col), device_id_type=MESH)
    count = jnp.int32(3)
    for step in steps:
        here = there(step)

        @pl.when(here)
        def _():
            pl.semaphore_signal(
                barrier,
                inc=1,
                device_id=(date, row + step[0], col + step[1]),
                device_id_type=MESH,
            )

        count = count + here.astype(jnp.int32)
    pl.semaphore_wait(barrier, count)

    def band(c):
        return pl.ds(c * BAND, BAND)

    pieces = cols // PIECE

    def far_copy(c, h):
        part = (slice(None), slice(None), band(c), pl.ds(h * PIECE, PIECE))
        return pltpu.make_async_remote_copy(
            src_ref=img_hbm.at[part],
            dst_ref=far.at[part],
            send_sem=far_send.at[c * pieces + h],
            recv_sem=far_recv.at[c * pieces + h],
            device_id=(before, row, col),
            device_id_type=MESH,
        )

    def near_copy(c, h, source):
        part = (slice(None), slice(None), band(c), pl.ds(h * PIECE, PIECE))
        return pltpu.make_async_remote_copy(
            src_ref=source.at[part],
            dst_ref=near.at[part],
            send_sem=near_send.at[c * pieces + h],
            recv_sem=near_recv.at[c * pieces + h],
            device_id=(mate, row, col),
            device_id_type=MESH,
        )

    every = [(c, h) for c in order for h in range(pieces)]
    direct = every[len(every) - DIRECT :]

    def pass_copy(c, h):
        n = direct.index((c, h))
        return pltpu.make_async_remote_copy(
            src_ref=img_hbm.at[:, :, band(c), pl.ds(h * PIECE, PIECE)],
            dst_ref=passing.at[n],
            send_sem=pass_send.at[n],
            recv_sem=pass_recv.at[n],
            device_id=(mate, row, col),
            device_id_type=MESH,
        )

    def last_copy(c, h):
        n = direct.index((c, h))
        return pltpu.make_async_remote_copy(
            src_ref=passing.at[n],
            dst_ref=near.at[:, :, band(c), pl.ds(h * PIECE, PIECE)],
            send_sem=pass_send.at[n],
            recv_sem=near_recv.at[c * pieces + h],
            device_id=(before, row, col),
            device_id_type=MESH,
        )

    for c, h in direct:

        @pl.when(jnp.logical_not(odd))
        def _():
            pass_copy(c, h).start()

    for c in order:
        for h in range(pieces):
            far_copy(c, h).start()

            @pl.when(odd)
            def _():
                near_copy(c, h, img_hbm).start()

    for step in steps:

        @pl.when(jnp.logical_not(there(step)))
        def _():
            r, c = step
            at = {-1: slice(0, halo), 0: slice(halo, halo + rows), 1: slice(halo + rows, None)}[r]
            if c == 0:
                planes[:, at] = jnp.zeros_like(planes[:, at])
            else:
                side = side_l if c < 0 else side_r
                side[at] = jnp.zeros_like(side[at])

    total = 2 * dates
    load_sec.wait()

    def is_first(k, l):
        return lax.rem(sec_ref[k, l] - (2 * date + k) + total, total) == l + 1

    first = [[is_first(k, l) for l in range(3)] for k in range(2)]

    def lane_of(x):
        return jnp.where(x < 0, cells_c + MARGIN + x, jnp.where(x < cells_c, x, x + MARGIN))

    cell = lax.broadcasted_iota(jnp.int32, (cols, LANES), 0) // LOOK_C
    looks = jnp.where(
        cell == lax.broadcasted_iota(jnp.int32, (cols, LANES), 1), 1.0 / (LOOK_R * LOOK_C), 0.0
    ).astype(jnp.bfloat16)
    from_lane = lax.broadcasted_iota(jnp.int32, (LANES, LANES), 0)
    to_lane = lax.broadcasted_iota(jnp.int32, (LANES, LANES), 1)
    box_c = (from_lane == to_lane) | (from_lane == lane_of(to_lane - 1))
    box_c = box_c | (from_lane == lane_of(to_lane + 1))
    box_c = jnp.where(box_c & (to_lane < cells_c), 1.0, 0.0).astype(jnp.bfloat16)
    box_c = jnp.concatenate([box_c, box_c], axis=0)
    from_cell = jnp.where(
        from_lane < cells_c,
        from_lane,
        jnp.where(from_lane < cells_c + MARGIN, from_lane - cells_c, from_lane) - MARGIN,
    )
    in_patch = from_cell - (to_lane // PATCH * KEEP - MARGIN)
    window = (in_patch >= 0) & (in_patch < PATCH) & (from_lane < cells_c + 2 * MARGIN)
    window = jnp.where(window, 1.0, 0.0).astype(jnp.bfloat16)
    group = jnp.where(from_lane // PATCH == to_lane // PATCH, 1.0, 0.0).astype(jnp.bfloat16)

    def look_sums(c, h):
        at, across = band(c), pl.ds(h * PIECE, PIECE)

        def date_image(i):
            source = (img_ref, near, far)[i // 2]
            return source[i % 2, 0, at, across], source[i % 2, 1, at, across]

        images = [date_image(i) for i in range(6)]
        parts = []
        for k in range(2):
            a_r, a_i = images[k]
            for l in range(3):
                low, high = images[k + l + 1], images[k + l + 2]
                b_r = jnp.where(first[k][l], low[0], high[0])
                b_i = jnp.where(first[k][l], low[1], high[1])
                parts += [a_r * b_r + a_i * b_i, a_i * b_r - a_r * b_i]
        parts += [r * r + i * i for r, i in images]
        return dot_exact(jnp.concatenate(parts, axis=0), looks[h * PIECE : (h + 1) * PIECE])

    def keep(c, summed):
        at = band(c)
        lanes = lax.broadcasted_iota(jnp.int32, (BAND, LANES), 1)
        pack_l = jnp.zeros((BAND, LANES), jnp.float32)
        pack_r = jnp.zeros((BAND, LANES), jnp.float32)
        for p in range(planes.shape[0]):
            own = summed[p * BAND : (p + 1) * BAND]
            planes[p, pl.ds(halo + c * BAND, BAND)] = own
            mine = (lanes >= p * MARGIN) & (lanes < (p + 1) * MARGIN)
            pack_l = jnp.where(mine, pltpu.roll(own, (p * MARGIN) % LANES, 1), pack_l)
            shift = (p * MARGIN - (cells_c - MARGIN)) % LANES
            pack_r = jnp.where(mine, pltpu.roll(own, shift, 1), pack_r)
        edge_l[at] = pack_l
        edge_r[at] = pack_r

    messages = []
    for step in steps:
        if step[0] == 0:
            messages += [(step, c * BAND, BAND, c) for c in range(chunks)]
        else:
            c = 0 if step[0] < 0 else chunks - 1
            messages.append((step, c * BAND, BAND, c))

    def halo_copy(n):
        (r, c), start, size, _ = messages[n]
        source_at = pl.ds(start, size)
        target_at = pl.ds(halo + start - r * rows, size)
        if c == 0:
            source, target = planes.at[:, pl.ds(halo + start, size)], planes.at[:, target_at]
        elif c < 0:
            source, target = edge_l.at[source_at], side_r.at[target_at]
        else:
            source, target = edge_r.at[source_at], side_l.at[target_at]
        return pltpu.make_async_remote_copy(
            src_ref=source,
            dst_ref=target,
            send_sem=halo_send.at[n],
            recv_sem=halo_recv.at[n],
            device_id=(date, row + r, col + c),
            device_id_type=MESH,
        )

    for c, h in direct:

        @pl.when(odd)
        def _():
            pass_copy(c, h).wait_recv()
            last_copy(c, h).start()

    load_img.wait()
    summed = None
    for now, done in zip(every + [None], [None] + every):
        if now is not None:
            far_copy(*now).wait_recv()

            if now not in direct:

                @pl.when(jnp.logical_not(odd))
                def _():
                    near_copy(*now, far).start()

        if done is None:
            continue
        c, h = done
        near_copy(c, h, img_hbm).wait_recv()
        part = look_sums(c, h)
        summed = part if h == 0 else summed + part
        if h < pieces - 1:
            continue
        keep(c, summed)
        for step in steps:

            @pl.when(there(step))
            def _():
                for n, message in enumerate(messages):
                    if message[0] == step and message[3] == c:
                        halo_copy(n).start()

    load_table.wait()

    def part_of(i, j, lanes=LANES):
        rows_at = slice(starts[i], starts[j])
        return table[0, rows_at, :lanes], table[1, rows_at, :lanes]

    row_fwd, row_fwd_low = part_of(0, 1)
    row_fwd = jnp.concatenate([row_fwd, row_fwd], axis=1)
    box_r = table[0, starts[0] + 2 * PATCH : starts[0] + 2 * PATCH + cells_r, : rows + 2 * halo]
    col_fwd = [
        jnp.concatenate(
            [
                jnp.concatenate([cosine, -sine], axis=1),
                jnp.concatenate([sine, cosine], axis=1),
            ],
            axis=0,
        )
        for cosine, sine in zip(part_of(1, 2), part_of(2, 3))
    ]
    col_inv = [
        jnp.concatenate(
            [
                jnp.concatenate([cosine, sine], axis=1),
                jnp.concatenate([-sine, cosine], axis=1),
            ],
            axis=0,
        )
        for cosine, sine in zip(part_of(3, 4), part_of(4, 5))
    ]
    row_inv = table[0, starts[5] : starts[6]]
    row_inv_low = table[1, starts[5] : starts[6], : 2 * PATCH]

    def wait_halo(sides):
        for step in steps:
            if (step[1] != 0) != sides:
                continue

            @pl.when(there((-step[0], -step[1])))
            def _():
                for n, message in enumerate(messages):
                    if message[0] == step:
                        halo_copy(n).wait_recv()

    def lane_tiles(x):
        return [x[:, i : i + LANES] for i in range(0, x.shape[1], LANES)]

    wait_halo(False)
    fields = [jnp.concatenate([planes[2 * p], planes[2 * p + 1]], axis=0) for p in range(6)]
    outs = lane_tiles(dot_rows(row_fwd, row_fwd_low, jnp.concatenate(fields, axis=1)))
    powers = jnp.concatenate([planes[p] for p in range(12, 18)], axis=1)
    box_twice = jnp.concatenate([box_r, box_r], axis=1)
    outs += lane_tiles(mul(box_twice, jnp.concatenate(split(powers), axis=0)))
    wait_halo(True)

    tall = rows + 2 * halo
    wide = lax.broadcasted_iota(jnp.int32, (tall, LANES), 1)
    in_left = lax.rem(wide, 2 * MARGIN) < MARGIN
    got_l, got_r = side_l[...], side_r[...]
    even = jnp.where(in_left, got_l, pltpu.roll(got_r, MARGIN, 1))
    later = jnp.where(in_left, pltpu.roll(got_l, LANES - MARGIN, 1), got_r)
    margins = dot_rows(row_fwd, row_fwd_low, jnp.concatenate([even, later], axis=0))

    def with_margins(out, q, at):
        moved = pltpu.roll(margins[at], (cells_c - 2 * MARGIN * q) % LANES, 1)
        lanes = lax.broadcasted_iota(jnp.int32, out.shape, 1)
        return jnp.where((lanes >= cells_c) & (lanes < cells_c + 2 * MARGIN), moved, out)

    middle = 2 * PATCH
    spectra, boxes = [], []
    for p in range(6):
        out = with_margins(outs[p], p, slice(None))
        spectra.append(jnp.concatenate([out[:PATCH], out[PATCH:middle]], axis=1))
        boxes.append(out[middle:])
    for i in range(6):
        start = middle + (i % 2) * cells_r
        boxes.append(with_margins(outs[6 + i], 6 + i // 2, slice(start, start + cells_r)))
    box = dot_twice(jnp.concatenate(boxes, axis=0), box_c) * (1.0 / 9.0)
    base = 12 * cells_r
    power = [box[base + i * cells_r : base + (i + 1) * cells_r] for i in range(6)]
    for k in range(2):
        for l in range(3):
            second = jnp.where(first[k][l], power[k + l + 1], power[k + l + 2])
            factor = lax.rsqrt(power[k] * second + 1e-06)
            for part in range(2):
                at = ((k * 3 + l) * 2 + part) * cells_r
                coh_ref[k, l, part] = (box[at : at + cells_r] * factor)[:, :cells_c]

    z = dot(split(jnp.concatenate(spectra, axis=0)), col_fwd)
    z_r, z_i = z[:, :LANES], z[:, LANES:]
    energy = z_r * z_r + z_i * z_i
    lane32 = lax.rem(lax.broadcasted_iota(jnp.int32, (6 * PATCH, LANES), 1), PATCH)
    left = jnp.where(lane32 == 0, pltpu.roll(energy, LANES - PATCH + 1, 1), pltpu.roll(energy, 1, 1))
    right = jnp.where(
        lane32 == PATCH - 1, pltpu.roll(energy, PATCH - 1, 1), pltpu.roll(energy, LANES - 1, 1)
    )
    across = energy + left + right

    def per_patch(tiles, sums_of, scale):
        sums = [jnp.sum(tile, axis=0, keepdims=True) for tile in tiles]
        sums += [jnp.zeros((2, LANES), jnp.float32)]
        return dot_exact(jnp.concatenate(sums, axis=0), sums_of) * scale

    level = per_patch(
        [s[:, :LANES] * s[:, :LANES] + s[:, LANES:] * s[:, LANES:] for s in spectra],
        window,
        1.0 / PATCH,
    )
    weights = []
    for p in range(6):
        part = across[p * PATCH : (p + 1) * PATCH]
        smooth = (part + pltpu.roll(part, 1, 0) + pltpu.roll(part, PATCH - 1, 0)) * (1.0 / 9.0)
        weights.append(jnp.sqrt(jnp.sqrt(smooth + level[p : p + 1] + 1e-06)))
    scale = 1.0 / per_patch(weights, group, 1.0 / (PATCH * PATCH))
    filtered = []
    for p in range(6):
        weight = weights[p]
        at = slice(p * PATCH, (p + 1) * PATCH)
        filtered.append(jnp.concatenate([z_r[at] * weight, z_i[at] * weight], axis=0))
    outs = lane_tiles(dot_rows(row_inv, row_inv_low, jnp.concatenate(filtered, axis=1)))
    outs = [o * scale[p : p + 1] for p, o in enumerate(outs)]
    back = [jnp.concatenate([o[:KEEP], o[KEEP:]], axis=1) for o in outs]
    final = dot(split(jnp.concatenate(back, axis=0)), col_inv)
    for p in range(6):
        at = slice(p * KEEP, (p + 1) * KEEP)
        filt_ref[p // 3, p % 3, 0] = final[at, :cells_c]
        filt_ref[p // 3, p % 3, 1] = final[at, LANES : LANES + cells_c]

    for c in range(chunks):
        for h in range(pieces):
            far_copy(c, h).wait_send()
            if (c, h) not in direct:
                near_copy(c, h, img_hbm).wait_send()
    for c, h in direct:
        pass_copy(c, h).wait_send()

        @pl.when(odd)
        def _():
            near_copy(c, h, img_hbm).wait_send()

    for step in steps:

        @pl.when(there(step))
        def _():
            for n, message in enumerate(messages):
                if message[0] == step:
                    halo_copy(n).wait_send()


def write(filt_in, coh_in, filt_out, coh_out, sems):
    copies = [
        pltpu.make_async_copy(filt_in, filt_out, sems.at[0]),
        pltpu.make_async_copy(coh_in, coh_out, sems.at[1]),
    ]
    for copy in copies:
        copy.start()
    for copy in copies:
        copy.wait()


def body(images, secondaries):
    per_device, _, rows, cols = images.shape
    links = secondaries.shape[1]
    dates = lax.axis_size("date")
    assert per_device == 2 and links == 3 and rows == 2 * KEEP and dates % 2 == 0 and dates > 4
    cells_r, cells_c = rows // LOOK_R, cols // LOOK_C
    tall = rows + 2 * MARGIN * LOOK_R
    chunks = rows // BAND
    out = jax.ShapeDtypeStruct((per_device, links, 2, cells_r, cells_c), jnp.float32)
    table, starts = tables(rows, cols)
    vmem = pl.BlockSpec(memory_space=pltpu.VMEM)
    hbm = pl.BlockSpec(memory_space=pltpu.HBM)
    sizes = (dates, lax.axis_size("row"), lax.axis_size("col"))
    dma = pltpu.SemaphoreType.DMA
    results = pl.pallas_call(
        functools.partial(kernel, sizes, starts),
        out_shape=(pltpu.VMEM(out.shape, out.dtype),) * 2,
        in_specs=[hbm, hbm, hbm],
        out_specs=(vmem, vmem),
        scratch_shapes=[
            pltpu.SMEM(secondaries.shape, jnp.int32),
            pltpu.VMEM(images.shape, jnp.float32),
            pltpu.VMEM(table.shape, jnp.bfloat16),
            pltpu.VMEM(images.shape, jnp.float32),
            pltpu.VMEM(images.shape, jnp.float32),
            pltpu.VMEM((DIRECT,) + images.shape[:2] + (BAND, PIECE), jnp.float32),
            pltpu.VMEM((18, tall, LANES), jnp.float32),
            pltpu.VMEM((rows, LANES), jnp.float32),
            pltpu.VMEM((rows, LANES), jnp.float32),
            pltpu.VMEM((tall, LANES), jnp.float32),
            pltpu.VMEM((tall, LANES), jnp.float32),
            dma((chunks * (cols // PIECE),)),
            dma((chunks * (cols // PIECE),)),
            dma((chunks * (cols // PIECE),)),
            dma((chunks * (cols // PIECE),)),
            dma((6 + 2 * chunks,)),
            dma((6 + 2 * chunks,)),
            dma((DIRECT,)),
            dma((DIRECT,)),
            dma((3,)),
        ],
        compiler_params=pltpu.CompilerParams(
            collective_id=0, has_side_effects=True, vmem_limit_bytes=VMEM_BYTES
        ),
        cost_estimate=pl.CostEstimate(flops=10**9, bytes_accessed=10**6, transcendentals=0),
    )(secondaries, images, jnp.asarray(table))
    return pl.pallas_call(
        write,
        out_shape=(out, out),
        in_specs=[vmem, vmem],
        out_specs=(hbm, hbm),
        scratch_shapes=[dma((2,))],
        compiler_params=pltpu.CompilerParams(vmem_limit_bytes=1024 * 1024),
    )(*results)


def solution(mesh):
    in_specs = (P("date", None, "row", "col"), P("date", None))
    out_specs = (P("date", None, None, "row", "col"), P("date", None, None, "row", "col"))
    return jax.shard_map(body, mesh=mesh, in_specs=in_specs, out_specs=out_specs, check_vma=False)
```

```python
import functools
import math

import jax
import jax.numpy as jnp
import ml_dtypes
import numpy as np
from jax import lax
from jax.experimental import pallas as pl
from jax.experimental.pallas import tpu as pltpu
from jax.sharding import PartitionSpec as P

LOOK_R = 2
LOOK_C = 8
PATCH = 32
KEEP = 24
MARGIN = 4
LANES = 128
BAND = 8
PIECE = 256
DIRECT = 1
VMEM_BYTES = 64 * 1024 * 1024 - 800 * 1024
MESH = pl.DeviceIdType.MESH


def tables(rows, cols):
    cells_r, cells_c = rows // LOOK_R, cols // LOOK_C
    blocks = cells_c // KEEP
    halo_r = MARGIN * LOOK_R
    tall = rows + 2 * halo_r

    def lane(x):
        if x < 0:
            return cells_c + MARGIN + x
        return x if x < cells_c else x + MARGIN

    ticks = np.arange(PATCH)
    angle = (ticks[:, None] * ticks[None, :] % PATCH) * (2.0 * math.pi / PATCH)
    cosine, sine = np.cos(angle), np.sin(angle)

    pick = np.zeros((PATCH, tall))
    pick[np.arange(tall) // LOOK_R, np.arange(tall)] = 1.0
    row_c, row_s = cosine @ pick, sine @ pick
    box_r = np.zeros((cells_r, PATCH))
    for y in range(cells_r):
        box_r[y, MARGIN + y - 1 : MARGIN + y + 2] = 1.0
    box_r = box_r @ pick
    none = np.zeros_like(box_r)
    row_fwd = np.block([[row_c, row_s], [-row_s, row_c], [box_r, none], [none, box_r]])

    col_c, col_s = np.zeros((LANES, LANES)), np.zeros((LANES, LANES))
    for b in range(blocks):
        for x in range(PATCH):
            at = lane(b * KEEP - MARGIN + x)
            col_c[at, b * PATCH : (b + 1) * PATCH] = cosine[x]
            col_s[at, b * PATCH : (b + 1) * PATCH] = sine[x]
    centre = slice(MARGIN, MARGIN + KEEP)
    row_inv = np.block([[cosine[centre], -sine[centre]], [sine[centre], cosine[centre]]])
    inv_c, inv_s = np.zeros((LANES, LANES)), np.zeros((LANES, LANES))
    for b in range(blocks):
        inv_c[b * PATCH : (b + 1) * PATCH, b * KEEP : (b + 1) * KEEP] = cosine[:, centre]
        inv_s[b * PATCH : (b + 1) * PATCH, b * KEEP : (b + 1) * KEEP] = sine[:, centre]
    scale = 1.0 / (PATCH * PATCH)
    row_inv = np.concatenate([row_inv, row_inv], axis=1)
    stacked = [row_fwd, col_c, col_s, inv_c * scale, inv_s * scale, row_inv]
    whole = np.concatenate(stacked, axis=0).astype(np.float32)
    high = whole.astype(ml_dtypes.bfloat16)
    low = (whole - high.astype(np.float32)).astype(ml_dtypes.bfloat16)
    starts = np.cumsum([0] + [t.shape[0] for t in stacked])
    return np.stack([high, low]), [int(n) for n in starts]


def split(x):
    high = x.astype(jnp.bfloat16)
    return high, (x - high.astype(jnp.float32)).astype(jnp.bfloat16)


def mul(a, b):
    return lax.dot_general(a, b, (((1,), (0,)), ((), ())), preferred_element_type=jnp.float32)


def dot(a, b):
    return mul(a[0], b[0]) + (mul(a[1], b[0]) + mul(a[0], b[1]))


def dot_exact(x, b):
    high, low = split(x)
    return mul(high, b) + mul(low, b)


def dot_rows(twice, low_table, x):
    high, low = split(x)
    return mul(twice, jnp.concatenate([high, low], axis=0)) + mul(low_table, high)


def dot_twice(x, twice):
    return mul(jnp.concatenate(split(x), axis=1), twice)


def kernel(
    sizes,
    starts,
    sec_hbm,
    img_hbm,
    table_hbm,
    filt_ref,
    coh_ref,
    sec_ref,
    img_ref,
    table,
    near,
    far,
    passing,
    planes,
    edge_l,
    edge_r,
    side_l,
    side_r,
    near_send,
    near_recv,
    far_send,
    far_recv,
    halo_send,
    halo_recv,
    pass_send,
    pass_recv,
    local_sem,
):
    dates, n_rows, n_cols = sizes
    rows, cols = img_ref.shape[2], img_ref.shape[3]
    cells_c = cols // LOOK_C
    cells_r = rows // LOOK_R
    halo = MARGIN * LOOK_R
    chunks = rows // BAND
    date, row, col = lax.axis_index("date"), lax.axis_index("row"), lax.axis_index("col")
    odd = lax.rem(date, 2) == 1
    mate = date + 1 - 2 * lax.rem(date, 2)
    before = lax.rem(date + dates - 2, dates)
    after = lax.rem(date + 2, dates)
    steps = [(r, c) for r in (-1, 0, 1) for c in (-1, 0, 1) if (r, c) != (0, 0)]

    def there(step):
        test_r = [None, row < n_rows - 1, row > 0][step[0]]
        test_c = [None, col < n_cols - 1, col > 0][step[1]]
        tests = [t for t in (test_r, test_c) if t is not None]
        return functools.reduce(jnp.logical_and, tests)

    order = [0, chunks - 1] + list(range(1, chunks - 1))
    load_img = pltpu.make_async_copy(img_hbm, img_ref, local_sem.at[0])
    load_table = pltpu.make_async_copy(table_hbm, table, local_sem.at[1])
    load_sec = pltpu.make_async_copy(sec_hbm, sec_ref, local_sem.at[2])
    load_sec.start()
    load_img.start()
    load_table.start()
    barrier = pltpu.get_barrier_semaphore()
    for other in (before, after, mate):
        pl.semaphore_signal(barrier, inc=1, device_id=(other, row, col), device_id_type=MESH)
    count = jnp.int32(3)
    for step in steps:
        here = there(step)

        @pl.when(here)
        def _():
            pl.semaphore_signal(
                barrier,
                inc=1,
                device_id=(date, row + step[0], col + step[1]),
                device_id_type=MESH,
            )

        count = count + here.astype(jnp.int32)
    pl.semaphore_wait(barrier, count)

    def band(c):
        return pl.ds(c * BAND, BAND)

    pieces = cols // PIECE

    def far_copy(c, h):
        part = (slice(None), slice(None), band(c), pl.ds(h * PIECE, PIECE))
        return pltpu.make_async_remote_copy(
            src_ref=img_hbm.at[part],
            dst_ref=far.at[part],
            send_sem=far_send.at[c * pieces + h],
            recv_sem=far_recv.at[c * pieces + h],
            device_id=(before, row, col),
            device_id_type=MESH,
        )

    def near_copy(c, h, source):
        part = (slice(None), slice(None), band(c), pl.ds(h * PIECE, PIECE))
        return pltpu.make_async_remote_copy(
            src_ref=source.at[part],
            dst_ref=near.at[part],
            send_sem=near_send.at[c * pieces + h],
            recv_sem=near_recv.at[c * pieces + h],
            device_id=(mate, row, col),
            device_id_type=MESH,
        )

    every = [(c, h) for c in order for h in range(pieces)]
    direct = every[len(every) - DIRECT :]

    def pass_copy(c, h):
        n = direct.index((c, h))
        return pltpu.make_async_remote_copy(
            src_ref=img_hbm.at[:, :, band(c), pl.ds(h * PIECE, PIECE)],
            dst_ref=passing.at[n],
            send_sem=pass_send.at[n],
            recv_sem=pass_recv.at[n],
            device_id=(mate, row, col),
            device_id_type=MESH,
        )

    def last_copy(c, h):
        n = direct.index((c, h))
        return pltpu.make_async_remote_copy(
            src_ref=passing.at[n],
            dst_ref=near.at[:, :, band(c), pl.ds(h * PIECE, PIECE)],
            send_sem=pass_send.at[n],
            recv_sem=near_recv.at[c * pieces + h],
            device_id=(before, row, col),
            device_id_type=MESH,
        )

    for c, h in direct:

        @pl.when(jnp.logical_not(odd))
        def _():
            pass_copy(c, h).start()

    for c in order:
        for h in range(pieces):
            far_copy(c, h).start()

            @pl.when(odd)
            def _():
                near_copy(c, h, img_hbm).start()

    for step in steps:

        @pl.when(jnp.logical_not(there(step)))
        def _():
            r, c = step
            at = {-1: slice(0, halo), 0: slice(halo, halo + rows), 1: slice(halo + rows, None)}[r]
            if c == 0:
                planes[:, at] = jnp.zeros_like(planes[:, at])
            else:
                side = side_l if c < 0 else side_r
                side[at] = jnp.zeros_like(side[at])

    total = 2 * dates
    load_sec.wait()

    def is_first(k, l):
        return lax.rem(sec_ref[k, l] - (2 * date + k) + total, total) == l + 1

    first = [[is_first(k, l) for l in range(3)] for k in range(2)]

    def lane_of(x):
        return jnp.where(x < 0, cells_c + MARGIN + x, jnp.where(x < cells_c, x, x + MARGIN))

    cell = lax.broadcasted_iota(jnp.int32, (cols, LANES), 0) // LOOK_C
    looks = jnp.where(
        cell == lax.broadcasted_iota(jnp.int32, (cols, LANES), 1), 1.0 / (LOOK_R * LOOK_C), 0.0
    ).astype(jnp.bfloat16)
    from_lane = lax.broadcasted_iota(jnp.int32, (LANES, LANES), 0)
    to_lane = lax.broadcasted_iota(jnp.int32, (LANES, LANES), 1)
    box_c = (from_lane == to_lane) | (from_lane == lane_of(to_lane - 1))
    box_c = box_c | (from_lane == lane_of(to_lane + 1))
    box_c = jnp.where(box_c & (to_lane < cells_c), 1.0, 0.0).astype(jnp.bfloat16)
    box_c = jnp.concatenate([box_c, box_c], axis=0)
    from_cell = jnp.where(
        from_lane < cells_c,
        from_lane,
        jnp.where(from_lane < cells_c + MARGIN, from_lane - cells_c, from_lane) - MARGIN,
    )
    in_patch = from_cell - (to_lane // PATCH * KEEP - MARGIN)
    window = (in_patch >= 0) & (in_patch < PATCH) & (from_lane < cells_c + 2 * MARGIN)
    window = jnp.where(window, 1.0, 0.0).astype(jnp.bfloat16)
    group = jnp.where(from_lane // PATCH == to_lane // PATCH, 1.0, 0.0).astype(jnp.bfloat16)

    def look_sums(c, h):
        at, across = band(c), pl.ds(h * PIECE, PIECE)

        def date_image(i):
            source = (img_ref, near, far)[i // 2]
            return source[i % 2, 0, at, across], source[i % 2, 1, at, across]

        images = [date_image(i) for i in range(6)]
        parts = []
        for k in range(2):
            a_r, a_i = images[k]
            for l in range(3):
                low, high = images[k + l + 1], images[k + l + 2]
                b_r = jnp.where(first[k][l], low[0], high[0])
                b_i = jnp.where(first[k][l], low[1], high[1])
                parts += [a_r * b_r + a_i * b_i, a_i * b_r - a_r * b_i]
        parts += [r * r + i * i for r, i in images]
        return dot_exact(jnp.concatenate(parts, axis=0), looks[h * PIECE : (h + 1) * PIECE])

    def keep(c, summed):
        at = band(c)
        lanes = lax.broadcasted_iota(jnp.int32, (BAND, LANES), 1)
        pack_l = jnp.zeros((BAND, LANES), jnp.float32)
        pack_r = jnp.zeros((BAND, LANES), jnp.float32)
        for p in range(planes.shape[0]):
            own = summed[p * BAND : (p + 1) * BAND]
            planes[p, pl.ds(halo + c * BAND, BAND)] = own
            mine = (lanes >= p * MARGIN) & (lanes < (p + 1) * MARGIN)
            pack_l = jnp.where(mine, pltpu.roll(own, (p * MARGIN) % LANES, 1), pack_l)
            shift = (p * MARGIN - (cells_c - MARGIN)) % LANES
            pack_r = jnp.where(mine, pltpu.roll(own, shift, 1), pack_r)
        edge_l[at] = pack_l
        edge_r[at] = pack_r

    messages = []
    for step in steps:
        if step[0] == 0:
            messages += [(step, c * BAND, BAND, c) for c in range(chunks)]
        else:
            c = 0 if step[0] < 0 else chunks - 1
            messages.append((step, c * BAND, BAND, c))

    def halo_copy(n):
        (r, c), start, size, _ = messages[n]
        source_at = pl.ds(start, size)
        target_at = pl.ds(halo + start - r * rows, size)
        if c == 0:
            source, target = planes.at[:, pl.ds(halo + start, size)], planes.at[:, target_at]
        elif c < 0:
            source, target = edge_l.at[source_at], side_r.at[target_at]
        else:
            source, target = edge_r.at[source_at], side_l.at[target_at]
        return pltpu.make_async_remote_copy(
            src_ref=source,
            dst_ref=target,
            send_sem=halo_send.at[n],
            recv_sem=halo_recv.at[n],
            device_id=(date, row + r, col + c),
            device_id_type=MESH,
        )

    for c, h in direct:

        @pl.when(odd)
        def _():
            pass_copy(c, h).wait_recv()
            last_copy(c, h).start()

    load_img.wait()
    summed = None
    for now, done in zip(every + [None], [None] + every):
        if now is not None:
            far_copy(*now).wait_recv()

            if now not in direct:

                @pl.when(jnp.logical_not(odd))
                def _():
                    near_copy(*now, far).start()

        if done is None:
            continue
        c, h = done
        near_copy(c, h, img_hbm).wait_recv()
        part = look_sums(c, h)
        summed = part if h == 0 else summed + part
        if h < pieces - 1:
            continue
        keep(c, summed)
        for step in steps:

            @pl.when(there(step))
            def _():
                for n, message in enumerate(messages):
                    if message[0] == step and message[3] == c:
                        halo_copy(n).start()

    load_table.wait()

    def part_of(i, j, lanes=LANES):
        rows_at = slice(starts[i], starts[j])
        return table[0, rows_at, :lanes], table[1, rows_at, :lanes]

    row_fwd, row_fwd_low = part_of(0, 1)
    row_fwd = jnp.concatenate([row_fwd, row_fwd], axis=1)
    box_r = table[0, starts[0] + 2 * PATCH : starts[0] + 2 * PATCH + cells_r, : rows + 2 * halo]
    col_fwd = [
        jnp.concatenate(
            [
                jnp.concatenate([cosine, -sine], axis=1),
                jnp.concatenate([sine, cosine], axis=1),
            ],
            axis=0,
        )
        for cosine, sine in zip(part_of(1, 2), part_of(2, 3))
    ]
    col_inv = [
        jnp.concatenate(
            [
                jnp.concatenate([cosine, sine], axis=1),
                jnp.concatenate([-sine, cosine], axis=1),
            ],
            axis=0,
        )
        for cosine, sine in zip(part_of(3, 4), part_of(4, 5))
    ]
    row_inv = table[0, starts[5] : starts[6]]
    row_inv_low = table[1, starts[5] : starts[6], : 2 * PATCH]

    def wait_halo(sides):
        for step in steps:
            if (step[1] != 0) != sides:
                continue

            @pl.when(there((-step[0], -step[1])))
            def _():
                for n, message in enumerate(messages):
                    if message[0] == step:
                        halo_copy(n).wait_recv()

    def lane_tiles(x):
        return [x[:, i : i + LANES] for i in range(0, x.shape[1], LANES)]

    wait_halo(False)
    fields = [jnp.concatenate([planes[2 * p], planes[2 * p + 1]], axis=0) for p in range(6)]
    outs = lane_tiles(dot_rows(row_fwd, row_fwd_low, jnp.concatenate(fields, axis=1)))
    powers = jnp.concatenate([planes[p] for p in range(12, 18)], axis=1)
    box_twice = jnp.concatenate([box_r, box_r], axis=1)
    outs += lane_tiles(mul(box_twice, jnp.concatenate(split(powers), axis=0)))
    wait_halo(True)

    tall = rows + 2 * halo
    wide = lax.broadcasted_iota(jnp.int32, (tall, LANES), 1)
    in_left = lax.rem(wide, 2 * MARGIN) < MARGIN
    got_l, got_r = side_l[...], side_r[...]
    even = jnp.where(in_left, got_l, pltpu.roll(got_r, MARGIN, 1))
    later = jnp.where(in_left, pltpu.roll(got_l, LANES - MARGIN, 1), got_r)
    margins = dot_rows(row_fwd, row_fwd_low, jnp.concatenate([even, later], axis=0))

    def with_margins(out, q, at):
        moved = pltpu.roll(margins[at], (cells_c - 2 * MARGIN * q) % LANES, 1)
        lanes = lax.broadcasted_iota(jnp.int32, out.shape, 1)
        return jnp.where((lanes >= cells_c) & (lanes < cells_c + 2 * MARGIN), moved, out)

    middle = 2 * PATCH
    spectra, boxes = [], []
    for p in range(6):
        out = with_margins(outs[p], p, slice(None))
        spectra.append(jnp.concatenate([out[:PATCH], out[PATCH:middle]], axis=1))
        boxes.append(out[middle:])
    for i in range(6):
        start = middle + (i % 2) * cells_r
        boxes.append(with_margins(outs[6 + i], 6 + i // 2, slice(start, start + cells_r)))
    box = dot_twice(jnp.concatenate(boxes, axis=0), box_c) * (1.0 / 9.0)
    base = 12 * cells_r
    power = [box[base + i * cells_r : base + (i + 1) * cells_r] for i in range(6)]
    for k in range(2):
        for l in range(3):
            second = jnp.where(first[k][l], power[k + l + 1], power[k + l + 2])
            factor = lax.rsqrt(power[k] * second + 1e-06)
            for part in range(2):
                at = ((k * 3 + l) * 2 + part) * cells_r
                coh_ref[k, l, part] = (box[at : at + cells_r] * factor)[:, :cells_c]

    z = dot(split(jnp.concatenate(spectra, axis=0)), col_fwd)
    z_r, z_i = z[:, :LANES], z[:, LANES:]
    energy = z_r * z_r + z_i * z_i
    lane32 = lax.rem(lax.broadcasted_iota(jnp.int32, (6 * PATCH, LANES), 1), PATCH)
    left = jnp.where(lane32 == 0, pltpu.roll(energy, LANES - PATCH + 1, 1), pltpu.roll(energy, 1, 1))
    right = jnp.where(
        lane32 == PATCH - 1, pltpu.roll(energy, PATCH - 1, 1), pltpu.roll(energy, LANES - 1, 1)
    )
    across = energy + left + right

    def per_patch(tiles, sums_of, scale):
        sums = [jnp.sum(tile, axis=0, keepdims=True) for tile in tiles]
        sums += [jnp.zeros((2, LANES), jnp.float32)]
        return dot_exact(jnp.concatenate(sums, axis=0), sums_of) * scale

    level = per_patch(
        [s[:, :LANES] * s[:, :LANES] + s[:, LANES:] * s[:, LANES:] for s in spectra],
        window,
        1.0 / PATCH,
    )
    weights = []
    for p in range(6):
        part = across[p * PATCH : (p + 1) * PATCH]
        smooth = (part + pltpu.roll(part, 1, 0) + pltpu.roll(part, PATCH - 1, 0)) * (1.0 / 9.0)
        weights.append(jnp.sqrt(jnp.sqrt(smooth + level[p : p + 1] + 1e-06)))
    scale = 1.0 / per_patch(weights, group, 1.0 / (PATCH * PATCH))
    filtered = []
    for p in range(6):
        weight = weights[p]
        at = slice(p * PATCH, (p + 1) * PATCH)
        filtered.append(jnp.concatenate([z_r[at] * weight, z_i[at] * weight], axis=0))
    outs = lane_tiles(dot_rows(row_inv, row_inv_low, jnp.concatenate(filtered, axis=1)))
    outs = [o * scale[p : p + 1] for p, o in enumerate(outs)]
    back = [jnp.concatenate([o[:KEEP], o[KEEP:]], axis=1) for o in outs]
    final = dot(split(jnp.concatenate(back, axis=0)), col_inv)
    for p in range(6):
        at = slice(p * KEEP, (p + 1) * KEEP)
        filt_ref[p // 3, p % 3, 0] = final[at, :cells_c]
        filt_ref[p // 3, p % 3, 1] = final[at, LANES : LANES + cells_c]

    for c in range(chunks):
        for h in range(pieces):
            far_copy(c, h).wait_send()
            if (c, h) not in direct:
                near_copy(c, h, img_hbm).wait_send()
    for c, h in direct:
        pass_copy(c, h).wait_send()

        @pl.when(odd)
        def _():
            near_copy(c, h, img_hbm).wait_send()

    for step in steps:

        @pl.when(there(step))
        def _():
            for n, message in enumerate(messages):
                if message[0] == step:
                    halo_copy(n).wait_send()


def write(filt_in, coh_in, filt_out, coh_out, sems):
    copies = [
        pltpu.make_async_copy(filt_in, filt_out, sems.at[0]),
        pltpu.make_async_copy(coh_in, coh_out, sems.at[1]),
    ]
    for copy in copies:
        copy.start()
    for copy in copies:
        copy.wait()


def body(images, secondaries):
    per_device, _, rows, cols = images.shape
    links = secondaries.shape[1]
    dates = lax.axis_size("date")
    assert per_device == 2 and links == 3 and rows == 2 * KEEP and dates % 2 == 0 and dates > 4
    cells_r, cells_c = rows // LOOK_R, cols // LOOK_C
    tall = rows + 2 * MARGIN * LOOK_R
    chunks = rows // BAND
    out = jax.ShapeDtypeStruct((per_device, links, 2, cells_r, cells_c), jnp.float32)
    table, starts = tables(rows, cols)
    vmem = pl.BlockSpec(memory_space=pltpu.VMEM)
    hbm = pl.BlockSpec(memory_space=pltpu.HBM)
    sizes = (dates, lax.axis_size("row"), lax.axis_size("col"))
    dma = pltpu.SemaphoreType.DMA
    results = pl.pallas_call(
        functools.partial(kernel, sizes, starts),
        out_shape=(pltpu.VMEM(out.shape, out.dtype),) * 2,
        in_specs=[hbm, hbm, hbm],
        out_specs=(vmem, vmem),
        scratch_shapes=[
            pltpu.SMEM(secondaries.shape, jnp.int32),
            pltpu.VMEM(images.shape, jnp.float32),
            pltpu.VMEM(table.shape, jnp.bfloat16),
            pltpu.VMEM(images.shape, jnp.float32),
            pltpu.VMEM(images.shape, jnp.float32),
            pltpu.VMEM((DIRECT,) + images.shape[:2] + (BAND, PIECE), jnp.float32),
            pltpu.VMEM((18, tall, LANES), jnp.float32),
            pltpu.VMEM((rows, LANES), jnp.float32),
            pltpu.VMEM((rows, LANES), jnp.float32),
            pltpu.VMEM((tall, LANES), jnp.float32),
            pltpu.VMEM((tall, LANES), jnp.float32),
            dma((chunks * (cols // PIECE),)),
            dma((chunks * (cols // PIECE),)),
            dma((chunks * (cols // PIECE),)),
            dma((chunks * (cols // PIECE),)),
            dma((6 + 2 * chunks,)),
            dma((6 + 2 * chunks,)),
            dma((DIRECT,)),
            dma((DIRECT,)),
            dma((3,)),
        ],
        compiler_params=pltpu.CompilerParams(
            collective_id=0, has_side_effects=True, vmem_limit_bytes=VMEM_BYTES
        ),
        cost_estimate=pl.CostEstimate(flops=10**9, bytes_accessed=10**6, transcendentals=0),
    )(secondaries, images, jnp.asarray(table))
    return pl.pallas_call(
        write,
        out_shape=(out, out),
        in_specs=[vmem, vmem],
        out_specs=(hbm, hbm),
        scratch_shapes=[dma((2,))],
        compiler_params=pltpu.CompilerParams(vmem_limit_bytes=1024 * 1024),
    )(*results)


def solution(mesh):
    in_specs = (P("date", None, "row", "col"), P("date", None))
    out_specs = (P("date", None, None, "row", "col"), P("date", None, None, "row", "col"))
    return jax.shard_map(body, mesh=mesh, in_specs=in_specs, out_specs=out_specs, check_vma=False)
```

```python
import functools
import math

import jax
import jax.numpy as jnp
import ml_dtypes
import numpy as np
from jax import lax
from jax.experimental import pallas as pl
from jax.experimental.pallas import tpu as pltpu
from jax.sharding import PartitionSpec as P

LOOK_R = 2
LOOK_C = 8
PATCH = 32
KEEP = 24
MARGIN = 4
LANES = 128
BAND = 8
PIECE = 256
DIRECT = 2
VMEM_BYTES = 64 * 1024 * 1024 - 800 * 1024
MESH = pl.DeviceIdType.MESH


def tables(rows, cols):
    cells_r, cells_c = rows // LOOK_R, cols // LOOK_C
    blocks = cells_c // KEEP
    halo_r = MARGIN * LOOK_R
    tall = rows + 2 * halo_r

    def lane(x):
        if x < 0:
            return cells_c + MARGIN + x
        return x if x < cells_c else x + MARGIN

    ticks = np.arange(PATCH)
    angle = (ticks[:, None] * ticks[None, :] % PATCH) * (2.0 * math.pi / PATCH)
    cosine, sine = np.cos(angle), np.sin(angle)

    pick = np.zeros((PATCH, tall))
    pick[np.arange(tall) // LOOK_R, np.arange(tall)] = 1.0
    row_c, row_s = cosine @ pick, sine @ pick
    box_r = np.zeros((cells_r, PATCH))
    for y in range(cells_r):
        box_r[y, MARGIN + y - 1 : MARGIN + y + 2] = 1.0
    box_r = box_r @ pick
    none = np.zeros_like(box_r)
    row_fwd = np.block([[row_c, row_s], [-row_s, row_c], [box_r, none], [none, box_r]])

    col_c, col_s = np.zeros((LANES, LANES)), np.zeros((LANES, LANES))
    for b in range(blocks):
        for x in range(PATCH):
            at = lane(b * KEEP - MARGIN + x)
            col_c[at, b * PATCH : (b + 1) * PATCH] = cosine[x]
            col_s[at, b * PATCH : (b + 1) * PATCH] = sine[x]
    centre = slice(MARGIN, MARGIN + KEEP)
    row_inv = np.block([[cosine[centre], -sine[centre]], [sine[centre], cosine[centre]]])
    inv_c, inv_s = np.zeros((LANES, LANES)), np.zeros((LANES, LANES))
    for b in range(blocks):
        inv_c[b * PATCH : (b + 1) * PATCH, b * KEEP : (b + 1) * KEEP] = cosine[:, centre]
        inv_s[b * PATCH : (b + 1) * PATCH, b * KEEP : (b + 1) * KEEP] = sine[:, centre]
    scale = 1.0 / (PATCH * PATCH)
    row_inv = np.concatenate([row_inv, row_inv], axis=1)
    stacked = [row_fwd, col_c, col_s, inv_c * scale, inv_s * scale, row_inv]
    whole = np.concatenate(stacked, axis=0).astype(np.float32)
    high = whole.astype(ml_dtypes.bfloat16)
    low = (whole - high.astype(np.float32)).astype(ml_dtypes.bfloat16)
    starts = np.cumsum([0] + [t.shape[0] for t in stacked])
    return np.stack([high, low]), [int(n) for n in starts]


def split(x):
    high = x.astype(jnp.bfloat16)
    return high, (x - high.astype(jnp.float32)).astype(jnp.bfloat16)


def mul(a, b):
    return lax.dot_general(a, b, (((1,), (0,)), ((), ())), preferred_element_type=jnp.float32)


def dot(a, b):
    return mul(a[0], b[0]) + (mul(a[1], b[0]) + mul(a[0], b[1]))


def dot_exact(x, b):
    high, low = split(x)
    return mul(high, b) + mul(low, b)


def dot_rows(twice, low_table, x):
    high, low = split(x)
    return mul(twice, jnp.concatenate([high, low], axis=0)) + mul(low_table, high)


def dot_twice(x, twice):
    return mul(jnp.concatenate(split(x), axis=1), twice)


def kernel(
    sizes,
    starts,
    sec_hbm,
    img_hbm,
    table_hbm,
    filt_ref,
    coh_ref,
    sec_ref,
    img_ref,
    table,
    near,
    far,
    passing,
    planes,
    edge_l,
    edge_r,
    side_l,
    side_r,
    near_send,
    near_recv,
    far_send,
    far_recv,
    halo_send,
    halo_recv,
    pass_send,
    pass_recv,
    local_sem,
):
    dates, n_rows, n_cols = sizes
    rows, cols = img_ref.shape[2], img_ref.shape[3]
    cells_c = cols // LOOK_C
    cells_r = rows // LOOK_R
    halo = MARGIN * LOOK_R
    chunks = rows // BAND
    date, row, col = lax.axis_index("date"), lax.axis_index("row"), lax.axis_index("col")
    odd = lax.rem(date, 2) == 1
    mate = date + 1 - 2 * lax.rem(date, 2)
    before = lax.rem(date + dates - 2, dates)
    after = lax.rem(date + 2, dates)
    steps = [(r, c) for r in (-1, 0, 1) for c in (-1, 0, 1) if (r, c) != (0, 0)]

    def there(step):
        test_r = [None, row < n_rows - 1, row > 0][step[0]]
        test_c = [None, col < n_cols - 1, col > 0][step[1]]
        tests = [t for t in (test_r, test_c) if t is not None]
        return functools.reduce(jnp.logical_and, tests)

    order = [0, chunks - 1] + list(range(1, chunks - 1))
    load_img = pltpu.make_async_copy(img_hbm, img_ref, local_sem.at[0])
    load_table = pltpu.make_async_copy(table_hbm, table, local_sem.at[1])
    load_sec = pltpu.make_async_copy(sec_hbm, sec_ref, local_sem.at[2])
    load_sec.start()
    load_img.start()
    load_table.start()
    barrier = pltpu.get_barrier_semaphore()
    for other in (before, after, mate):
        pl.semaphore_signal(barrier, inc=1, device_id=(other, row, col), device_id_type=MESH)
    count = jnp.int32(3)
    for step in steps:
        here = there(step)

        @pl.when(here)
        def _():
            pl.semaphore_signal(
                barrier,
                inc=1,
                device_id=(date, row + step[0], col + step[1]),
                device_id_type=MESH,
            )

        count = count + here.astype(jnp.int32)
    pl.semaphore_wait(barrier, count)

    def band(c):
        return pl.ds(c * BAND, BAND)

    pieces = cols // PIECE

    def far_copy(c, h):
        part = (slice(None), slice(None), band(c), pl.ds(h * PIECE, PIECE))
        return pltpu.make_async_remote_copy(
            src_ref=img_hbm.at[part],
            dst_ref=far.at[part],
            send_sem=far_send.at[c * pieces + h],
            recv_sem=far_recv.at[c * pieces + h],
            device_id=(before, row, col),
            device_id_type=MESH,
        )

    def near_copy(c, h, source):
        part = (slice(None), slice(None), band(c), pl.ds(h * PIECE, PIECE))
        return pltpu.make_async_remote_copy(
            src_ref=source.at[part],
            dst_ref=near.at[part],
            send_sem=near_send.at[c * pieces + h],
            recv_sem=near_recv.at[c * pieces + h],
            device_id=(mate, row, col),
            device_id_type=MESH,
        )

    every = [(c, h) for c in order for h in range(pieces)]
    direct = every[len(every) - DIRECT :]

    def pass_copy(c, h):
        n = direct.index((c, h))
        return pltpu.make_async_remote_copy(
            src_ref=img_hbm.at[:, :, band(c), pl.ds(h * PIECE, PIECE)],
            dst_ref=passing.at[n],
            send_sem=pass_send.at[n],
            recv_sem=pass_recv.at[n],
            device_id=(mate, row, col),
            device_id_type=MESH,
        )

    def last_copy(c, h):
        n = direct.index((c, h))
        return pltpu.make_async_remote_copy(
            src_ref=passing.at[n],
            dst_ref=near.at[:, :, band(c), pl.ds(h * PIECE, PIECE)],
            send_sem=pass_send.at[n],
            recv_sem=near_recv.at[c * pieces + h],
            device_id=(before, row, col),
            device_id_type=MESH,
        )

    for c, h in direct:

        @pl.when(jnp.logical_not(odd))
        def _():
            pass_copy(c, h).start()

    for c in order:
        for h in range(pieces):
            far_copy(c, h).start()

            @pl.when(odd)
            def _():
                near_copy(c, h, img_hbm).start()

    for step in steps:

        @pl.when(jnp.logical_not(there(step)))
        def _():
            r, c = step
            at = {-1: slice(0, halo), 0: slice(halo, halo + rows), 1: slice(halo + rows, None)}[r]
            if c == 0:
                planes[:, at] = jnp.zeros_like(planes[:, at])
            else:
                side = side_l if c < 0 else side_r
                side[at] = jnp.zeros_like(side[at])

    total = 2 * dates
    load_sec.wait()

    def is_first(k, l):
        return lax.rem(sec_ref[k, l] - (2 * date + k) + total, total) == l + 1

    first = [[is_first(k, l) for l in range(3)] for k in range(2)]

    def lane_of(x):
        return jnp.where(x < 0, cells_c + MARGIN + x, jnp.where(x < cells_c, x, x + MARGIN))

    cell = lax.broadcasted_iota(jnp.int32, (cols, LANES), 0) // LOOK_C
    looks = jnp.where(
        cell == lax.broadcasted_iota(jnp.int32, (cols, LANES), 1), 1.0 / (LOOK_R * LOOK_C), 0.0
    ).astype(jnp.bfloat16)
    from_lane = lax.broadcasted_iota(jnp.int32, (LANES, LANES), 0)
    to_lane = lax.broadcasted_iota(jnp.int32, (LANES, LANES), 1)
    box_c = (from_lane == to_lane) | (from_lane == lane_of(to_lane - 1))
    box_c = box_c | (from_lane == lane_of(to_lane + 1))
    box_c = jnp.where(box_c & (to_lane < cells_c), 1.0, 0.0).astype(jnp.bfloat16)
    box_c = jnp.concatenate([box_c, box_c], axis=0)
    from_cell = jnp.where(
        from_lane < cells_c,
        from_lane,
        jnp.where(from_lane < cells_c + MARGIN, from_lane - cells_c, from_lane) - MARGIN,
    )
    in_patch = from_cell - (to_lane // PATCH * KEEP - MARGIN)
    window = (in_patch >= 0) & (in_patch < PATCH) & (from_lane < cells_c + 2 * MARGIN)
    window = jnp.where(window, 1.0, 0.0).astype(jnp.bfloat16)
    group = jnp.where(from_lane // PATCH == to_lane // PATCH, 1.0, 0.0).astype(jnp.bfloat16)

    def look_sums(c, h):
        at, across = band(c), pl.ds(h * PIECE, PIECE)

        def date_image(i):
            source = (img_ref, near, far)[i // 2]
            return source[i % 2, 0, at, across], source[i % 2, 1, at, across]

        images = [date_image(i) for i in range(6)]
        parts = []
        for k in range(2):
            a_r, a_i = images[k]
            for l in range(3):
                low, high = images[k + l + 1], images[k + l + 2]
                b_r = jnp.where(first[k][l], low[0], high[0])
                b_i = jnp.where(first[k][l], low[1], high[1])
                parts += [a_r * b_r + a_i * b_i, a_i * b_r - a_r * b_i]
        parts += [r * r + i * i for r, i in images]
        return dot_exact(jnp.concatenate(parts, axis=0), looks[h * PIECE : (h + 1) * PIECE])

    def keep(c, summed):
        at = band(c)
        lanes = lax.broadcasted_iota(jnp.int32, (BAND, LANES), 1)
        pack_l = jnp.zeros((BAND, LANES), jnp.float32)
        pack_r = jnp.zeros((BAND, LANES), jnp.float32)
        for p in range(planes.shape[0]):
            own = summed[p * BAND : (p + 1) * BAND]
            planes[p, pl.ds(halo + c * BAND, BAND)] = own
            mine = (lanes >= p * MARGIN) & (lanes < (p + 1) * MARGIN)
            pack_l = jnp.where(mine, pltpu.roll(own, (p * MARGIN) % LANES, 1), pack_l)
            shift = (p * MARGIN - (cells_c - MARGIN)) % LANES
            pack_r = jnp.where(mine, pltpu.roll(own, shift, 1), pack_r)
        edge_l[at] = pack_l
        edge_r[at] = pack_r

    messages = []
    for step in steps:
        if step[0] == 0:
            messages += [(step, c * BAND, BAND, c) for c in range(chunks)]
        else:
            c = 0 if step[0] < 0 else chunks - 1
            messages.append((step, c * BAND, BAND, c))

    def halo_copy(n):
        (r, c), start, size, _ = messages[n]
        source_at = pl.ds(start, size)
        target_at = pl.ds(halo + start - r * rows, size)
        if c == 0:
            source, target = planes.at[:, pl.ds(halo + start, size)], planes.at[:, target_at]
        elif c < 0:
            source, target = edge_l.at[source_at], side_r.at[target_at]
        else:
            source, target = edge_r.at[source_at], side_l.at[target_at]
        return pltpu.make_async_remote_copy(
            src_ref=source,
            dst_ref=target,
            send_sem=halo_send.at[n],
            recv_sem=halo_recv.at[n],
            device_id=(date, row + r, col + c),
            device_id_type=MESH,
        )

    for c, h in direct:

        @pl.when(odd)
        def _():
            pass_copy(c, h).wait_recv()
            last_copy(c, h).start()

    load_img.wait()
    summed = None
    for now, done in zip(every + [None], [None] + every):
        if now is not None and now not in direct:
            far_copy(*now).wait_recv()

            @pl.when(jnp.logical_not(odd))
            def _():
                near_copy(*now, far).start()

        if done is None:
            continue
        c, h = done
        if done in direct:
            far_copy(c, h).wait_recv()
        near_copy(c, h, img_hbm).wait_recv()
        part = look_sums(c, h)
        summed = part if h == 0 else summed + part
        if h < pieces - 1:
            continue
        keep(c, summed)
        for step in steps:

            @pl.when(there(step))
            def _():
                for n, message in enumerate(messages):
                    if message[0] == step and message[3] == c:
                        halo_copy(n).start()

    load_table.wait()

    def part_of(i, j, lanes=LANES):
        rows_at = slice(starts[i], starts[j])
        return table[0, rows_at, :lanes], table[1, rows_at, :lanes]

    row_fwd, row_fwd_low = part_of(0, 1)
    row_fwd = jnp.concatenate([row_fwd, row_fwd], axis=1)
    box_r = table[0, starts[0] + 2 * PATCH : starts[0] + 2 * PATCH + cells_r, : rows + 2 * halo]
    col_fwd = [
        jnp.concatenate(
            [
                jnp.concatenate([cosine, -sine], axis=1),
                jnp.concatenate([sine, cosine], axis=1),
            ],
            axis=0,
        )
        for cosine, sine in zip(part_of(1, 2), part_of(2, 3))
    ]
    col_inv = [
        jnp.concatenate(
            [
                jnp.concatenate([cosine, sine], axis=1),
                jnp.concatenate([-sine, cosine], axis=1),
            ],
            axis=0,
        )
        for cosine, sine in zip(part_of(3, 4), part_of(4, 5))
    ]
    row_inv = table[0, starts[5] : starts[6]]
    row_inv_low = table[1, starts[5] : starts[6], : 2 * PATCH]

    def wait_halo(sides):
        for step in steps:
            if (step[1] != 0) != sides:
                continue

            @pl.when(there((-step[0], -step[1])))
            def _():
                for n, message in enumerate(messages):
                    if message[0] == step:
                        halo_copy(n).wait_recv()

    def lane_tiles(x):
        return [x[:, i : i + LANES] for i in range(0, x.shape[1], LANES)]

    wait_halo(False)
    fields = [jnp.concatenate([planes[2 * p], planes[2 * p + 1]], axis=0) for p in range(6)]
    outs = lane_tiles(dot_rows(row_fwd, row_fwd_low, jnp.concatenate(fields, axis=1)))
    powers = jnp.concatenate([planes[p] for p in range(12, 18)], axis=1)
    box_twice = jnp.concatenate([box_r, box_r], axis=1)
    outs += lane_tiles(mul(box_twice, jnp.concatenate(split(powers), axis=0)))
    wait_halo(True)

    tall = rows + 2 * halo
    wide = lax.broadcasted_iota(jnp.int32, (tall, LANES), 1)
    in_left = lax.rem(wide, 2 * MARGIN) < MARGIN
    got_l, got_r = side_l[...], side_r[...]
    even = jnp.where(in_left, got_l, pltpu.roll(got_r, MARGIN, 1))
    later = jnp.where(in_left, pltpu.roll(got_l, LANES - MARGIN, 1), got_r)
    margins = dot_rows(row_fwd, row_fwd_low, jnp.concatenate([even, later], axis=0))

    def with_margins(out, q, at):
        moved = pltpu.roll(margins[at], (cells_c - 2 * MARGIN * q) % LANES, 1)
        lanes = lax.broadcasted_iota(jnp.int32, out.shape, 1)
        return jnp.where((lanes >= cells_c) & (lanes < cells_c + 2 * MARGIN), moved, out)

    middle = 2 * PATCH
    spectra, boxes = [], []
    for p in range(6):
        out = with_margins(outs[p], p, slice(None))
        spectra.append(jnp.concatenate([out[:PATCH], out[PATCH:middle]], axis=1))
        boxes.append(out[middle:])
    for i in range(6):
        start = middle + (i % 2) * cells_r
        boxes.append(with_margins(outs[6 + i], 6 + i // 2, slice(start, start + cells_r)))
    box = dot_twice(jnp.concatenate(boxes, axis=0), box_c) * (1.0 / 9.0)
    base = 12 * cells_r
    power = [box[base + i * cells_r : base + (i + 1) * cells_r] for i in range(6)]
    for k in range(2):
        for l in range(3):
            second = jnp.where(first[k][l], power[k + l + 1], power[k + l + 2])
            factor = lax.rsqrt(power[k] * second + 1e-06)
            for part in range(2):
                at = ((k * 3 + l) * 2 + part) * cells_r
                coh_ref[k, l, part] = (box[at : at + cells_r] * factor)[:, :cells_c]

    z = dot(split(jnp.concatenate(spectra, axis=0)), col_fwd)
    z_r, z_i = z[:, :LANES], z[:, LANES:]
    energy = z_r * z_r + z_i * z_i
    lane32 = lax.rem(lax.broadcasted_iota(jnp.int32, (6 * PATCH, LANES), 1), PATCH)
    left = jnp.where(lane32 == 0, pltpu.roll(energy, LANES - PATCH + 1, 1), pltpu.roll(energy, 1, 1))
    right = jnp.where(
        lane32 == PATCH - 1, pltpu.roll(energy, PATCH - 1, 1), pltpu.roll(energy, LANES - 1, 1)
    )
    across = energy + left + right

    def per_patch(tiles, sums_of, scale):
        sums = [jnp.sum(tile, axis=0, keepdims=True) for tile in tiles]
        sums += [jnp.zeros((2, LANES), jnp.float32)]
        return dot_exact(jnp.concatenate(sums, axis=0), sums_of) * scale

    level = per_patch(
        [s[:, :LANES] * s[:, :LANES] + s[:, LANES:] * s[:, LANES:] for s in spectra],
        window,
        1.0 / PATCH,
    )
    weights = []
    for p in range(6):
        part = across[p * PATCH : (p + 1) * PATCH]
        smooth = (part + pltpu.roll(part, 1, 0) + pltpu.roll(part, PATCH - 1, 0)) * (1.0 / 9.0)
        weights.append(jnp.sqrt(jnp.sqrt(smooth + level[p : p + 1] + 1e-06)))
    scale = 1.0 / per_patch(weights, group, 1.0 / (PATCH * PATCH))
    filtered = []
    for p in range(6):
        weight = weights[p]
        at = slice(p * PATCH, (p + 1) * PATCH)
        filtered.append(jnp.concatenate([z_r[at] * weight, z_i[at] * weight], axis=0))
    outs = lane_tiles(dot_rows(row_inv, row_inv_low, jnp.concatenate(filtered, axis=1)))
    outs = [o * scale[p : p + 1] for p, o in enumerate(outs)]
    back = [jnp.concatenate([o[:KEEP], o[KEEP:]], axis=1) for o in outs]
    final = dot(split(jnp.concatenate(back, axis=0)), col_inv)
    for p in range(6):
        at = slice(p * KEEP, (p + 1) * KEEP)
        filt_ref[p // 3, p % 3, 0] = final[at, :cells_c]
        filt_ref[p // 3, p % 3, 1] = final[at, LANES : LANES + cells_c]

    for c in range(chunks):
        for h in range(pieces):
            far_copy(c, h).wait_send()
            if (c, h) not in direct:
                near_copy(c, h, img_hbm).wait_send()
    for c, h in direct:
        pass_copy(c, h).wait_send()

        @pl.when(odd)
        def _():
            near_copy(c, h, img_hbm).wait_send()

    for step in steps:

        @pl.when(there(step))
        def _():
            for n, message in enumerate(messages):
                if message[0] == step:
                    halo_copy(n).wait_send()


def write(filt_in, coh_in, filt_out, coh_out, sems):
    copies = [
        pltpu.make_async_copy(filt_in, filt_out, sems.at[0]),
        pltpu.make_async_copy(coh_in, coh_out, sems.at[1]),
    ]
    for copy in copies:
        copy.start()
    for copy in copies:
        copy.wait()


def body(images, secondaries):
    per_device, _, rows, cols = images.shape
    links = secondaries.shape[1]
    dates = lax.axis_size("date")
    assert per_device == 2 and links == 3 and rows == 2 * KEEP and dates % 2 == 0 and dates > 4
    cells_r, cells_c = rows // LOOK_R, cols // LOOK_C
    tall = rows + 2 * MARGIN * LOOK_R
    chunks = rows // BAND
    out = jax.ShapeDtypeStruct((per_device, links, 2, cells_r, cells_c), jnp.float32)
    table, starts = tables(rows, cols)
    vmem = pl.BlockSpec(memory_space=pltpu.VMEM)
    hbm = pl.BlockSpec(memory_space=pltpu.HBM)
    sizes = (dates, lax.axis_size("row"), lax.axis_size("col"))
    dma = pltpu.SemaphoreType.DMA
    results = pl.pallas_call(
        functools.partial(kernel, sizes, starts),
        out_shape=(pltpu.VMEM(out.shape, out.dtype),) * 2,
        in_specs=[hbm, hbm, hbm],
        out_specs=(vmem, vmem),
        scratch_shapes=[
            pltpu.SMEM(secondaries.shape, jnp.int32),
            pltpu.VMEM(images.shape, jnp.float32),
            pltpu.VMEM(table.shape, jnp.bfloat16),
            pltpu.VMEM(images.shape, jnp.float32),
            pltpu.VMEM(images.shape, jnp.float32),
            pltpu.VMEM((DIRECT,) + images.shape[:2] + (BAND, PIECE), jnp.float32),
            pltpu.VMEM((18, tall, LANES), jnp.float32),
            pltpu.VMEM((rows, LANES), jnp.float32),
            pltpu.VMEM((rows, LANES), jnp.float32),
            pltpu.VMEM((tall, LANES), jnp.float32),
            pltpu.VMEM((tall, LANES), jnp.float32),
            dma((chunks * (cols // PIECE),)),
            dma((chunks * (cols // PIECE),)),
            dma((chunks * (cols // PIECE),)),
            dma((chunks * (cols // PIECE),)),
            dma((6 + 2 * chunks,)),
            dma((6 + 2 * chunks,)),
            dma((DIRECT,)),
            dma((DIRECT,)),
            dma((3,)),
        ],
        compiler_params=pltpu.CompilerParams(
            collective_id=0, has_side_effects=True, vmem_limit_bytes=VMEM_BYTES
        ),
        cost_estimate=pl.CostEstimate(flops=10**9, bytes_accessed=10**6, transcendentals=0),
    )(secondaries, images, jnp.asarray(table))
    return pl.pallas_call(
        write,
        out_shape=(out, out),
        in_specs=[vmem, vmem],
        out_specs=(hbm, hbm),
        scratch_shapes=[dma((2,))],
        compiler_params=pltpu.CompilerParams(vmem_limit_bytes=1024 * 1024),
    )(*results)


def solution(mesh):
    in_specs = (P("date", None, "row", "col"), P("date", None))
    out_specs = (P("date", None, None, "row", "col"), P("date", None, None, "row", "col"))
    return jax.shard_map(body, mesh=mesh, in_specs=in_specs, out_specs=out_specs, check_vma=False)
```
